32 devices in a mesh: tile: 4 (over y, x), col: 8 (over z, core).
Axes of the slice: x: 2, y: 2, z: 4, core: 2. Of those that a mesh axis runs over, the one named last changes fastest.
Arguments:
- adjoint_in: float32 [25, 128, 1024], P(None, 'tile', 'col'), may hold values from -6 to 6
- centre: float32 [25, 128, 1024], P(None, 'tile', 'col'), may hold values from 0.2 to 0.6
- side_coeff: float32 [4, 25, 128, 1024], P(None, None, 'tile', 'col'), may hold values from 0.05 to 0.25
- vert_coeff: float32 [2, 25, 128, 1024], P(None, None, 'tile', 'col'), may hold values from 0.05 to 0.25
- land_mask: int32 [25, 128, 1024], P(None, 'tile', 'col'), may hold values 0 or 1
- obs_misfit: float32 [4, 8, 8, 128], P('tile', 'col'), may hold values from -6 to 6
- obs_cell: int32 [4, 8, 8, 128], P('tile', 'col'), may hold values from 0 to 102399
- obs_count: int32 [4, 8, 8], P('tile', 'col'), may hold values from 0 to 128, as said below
- fold_partner: int32 [8], replicated, may hold values from 0 to 7, as said below
- fold_flip: int32 [8], replicated, may hold values 0 or 1
Outputs:
- adjoint_out: float32 [25, 128, 1024], P(None, 'tile', 'col')
The draws below stay inside these ranges and needn't reach their ends.
Inputs may be any that keep to these rules, and one draw needn't show every extreme that they name: `obs_count`: slots at and beyond the count hold values that are ignored; some destination gets 128 from some source in every draw. `fold_partner`: each tile column appears exactly once.
All inputs are finite; a program needn't handle non-finite values. No bound on the sum of `land_mask` on one device may be relied on, other than what follows from the above.
Results may differ from the reference program's by a relative error of at most 0.0003.
Values sent between devices are 32-bit elements; how exact they have to be, the bound alone decides.
No kernel may reach another device: no remote copies, remote signals or barrier semaphores. Data moves between devices by JAX's collectives and lax.ppermute only.
A program may use at most 64 MiB of HBM per device.

```python
import jax
import jax.numpy as jnp

LEVELS = 25
ROWS = 32
COLS = 128
CAP = 128
STEPS = 2
TILE_ROWS = 4
TILE_COLS = 8
NY = 128
NX = 1024


def draw_obs_count(key, part):
    key_base, key_dense, key_full, key_empty = jax.random.split(key, 4)
    base = jax.random.randint(key_base, (TILE_ROWS, TILE_COLS, TILE_COLS), 0, CAP + 1)
    dense = jax.random.randint(key_dense, (1, TILE_COLS, 1), 1, 4)
    counts = jnp.minimum(CAP, base * dense // 2)
    empty_at = jax.random.randint(key_empty, (3,), 0, 1000000)
    full_at = jax.random.randint(key_full, (3,), 0, 1000000)
    counts = counts.at[empty_at[0] % TILE_ROWS, empty_at[1] % TILE_COLS, empty_at[2] % TILE_COLS].set(0)
    counts = counts.at[full_at[0] % TILE_ROWS, full_at[1] % TILE_COLS, full_at[2] % TILE_COLS].set(CAP)
    return counts.astype(jnp.int32)


def place_value(order, position, wanted):
    spots = jnp.arange(TILE_COLS, dtype=jnp.int32)
    found = jnp.sum(jnp.where(order == wanted, spots, 0)).astype(jnp.int32)
    moved = order[position]
    order = jnp.where(spots == found, moved, order)
    order = jnp.where(spots == position, wanted, order)
    return order


def draw_fold_partner(key, part):
    order = jax.random.permutation(jax.random.fold_in(key, 7), TILE_COLS).astype(jnp.int32)
    order = place_value(order, 0, 1 % TILE_COLS)
    order = place_value(order, 1, (1 + TILE_COLS // 2) % TILE_COLS)
    return order.astype(jnp.int32)


def with_ends(drawn, stream_key, least, top_value):
    longest = drawn.shape.index(max(drawn.shape))
    spots = []
    for shift in (0, 1):
        where = [jax.random.randint(jax.random.fold_in(stream_key, axis), (), 0, length) for axis, length in enumerate(drawn.shape)]
        where[longest] = (where[longest] + shift) % drawn.shape[longest]
        spots.append(tuple(where))
    return drawn.at[spots[0]].set(least).at[spots[1]].set(top_value)


def steps_of(key, dims, cuts, low, high):
    loudness, own = 1.0, jax.random.fold_in(key, 6)
    for dim, blocks in cuts:
        heights = jnp.exp(jax.random.uniform(jax.random.fold_in(own, dim), (blocks,), jnp.float32, low / len(cuts), high / len(cuts)))
        loudness = loudness * jnp.repeat(heights, dims[dim] // blocks).reshape([-1 if axis == dim else 1 for axis in range(len(dims))])
    return loudness


def scatter_about(stream_key, extent, scale, limit, cuts=(), held_as=jnp.bfloat16):
    entries = scale * jax.random.normal(stream_key, extent, jnp.float32)
    if cuts:
        entries = entries * steps_of(stream_key, extent, cuts, -0.22, 0.18)
    return jnp.clip(entries, -limit, limit).astype(held_as)


def setup_inputs(seed: int = 0) -> dict:
    keys = jax.random.split(jax.random.key(seed), 11)
    return {
        "adjoint_in": scatter_about(keys[0], (LEVELS, NY, NX), 1.0, 6.0, ((1, 4), (2, 8)), jnp.float32),
        "centre": jnp.clip(0.2 + 0.400000021 * jax.random.uniform(keys[1], (LEVELS, NY, NX), jnp.float32) ** steps_of(keys[1], (LEVELS, NY, NX), ((1, 4), (2, 8)), -0.2, 0.2), 0.2, 0.6),
        "side_coeff": jnp.clip(0.05 + 0.2 * jax.random.uniform(keys[2], (4, LEVELS, NY, NX), jnp.float32) ** steps_of(keys[2], (4, LEVELS, NY, NX), ((2, 4), (3, 8)), -0.2, 0.2), 0.05, 0.25),
        "vert_coeff": jnp.clip(0.05 + 0.2 * jax.random.uniform(keys[3], (2, LEVELS, NY, NX), jnp.float32) ** steps_of(keys[3], (2, LEVELS, NY, NX), ((2, 4), (3, 8)), -0.2, 0.2), 0.05, 0.25),
        "land_mask": with_ends((jax.random.randint(keys[4], (LEVELS, NY, NX), 0, 4) < 3).astype(jnp.int32), jax.random.fold_in(keys[4], 1), 0, 1),
        "obs_misfit": scatter_about(keys[5], (TILE_ROWS, TILE_COLS, TILE_COLS, CAP), 1.0, 6.0, ((0, 4), (1, 8)), jnp.float32),
        "obs_cell": with_ends(jax.random.randint(keys[6], (TILE_ROWS, TILE_COLS, TILE_COLS, CAP), 0, LEVELS * ROWS * COLS), jax.random.fold_in(keys[6], 1), 0, (LEVELS * ROWS * COLS) - 1).astype(jnp.int32),
        "obs_count": draw_obs_count(jax.random.fold_in(keys[10], 71), 0),
        "fold_partner": draw_fold_partner(jax.random.fold_in(keys[10], 71), 0),
        "fold_flip": with_ends((jax.random.randint(keys[9], (TILE_COLS,), 0, 2) < 1).astype(jnp.int32), jax.random.fold_in(keys[9], 1), 0, 1),
    }


def tile_forcing(misfit, cells, counts):
    usable = jnp.arange(misfit.shape[1])[None, :] < counts[:, None]
    values = jnp.where(usable, misfit, jnp.float32(0.0))
    total = jnp.zeros((LEVELS * ROWS * COLS,), jnp.float32)
    return total.at[cells.reshape(-1)].add(values.reshape(-1))


def adjoint_step(adjoint, centre, side_coeff, vert_coeff, fold_partner, fold_flip, ocean):
    partial_value = side_coeff * adjoint[None]
    result = centre * adjoint
    result = result + jnp.roll(partial_value[0], 1, axis=2) + jnp.roll(partial_value[1], -1, axis=2)
    result = result + jnp.pad(partial_value[2], ((0, 0), (1, 0), (0, 0)))[:, :-1, :]
    result = result + jnp.pad(partial_value[3], ((0, 0), (0, 1), (0, 0)))[:, 1:, :]
    upward = vert_coeff[0] * adjoint
    downward = vert_coeff[1] * adjoint
    result = result + jnp.pad(upward, ((0, 1), (0, 0), (0, 0)))[1:]
    result = result + jnp.pad(downward, ((1, 0), (0, 0), (0, 0)))[:-1]
    top_edge = partial_value[2][:, -1, :].reshape(LEVELS, TILE_COLS, COLS)
    turned = jnp.where(fold_flip[None, :, None] == 1, top_edge[:, :, ::-1], top_edge)
    landing = jnp.zeros_like(turned).at[:, fold_partner, :].set(turned)
    result = result.at[:, -1, :].add(landing.reshape(LEVELS, TILE_COLS * COLS))
    return ocean * result


def reference(adjoint_in, centre, side_coeff, vert_coeff, land_mask, obs_misfit, obs_cell, obs_count, fold_partner, fold_flip):
    by_landing = jnp.transpose(obs_misfit, (0, 2, 1, 3))
    forcing = jax.vmap(jax.vmap(tile_forcing))(by_landing, obs_cell, obs_count)
    forcing = forcing.reshape(TILE_ROWS, TILE_COLS, LEVELS, ROWS, COLS)
    forcing = jnp.transpose(forcing, (2, 0, 3, 1, 4)).reshape(LEVELS, TILE_ROWS * ROWS, TILE_COLS * COLS)
    adjoint = adjoint_in + forcing
    ocean = land_mask.astype(jnp.float32)
    for advance in range(STEPS):
        adjoint = adjoint_step(adjoint, centre, side_coeff, vert_coeff, fold_partner, fold_flip, ocean)
    return adjoint
```

```python
import functools

import jax
import jax.numpy as jnp
from jax import lax
from jax.experimental import pallas as pl
from jax.experimental.pallas import tpu as pltpu
from jax.sharding import PartitionSpec as P

LEVELS = 25
ROWS = 32
COLS = 128
CAP = 128
GROUP = 8
EDGE = 16
SLOT = 48
PAD = 32
VMEM = pl.BlockSpec(memory_space=pltpu.VMEM)
SMEM = pl.BlockSpec(memory_space=pltpu.SMEM)


def iota(shape, dim):
    return lax.broadcasted_iota(jnp.int32, shape, dim)


def one_step(value, centre, side, vert, out, edge, up, down):
    row, lane = iota((ROWS, COLS), 0), iota((ROWS, COLS), 1)
    packed = jnp.zeros((ROWS, COLS), jnp.float32)
    for k in range(LEVELS):
        y = value(k)
        east = pltpu.roll(side[0, k] * y, 1, 1)
        west = pltpu.roll(side[1, k] * y, COLS - 1, 1)
        north = pltpu.roll(side[2, k] * y, 1, 0)
        south = pltpu.roll(side[3, k] * y, ROWS - 1, 0)
        r = centre[k] * y
        r = r + jnp.where(lane > 0, east, 0.0) + jnp.where(lane < COLS - 1, west, 0.0)
        r = r + jnp.where(row > 0, north, 0.0) + jnp.where(row < ROWS - 1, south, 0.0)
        if k + 1 < LEVELS:
            r = r + vert[0, k + 1] * value(k + 1)
        if k > 0:
            r = r + vert[1, k - 1] * value(k - 1)
        out[k] = r
        up[k : k + 1, :] = north[0:1, :]
        down[k : k + 1, :] = south[ROWS - 1 : ROWS, :]
        leaving = jnp.where(lane == 0, east, jnp.where(lane == COLS - 1, west, 0.0))
        packed = packed + (pltpu.roll(leaving, 2 * k, 1) if k else leaving)
    for half in range(2):
        low = packed[16 * half : 16 * half + 8]
        high = packed[16 * half + 8 : 16 * half + 16]
        edge[8 * half : 8 * half + 8, :] = low + pltpu.roll(high, 2 * LEVELS, 1)


def spread(slots, up, edge):
    for s in range(slots.shape[0]):
        slots[s, 0:EDGE, :] = edge[...]
        slots[s, EDGE:SLOT, :] = up[...]


def clear_tail(ref):
    ref[24:PAD, :] = jnp.zeros((8, COLS), jnp.float32)


def first_kernel(sources, misfit, cell, count, adjoint, centre, side, vert, out, slots, up, down, hot, valued, forcing, held, edge):
    group = min(GROUP, sources)
    lane = iota((1, CAP), 1)
    for first in range(0, sources, group):
        for s in range(group):
            at = slice(s * CAP, (s + 1) * CAP)
            cells = cell[first + s : first + s + 1, :]
            v = jnp.where(lane < count[0, first + s], misfit[first + s : first + s + 1, :], 0.0)
            high = v.astype(jnp.bfloat16).astype(jnp.float32)
            middle = (v - high).astype(jnp.bfloat16).astype(jnp.float32)
            low = v - high - middle
            column = iota((COLS, CAP), 0) == (cells & (COLS - 1))
            for i, part in enumerate((high, middle, low)):
                valued[i * COLS : (i + 1) * COLS, at] = jnp.where(column, part, 0.0).astype(jnp.bfloat16)
            place = cells >> 7
            for k in range(LEVELS):
                match = (iota((ROWS, CAP), 0) + k * ROWS) == place
                hot[k * ROWS : (k + 1) * ROWS, at] = jnp.where(match, 1.0, 0.0).astype(jnp.bfloat16)
        part = lax.dot_general(hot[...], valued[...], (((1,), (1,)), ((), ())), preferred_element_type=jnp.float32)
        if first == 0:
            forcing[...] = part
        else:
            forcing[...] += part
    for k in range(LEVELS):
        rows = slice(k * ROWS, (k + 1) * ROWS)
        f = forcing[rows, 0:COLS] + forcing[rows, COLS : 2 * COLS] + forcing[rows, 2 * COLS : 3 * COLS]
        held[k] = adjoint[k] + f
    clear_tail(up)
    clear_tail(down)
    one_step(lambda k: held[k], centre, side, vert, out, edge, up, down)
    spread(slots, up, edge)


def arrivals(from_below, from_above, slots, partner, flip, where, landing, halo):
    sources = slots.shape[0]
    column, top = where[0], where[1]
    source = 0
    for s in range(sources):
        source = jnp.where(partner[s] == column, s, source)
    fold = slots[source, EDGE:SLOT, :]
    back = COLS - 1 - iota((PAD, COLS), 1)
    turned = jnp.take_along_axis(fold, back, axis=1)
    fold = jnp.where(flip[source] == 1, turned, fold)
    landing[...] = jnp.where(top == 1, fold, from_above[...])
    left = jnp.where(column == 0, sources - 1, column - 1)
    right = jnp.where(column == sources - 1, 0, column + 1)
    even = (iota((EDGE, COLS), 1) & 1) == 0
    packed = jnp.where(even, slots[left, 0:EDGE, :], slots[right, 0:EDGE, :])
    for half in range(2):
        rows = packed[8 * half : 8 * half + 8]
        halo[16 * half : 16 * half + 8, :] = rows
        halo[16 * half + 8 : 16 * half + 16, :] = pltpu.roll(rows, COLS - 2 * LEVELS, 1)


def joined(k, part, from_below, landing, halo, mask):
    row, lane = iota((ROWS, COLS), 0), iota((ROWS, COLS), 1)
    sides = halo[...]
    sides = pltpu.roll(sides, COLS - 2 * k, 1) if k else sides
    r = part[k] + jnp.where((lane == 0) | (lane == COLS - 1), sides, 0.0)
    r = r + jnp.where(row == 0, from_below[k : k + 1, :], 0.0)
    r = r + jnp.where(row == ROWS - 1, landing[k : k + 1, :], 0.0)
    return mask[k].astype(jnp.float32) * r


def middle_kernel(part, from_below, from_above, got, partner, flip, where, mask, centre, side, vert, out, slots, up, down, held, edge, landing, halo):
    arrivals(from_below, from_above, got, partner, flip, where, landing, halo)
    for k in range(LEVELS):
        held[k] = joined(k, part, from_below, landing, halo, mask)
    clear_tail(up)
    clear_tail(down)
    one_step(lambda k: held[k], centre, side, vert, out, edge, up, down)
    spread(slots, up, edge)


def last_kernel(part, from_below, from_above, got, partner, flip, where, mask, out, landing, halo):
    arrivals(from_below, from_above, got, partner, flip, where, landing, halo)
    for k in range(LEVELS):
        out[k] = joined(k, part, from_below, landing, halo, mask)


def exchange(slots, up, down, tiles):
    from_below = lax.ppermute(up, "tile", [(i, i + 1) for i in range(tiles - 1)])
    from_above = lax.ppermute(down, "tile", [(i + 1, i) for i in range(tiles - 1)])
    got = lax.all_to_all(slots, "col", split_axis=0, concat_axis=0, tiled=True)
    return from_below, from_above, got


def body(adjoint_in, centre, side_coeff, vert_coeff, land_mask, obs_misfit, obs_cell, obs_count, fold_partner, fold_flip):
    sources = obs_misfit.shape[2]
    tiles = lax.axis_size("tile")
    where = jnp.stack([lax.axis_index("col"), (lax.axis_index("tile") == tiles - 1).astype(jnp.int32)])
    received = lax.all_to_all(obs_misfit, "col", split_axis=2, concat_axis=1, tiled=True)
    f32 = jnp.float32
    tile = jax.ShapeDtypeStruct((LEVELS, ROWS, COLS), f32)
    leaving = (
        tile,
        jax.ShapeDtypeStruct((sources, SLOT, COLS), f32),
        jax.ShapeDtypeStruct((PAD, COLS), f32),
        jax.ShapeDtypeStruct((PAD, COLS), f32),
    )
    held = pltpu.VMEM((LEVELS, ROWS, COLS), f32)
    edge = pltpu.VMEM((EDGE, COLS), f32)
    line = pltpu.VMEM((PAD, COLS), f32)
    params = pltpu.CompilerParams(vmem_limit_bytes=24 * 1024 * 1024)
    group = min(GROUP, sources)
    part, slots, up, down = pl.pallas_call(
        functools.partial(first_kernel, sources),
        out_shape=leaving,
        in_specs=[VMEM, VMEM, SMEM, VMEM, VMEM, VMEM, VMEM],
        out_specs=(VMEM,) * 4,
        scratch_shapes=[
            pltpu.VMEM((LEVELS * ROWS, group * CAP), jnp.bfloat16),
            pltpu.VMEM((3 * COLS, group * CAP), jnp.bfloat16),
            pltpu.VMEM((LEVELS * ROWS, 3 * COLS), f32),
            held,
            edge,
        ],
        compiler_params=params,
        name="first_step",
    )(
        received.reshape(sources, CAP),
        obs_cell.reshape(sources, CAP),
        obs_count.reshape(1, sources),
        adjoint_in,
        centre,
        side_coeff,
        vert_coeff,
    )
    from_below, from_above, got = exchange(slots, up, down, tiles)
    part, slots, up, down = pl.pallas_call(
        middle_kernel,
        out_shape=leaving,
        in_specs=[VMEM, VMEM, VMEM, VMEM, SMEM, SMEM, SMEM, VMEM, VMEM, VMEM, VMEM],
        out_specs=(VMEM,) * 4,
        scratch_shapes=[held, edge, line, line],
        compiler_params=params,
        name="second_step",
    )(part, from_below, from_above, got, fold_partner, fold_flip, where, land_mask, centre, side_coeff, vert_coeff)
    from_below, from_above, got = exchange(slots, up, down, tiles)
    return pl.pallas_call(
        last_kernel,
        out_shape=tile,
        in_specs=[VMEM, VMEM, VMEM, VMEM, SMEM, SMEM, SMEM, VMEM],
        out_specs=VMEM,
        scratch_shapes=[line, line],
        compiler_params=params,
        name="last_join",
    )(part, from_below, from_above, got, fold_partner, fold_flip, where, land_mask)


def solution(mesh):
    in_specs = (
        P(None, "tile", "col"),
        P(None, "tile", "col"),
        P(None, None, "tile", "col"),
        P(None, None, "tile", "col"),
        P(None, "tile", "col"),
        P("tile", "col", None, None),
        P("tile", "col", None, None),
        P("tile", "col", None),
        P(),
        P(),
    )
    out_specs = P(None, "tile", "col")
    return jax.shard_map(body, mesh=mesh, in_specs=in_specs, out_specs=out_specs, check_vma=False)
```

```python
import functools

import jax
import jax.numpy as jnp
from jax import lax
from jax.experimental import pallas as pl
from jax.experimental.pallas import tpu as pltpu
from jax.sharding import PartitionSpec as P

LEVELS = 25
ROWS = 32
COLS = 128
CAP = 128
GROUP = 8
EDGE = 16
SLOT = 48
PAD = 32
VMEM = pl.BlockSpec(memory_space=pltpu.VMEM)
FAR = pl.BlockSpec(memory_space=pltpu.HBM)
SMEM = pl.BlockSpec(memory_space=pltpu.SMEM)


def iota(shape, dim):
    return lax.broadcasted_iota(jnp.int32, shape, dim)


def one_step(value, centre, side, vert, out, edge, up, down):
    row, lane = iota((ROWS, COLS), 0), iota((ROWS, COLS), 1)
    packed = jnp.zeros((ROWS, COLS), jnp.float32)
    for k in range(LEVELS):
        y = value(k)
        east = pltpu.roll(side[0, k] * y, 1, 1)
        west = pltpu.roll(side[1, k] * y, COLS - 1, 1)
        north = pltpu.roll(side[2, k] * y, 1, 0)
        south = pltpu.roll(side[3, k] * y, ROWS - 1, 0)
        r = centre[k] * y
        r = r + jnp.where(lane > 0, east, 0.0) + jnp.where(lane < COLS - 1, west, 0.0)
        r = r + jnp.where(row > 0, north, 0.0) + jnp.where(row < ROWS - 1, south, 0.0)
        if k + 1 < LEVELS:
            r = r + vert[0, k + 1] * value(k + 1)
        if k > 0:
            r = r + vert[1, k - 1] * value(k - 1)
        out[k] = r
        up[k : k + 1, :] = north[0:1, :]
        down[k : k + 1, :] = south[ROWS - 1 : ROWS, :]
        leaving = jnp.where(lane == 0, east, jnp.where(lane == COLS - 1, west, 0.0))
        packed = packed + (pltpu.roll(leaving, 2 * k, 1) if k else leaving)
    for half in range(2):
        low = packed[16 * half : 16 * half + 8]
        high = packed[16 * half + 8 : 16 * half + 16]
        edge[8 * half : 8 * half + 8, :] = low + pltpu.roll(high, 2 * LEVELS, 1)


def spread(slots, up, edge):
    for s in range(slots.shape[0]):
        slots[s, 0:EDGE, :] = edge[...]
        slots[s, EDGE:SLOT, :] = up[...]


def clear_tail(ref):
    ref[24:PAD, :] = jnp.zeros((8, COLS), jnp.float32)


def first_kernel(sources, misfit, cell, count, adjoint_far, centre_far, side_far, vert_far, out, slots, up, down, hot, valued, forcing, held, edge, adjoint, centre, side, vert, arrived):
    loads = [
        pltpu.make_async_copy(far, near, arrived.at[i])
        for i, (far, near) in enumerate(((adjoint_far, adjoint), (side_far, side), (centre_far, centre), (vert_far, vert)))
    ]
    for load in loads:
        load.start()
    group = min(GROUP, sources)
    lane = iota((1, CAP), 1)
    for first in range(0, sources, group):
        for s in range(group):
            at = slice(s * CAP, (s + 1) * CAP)
            cells = cell[first + s : first + s + 1, :]
            v = jnp.where(lane < count[0, first + s], misfit[first + s : first + s + 1, :], 0.0)
            high = v.astype(jnp.bfloat16).astype(jnp.float32)
            middle = (v - high).astype(jnp.bfloat16).astype(jnp.float32)
            low = v - high - middle
            column = iota((COLS, CAP), 0) == (cells & (COLS - 1))
            for i, part in enumerate((high, middle, low)):
                valued[i * COLS : (i + 1) * COLS, at] = jnp.where(column, part, 0.0).astype(jnp.bfloat16)
            place = cells >> 7
            for k in range(LEVELS):
                match = (iota((ROWS, CAP), 0) + k * ROWS) == place
                hot[k * ROWS : (k + 1) * ROWS, at] = jnp.where(match, 1.0, 0.0).astype(jnp.bfloat16)
        part = lax.dot_general(hot[...], valued[...], (((1,), (1,)), ((), ())), preferred_element_type=jnp.float32)
        if first == 0:
            forcing[...] = part
        else:
            forcing[...] += part
    for load in loads:
        load.wait()
    for k in range(LEVELS):
        rows = slice(k * ROWS, (k + 1) * ROWS)
        f = forcing[rows, 0:COLS] + forcing[rows, COLS : 2 * COLS] + forcing[rows, 2 * COLS : 3 * COLS]
        held[k] = adjoint[k] + f
    clear_tail(up)
    clear_tail(down)
    one_step(lambda k: held[k], centre, side, vert, out, edge, up, down)
    spread(slots, up, edge)


def arrivals(from_below, from_above, slots, partner, flip, where, landing, halo):
    sources = slots.shape[0]
    column, top = where[0], where[1]
    source = 0
    for s in range(sources):
        source = jnp.where(partner[s] == column, s, source)
    fold = slots[source, EDGE:SLOT, :]
    back = COLS - 1 - iota((PAD, COLS), 1)
    turned = jnp.take_along_axis(fold, back, axis=1)
    fold = jnp.where(flip[source] == 1, turned, fold)
    landing[...] = jnp.where(top == 1, fold, from_above[...])
    left = jnp.where(column == 0, sources - 1, column - 1)
    right = jnp.where(column == sources - 1, 0, column + 1)
    even = (iota((EDGE, COLS), 1) & 1) == 0
    packed = jnp.where(even, slots[left, 0:EDGE, :], slots[right, 0:EDGE, :])
    for half in range(2):
        rows = packed[8 * half : 8 * half + 8]
        halo[16 * half : 16 * half + 8, :] = rows
        halo[16 * half + 8 : 16 * half + 16, :] = pltpu.roll(rows, COLS - 2 * LEVELS, 1)


def joined(k, part, from_below, landing, halo, mask):
    row, lane = iota((ROWS, COLS), 0), iota((ROWS, COLS), 1)
    sides = halo[...]
    sides = pltpu.roll(sides, COLS - 2 * k, 1) if k else sides
    r = part[k] + jnp.where((lane == 0) | (lane == COLS - 1), sides, 0.0)
    r = r + jnp.where(row == 0, from_below[k : k + 1, :], 0.0)
    r = r + jnp.where(row == ROWS - 1, landing[k : k + 1, :], 0.0)
    return mask[k].astype(jnp.float32) * r


def middle_kernel(part, from_below, from_above, got, partner, flip, where, mask, centre, side, vert, out, slots, up, down, held, edge, landing, halo):
    arrivals(from_below, from_above, got, partner, flip, where, landing, halo)
    for k in range(LEVELS):
        held[k] = joined(k, part, from_below, landing, halo, mask)
    clear_tail(up)
    clear_tail(down)
    one_step(lambda k: held[k], centre, side, vert, out, edge, up, down)
    spread(slots, up, edge)


def last_kernel(part, from_below, from_above, got, partner, flip, where, mask, out, landing, halo):
    arrivals(from_below, from_above, got, partner, flip, where, landing, halo)
    for k in range(LEVELS):
        out[k] = joined(k, part, from_below, landing, halo, mask)


def exchange(slots, up, down, tiles):
    from_below = lax.ppermute(up, "tile", [(i, i + 1) for i in range(tiles - 1)])
    from_above = lax.ppermute(down, "tile", [(i + 1, i) for i in range(tiles - 1)])
    got = lax.all_to_all(slots, "col", split_axis=0, concat_axis=0, tiled=True)
    return from_below, from_above, got


def body(adjoint_in, centre, side_coeff, vert_coeff, land_mask, obs_misfit, obs_cell, obs_count, fold_partner, fold_flip):
    sources = obs_misfit.shape[2]
    tiles = lax.axis_size("tile")
    where = jnp.stack([lax.axis_index("col"), (lax.axis_index("tile") == tiles - 1).astype(jnp.int32)])
    received = lax.all_to_all(obs_misfit, "col", split_axis=2, concat_axis=1, tiled=True)
    f32 = jnp.float32
    tile = jax.ShapeDtypeStruct((LEVELS, ROWS, COLS), f32)
    leaving = (
        tile,
        jax.ShapeDtypeStruct((sources, SLOT, COLS), f32),
        jax.ShapeDtypeStruct((PAD, COLS), f32),
        jax.ShapeDtypeStruct((PAD, COLS), f32),
    )
    held = pltpu.VMEM((LEVELS, ROWS, COLS), f32)
    edge = pltpu.VMEM((EDGE, COLS), f32)
    line = pltpu.VMEM((PAD, COLS), f32)
    params = pltpu.CompilerParams(vmem_limit_bytes=10 * 1024 * 1024)
    group = min(GROUP, sources)
    part, slots, up, down = pl.pallas_call(
        functools.partial(first_kernel, sources),
        out_shape=leaving,
        in_specs=[VMEM, VMEM, SMEM, FAR, FAR, FAR, FAR],
        out_specs=(VMEM,) * 4,
        scratch_shapes=[
            pltpu.VMEM((LEVELS * ROWS, group * CAP), jnp.bfloat16),
            pltpu.VMEM((3 * COLS, group * CAP), jnp.bfloat16),
            pltpu.VMEM((LEVELS * ROWS, 3 * COLS), f32),
            held,
            edge,
            held,
            held,
            pltpu.VMEM((4, LEVELS, ROWS, COLS), f32),
            pltpu.VMEM((2, LEVELS, ROWS, COLS), f32),
            pltpu.SemaphoreType.DMA((4,)),
        ],
        compiler_params=pltpu.CompilerParams(vmem_limit_bytes=60 * 1024 * 1024),
        name="first_step",
    )(
        received.reshape(sources, CAP),
        obs_cell.reshape(sources, CAP),
        obs_count.reshape(1, sources),
        adjoint_in,
        centre,
        side_coeff,
        vert_coeff,
    )
    from_below, from_above, got = exchange(slots, up, down, tiles)
    part, slots, up, down = pl.pallas_call(
        middle_kernel,
        out_shape=leaving,
        in_specs=[VMEM, VMEM, VMEM, VMEM, SMEM, SMEM, SMEM, VMEM, VMEM, VMEM, VMEM],
        out_specs=(VMEM,) * 4,
        scratch_shapes=[held, edge, line, line],
        compiler_params=params,
        name="second_step",
    )(part, from_below, from_above, got, fold_partner, fold_flip, where, land_mask, centre, side_coeff, vert_coeff)
    from_below, from_above, got = exchange(slots, up, down, tiles)
    return pl.pallas_call(
        last_kernel,
        out_shape=tile,
        in_specs=[VMEM, VMEM, VMEM, VMEM, SMEM, SMEM, SMEM, VMEM],
        out_specs=VMEM,
        scratch_shapes=[line, line],
        compiler_params=params,
        name="last_join",
    )(part, from_below, from_above, got, fold_partner, fold_flip, where, land_mask)


def solution(mesh):
    in_specs = (
        P(None, "tile", "col"),
        P(None, "tile", "col"),
        P(None, None, "tile", "col"),
        P(None, None, "tile", "col"),
        P(None, "tile", "col"),
        P("tile", "col", None, None),
        P("tile", "col", None, None),
        P("tile", "col", None),
        P(),
        P(),
    )
    out_specs = P(None, "tile", "col")
    return jax.shard_map(body, mesh=mesh, in_specs=in_specs, out_specs=out_specs, check_vma=False)
```

```python
import functools

import jax
import jax.numpy as jnp
from jax import lax
from jax.experimental import pallas as pl
from jax.experimental.pallas import tpu as pltpu
from jax.sharding import PartitionSpec as P

LEVELS = 25
ROWS = 32
COLS = 128
CAP = 128
GROUP = 8
CHUNK = 5
PAD = 32
LINES = 4 * PAD
CORNER = 3 * LEVELS
EDGE = 80
SLOT = 104
OFFSET = (0, 50, 1, 51)
LIMIT = 60 * 1024 * 1024
VMEM = pl.BlockSpec(memory_space=pltpu.VMEM)
SMEM = pl.BlockSpec(memory_space=pltpu.SMEM)
FAR = pl.BlockSpec(memory_space=pltpu.HBM)


def iota(shape, dim):
    return lax.broadcasted_iota(jnp.int32, shape, dim)


def turn(x, shift, axis=1):
    shift = shift % x.shape[axis]
    return pltpu.roll(x, shift, axis) if shift else x


def terms(k, value, centre, side, vert):
    row, lane = iota((ROWS, COLS), 0), iota((ROWS, COLS), 1)
    y = value[k]
    east, west = side[0, k] * y, side[1, k] * y
    north, south = turn(side[2, k] * y, 1, 0), turn(side[3, k] * y, -1, 0)
    r = centre[k] * y
    r = r + jnp.where(lane > 0, turn(east, 1), 0.0) + jnp.where(lane < COLS - 1, turn(west, -1), 0.0)
    r = r + jnp.where(row > 0, north, 0.0) + jnp.where(row < ROWS - 1, south, 0.0)
    if k + 1 < LEVELS:
        r = r + vert[0, k + 1] * value[k + 1]
    if k > 0:
        r = r + vert[1, k - 1] * value[k - 1]
    return r, east, west, north, south


def outer(lane, last, first):
    return jnp.where(lane == COLS - 1, last, jnp.where(lane == 0, first, 0.0))


def one_hot(sources, misfit, cell, count, hot, valued, forcing):
    group = min(GROUP, sources)
    lane = iota((1, CAP), 1)
    for first in range(0, sources, group):
        for s in range(group):
            at = slice(s * CAP, (s + 1) * CAP)
            cells = cell[first + s : first + s + 1, :]
            v = jnp.where(lane < count[0, first + s], misfit[first + s : first + s + 1, :], 0.0)
            high = v.astype(jnp.bfloat16).astype(jnp.float32)
            middle = (v - high).astype(jnp.bfloat16).astype(jnp.float32)
            low = v - high - middle
            column = iota((COLS, CAP), 0) == (cells & (COLS - 1))
            for i, part in enumerate((high, middle, low)):
                valued[i * COLS : (i + 1) * COLS, at] = jnp.where(column, part, 0.0).astype(jnp.bfloat16)
            place = cells >> 7
            for k in range(LEVELS):
                match = (iota((ROWS, CAP), 0) + k * ROWS) == place
                hot[k * ROWS : (k + 1) * ROWS, at] = jnp.where(match, 1.0, 0.0).astype(jnp.bfloat16)
        part = lax.dot_general(hot[...], valued[...], (((1,), (1,)), ((), ())), preferred_element_type=jnp.float32)
        if first == 0:
            forcing[...] = part
        else:
            forcing[...] += part


def first_kernel(sources, misfit, cell, count, adjoint_far, side_far, centre_far, vert_far, mask_far, out, up, down, edges, hot, valued, forcing, held, adjoint, side, centre, vert, mask, part, arrived, sent):
    loads = [
        pltpu.make_async_copy(far, near, arrived.at[i])
        for i, (far, near) in enumerate(
            ((adjoint_far, adjoint), (side_far, side), (centre_far, centre), (vert_far, vert), (mask_far, mask))
        )
    ]
    for load in loads:
        load.start()
    one_hot(sources, misfit, cell, count, hot, valued, forcing)
    for i in range(4):
        for ref in (up, down):
            ref[i * PAD + 24 : (i + 1) * PAD, :] = jnp.zeros((8, COLS), jnp.float32)
    loads[0].wait()
    for k in range(LEVELS):
        rows = slice(k * ROWS, (k + 1) * ROWS)
        f = forcing[rows, 0:COLS] + forcing[rows, COLS : 2 * COLS] + forcing[rows, 2 * COLS : 3 * COLS]
        held[k] = adjoint[k] + f
    for load in loads[1:]:
        load.wait()
    lane = iota((ROWS, COLS), 1)
    packed = [jnp.zeros((ROWS, COLS), jnp.float32)] * 3
    stores = []
    for k in range(LEVELS):
        r, east, west, north, south = terms(k, held, centre, side, vert)
        m = mask[k].astype(jnp.float32)
        part[k] = r
        sides = outer(lane, east, west)
        for ref, leaving, at, which, i in ((up, north[0:1], ROWS - 1, 2, 0), (down, south[ROWS - 1 : ROWS], 0, 3, 1)):
            ref[k : k + 1, :] = leaving
            ref[PAD + k : PAD + k + 1, :] = r[at : at + 1]
            ref[2 * PAD + k : 2 * PAD + k + 1, :] = (m * side[which, k])[at : at + 1]
            ref[3 * PAD + k : 3 * PAD + k + 1, :] = sides[at : at + 1]
        fields = (sides, outer(lane, r, r), m * outer(lane, side[0, k], side[1, k]))
        packed = [p + turn(x, 2 * k + 1) for p, x in zip(packed, fields)]
        if (k + 1) % CHUNK == 0:
            levels = pl.ds(k + 1 - CHUNK, CHUNK)
            store = pltpu.make_async_copy(part.at[levels], out.at[levels], sent.at[k // CHUNK])
            store.start()
            stores.append(store)
    even = (iota((8, COLS), 1) & 1) == 0
    for i, p in enumerate(packed):
        eastward = westward = jnp.zeros((8, COLS), jnp.float32)
        for g, offset in enumerate(OFFSET):
            rows = p[8 * g : 8 * g + 8]
            eastward = eastward + turn(jnp.where(even, rows, 0.0), offset)
            westward = westward + turn(jnp.where(even, 0.0, rows), offset - 1)
        edges[8 * i : 8 * i + 8, :] = eastward
        edges[24 + 8 * i : 32 + 8 * i, :] = westward
    for store in stores:
        store.wait()


def to_lanes(column, offset):
    level = iota((PAD, COLS), 0)
    spot = (iota((PAD, COLS), 1) == 2 * level + offset) & (level < LEVELS)
    return jnp.sum(jnp.where(spot, column, 0.0), axis=0, keepdims=True)


def to_rows(line, offset):
    level = iota((PAD, COLS), 0)
    spot = (iota((PAD, COLS), 1) == 2 * level + offset) & (level < LEVELS)
    return jnp.sum(jnp.where(spot, line, 0.0), axis=1, keepdims=True)


def spot_rows(first, last):
    row = iota((8, COLS), 0)
    return jnp.where(row == 0, first, 0.0) + jnp.where(row == 7, last, 0.0)


def corner_kernel(below, above, up, edges, where, slots, base):
    def ends(ref, start):
        block = ref[start : start + PAD, :]
        return block[:, COLS - 1 : COLS], block[:, 0:1]

    low_last, low_first = ends(below, 0)
    high_last, high_first = ends(above, 0)
    low_east, low_west = ends(below, 3 * PAD)
    high_east, high_west = ends(above, 3 * PAD)
    own_east, own_west = ends(up, 3 * PAD)
    for i in range(3):
        base[i * LEVELS : (i + 1) * LEVELS, :] = up[i * PAD : i * PAD + LEVELS, :]
    base[CORNER : CORNER + 1, :] = (
        to_lanes(low_east, OFFSET[0]) + to_lanes(low_west, OFFSET[1]) + to_lanes(high_west, OFFSET[2]) + to_lanes(high_east, OFFSET[3])
    )
    base[CORNER + 1 : CORNER + 2, :] = to_lanes(own_east, OFFSET[0]) + to_lanes(own_west, OFFSET[1])
    base[CORNER + 2 : EDGE, :] = jnp.zeros((EDGE - CORNER - 2, COLS), jnp.float32)
    base[EDGE:SLOT, :] = edges[0:24, :]
    base[EDGE + 8 : EDGE + 16, :] += spot_rows(to_lanes(low_last, OFFSET[0]), to_lanes(high_last, OFFSET[3]))
    for s in range(slots.shape[0]):
        slots[s] = base[...]
    left = where[2]
    slots[left, EDGE:SLOT, :] = edges[24:48, :]
    slots[left, EDGE + 8 : EDGE + 16, :] = edges[32:40, :] + spot_rows(
        to_lanes(low_first, OFFSET[0]), to_lanes(high_first, OFFSET[3])
    )


def second_kernel(below, above, up, down, edges, got, partner, flip, where, part_far, mask_far, side_far, centre_far, vert_far, out, held, part, mask, side, centre, vert, result, lines, near_sides, far_sides, arrived, sent):
    loads = [
        pltpu.make_async_copy(far, near, arrived.at[i])
        for i, (far, near) in enumerate(
            ((part_far, part), (mask_far, mask), (side_far, side), (centre_far, centre), (vert_far, vert))
        )
    ]
    for load in loads:
        load.start()
    sources = got.shape[0]
    column, top, left, right = where[0], where[1], where[2], where[3]
    at_top = top == 1

    def comes_from(target):
        source = 0
        for s in range(sources):
            source = jnp.where(partner[s] == target, s, source)
        return source

    def turned(rows, source):
        back = COLS - 1 - iota((PAD, COLS), 1)
        return jnp.where(flip[source] == 1, jnp.take_along_axis(rows, back, axis=1), rows)

    level_lane = iota((PAD, COLS), 1)
    source = comes_from(column)
    earlier = comes_from(source)
    before = jnp.where(source == 0, sources - 1, source - 1)
    after = jnp.where(source == sources - 1, 0, source + 1)
    corner_left = got[left, CORNER : CORNER + 1, :]
    corner_right = got[right, CORNER : CORNER + 1, :]
    sum_low = below[PAD : 2 * PAD, :] + down[0:PAD, :]
    sum_low = sum_low + jnp.where(level_lane == 0, to_rows(corner_left, OFFSET[0]), 0.0)
    sum_low = sum_low + jnp.where(level_lane == COLS - 1, to_rows(corner_right, OFFSET[1]), 0.0)
    sum_high = above[PAD : 2 * PAD, :] + up[0:PAD, :]
    sum_high = sum_high + jnp.where(level_lane == 0, to_rows(corner_left, OFFSET[3]), 0.0)
    sum_high = sum_high + jnp.where(level_lane == COLS - 1, to_rows(corner_right, OFFSET[2]), 0.0)
    fold_first = turned(got[source, 0:PAD, :], source)
    sum_fold = got[source, LEVELS : LEVELS + PAD, :] + turned(got[earlier, 0:PAD, :], earlier)
    cross_west = to_rows(got[before, CORNER + 1 : CORNER + 2, :], OFFSET[0])
    cross_east = to_rows(got[after, CORNER + 1 : CORNER + 2, :], OFFSET[1])
    sum_fold = sum_fold + jnp.where(level_lane == 0, cross_west, 0.0) + jnp.where(level_lane == COLS - 1, cross_east, 0.0)
    fold_second = turned(got[source, 2 * LEVELS : 2 * LEVELS + PAD, :] * sum_fold, source)
    lines[0:PAD, :] = jnp.where(at_top, fold_first, above[0:PAD, :])
    lines[PAD : 2 * PAD, :] = below[2 * PAD : 3 * PAD, :] * sum_low
    lines[2 * PAD : 3 * PAD, :] = jnp.where(at_top, fold_second, above[2 * PAD : 3 * PAD, :] * sum_high)
    from_left = comes_from(left)
    from_right = comes_from(right)
    fold_left = turned(got[from_left, 0:PAD, :], from_left)[:, COLS - 1 : COLS]
    fold_right = turned(got[from_right, 0:PAD, :], from_right)[:, 0:1]
    fold_left = jnp.where(at_top, to_lanes(fold_left, OFFSET[3]), 0.0)
    fold_right = jnp.where(at_top, to_lanes(fold_right, OFFSET[3]), 0.0)
    near_left = got[left, EDGE : EDGE + 8, :]
    near_right = got[right, EDGE : EDGE + 8, :]
    next_left = got[left, EDGE + 16 : EDGE + 24, :] * (
        got[left, EDGE + 8 : EDGE + 16, :] + edges[24:32, :] + spot_rows(0.0, fold_left)
    )
    next_right = got[right, EDGE + 16 : EDGE + 24, :] * (
        got[right, EDGE + 8 : EDGE + 16, :] + edges[0:8, :] + spot_rows(0.0, fold_right)
    )
    even = (iota((8, COLS), 1) & 1) == 0
    for ref, from_west, from_east in ((near_sides, near_left, near_right), (far_sides, next_left, next_right)):
        for g, offset in enumerate(OFFSET):
            ref[8 * g : 8 * g + 8, :] = jnp.where(even, turn(from_west, -offset), turn(from_east, -offset - 1))

    row, lane = iota((ROWS, COLS), 0), iota((ROWS, COLS), 1)

    def joined(k, r, sides, first, last):
        r = r + jnp.where((lane == 0) | (lane == COLS - 1), turn(sides[...], -2 * k), 0.0)
        r = r + jnp.where(row == 0, first, 0.0) + jnp.where(row == ROWS - 1, last, 0.0)
        return mask[k].astype(jnp.float32) * r

    loads[0].wait()
    loads[1].wait()
    for k in range(LEVELS):
        held[k] = joined(k, part[k], near_sides, below[k : k + 1, :], lines[k : k + 1, :])
    for load in loads[2:]:
        load.wait()
    stores = []
    for k in range(LEVELS):
        r = terms(k, held, centre, side, vert)[0]
        result[k] = joined(k, r, far_sides, lines[PAD + k : PAD + k + 1, :], lines[2 * PAD + k : 2 * PAD + k + 1, :])
        if (k + 1) % CHUNK == 0:
            levels = pl.ds(k + 1 - CHUNK, CHUNK)
            store = pltpu.make_async_copy(result.at[levels], out.at[levels], sent.at[k // CHUNK])
            store.start()
            stores.append(store)
    for store in stores:
        store.wait()


def body(adjoint_in, centre, side_coeff, vert_coeff, land_mask, obs_misfit, obs_cell, obs_count, fold_partner, fold_flip):
    sources = obs_misfit.shape[2]
    tiles = lax.axis_size("tile")
    column = lax.axis_index("col")
    where = jnp.stack(
        [
            column,
            (lax.axis_index("tile") == tiles - 1).astype(jnp.int32),
            jnp.where(column == 0, sources - 1, column - 1),
            jnp.where(column == sources - 1, 0, column + 1),
        ]
    )
    received = lax.all_to_all(obs_misfit, "col", split_axis=2, concat_axis=1, tiled=True)
    f32 = jnp.float32
    tile = jax.ShapeDtypeStruct((LEVELS, ROWS, COLS), f32)
    lines = jax.ShapeDtypeStruct((LINES, COLS), f32)
    field = pltpu.VMEM((LEVELS, ROWS, COLS), f32)
    whole_mask = pltpu.VMEM((LEVELS, ROWS, COLS), jnp.int32)
    four = pltpu.VMEM((4, LEVELS, ROWS, COLS), f32)
    two = pltpu.VMEM((2, LEVELS, ROWS, COLS), f32)
    copies = pltpu.SemaphoreType.DMA((5,))
    params = pltpu.CompilerParams(vmem_limit_bytes=LIMIT)
    group = min(GROUP, sources)
    part, up, down, edges = pl.pallas_call(
        functools.partial(first_kernel, sources),
        out_shape=(tile, lines, lines, jax.ShapeDtypeStruct((48, COLS), f32)),
        in_specs=[VMEM, VMEM, SMEM, FAR, FAR, FAR, FAR, FAR],
        out_specs=(FAR, VMEM, VMEM, VMEM),
        scratch_shapes=[
            pltpu.VMEM((LEVELS * ROWS, group * CAP), jnp.bfloat16),
            pltpu.VMEM((3 * COLS, group * CAP), jnp.bfloat16),
            pltpu.VMEM((LEVELS * ROWS, 3 * COLS), f32),
            field,
            field,
            four,
            field,
            two,
            whole_mask,
            field,
            copies,
            copies,
        ],
        compiler_params=params,
        name="first_step",
    )(
        received.reshape(sources, CAP),
        obs_cell.reshape(sources, CAP),
        obs_count.reshape(1, sources),
        adjoint_in,
        side_coeff,
        centre,
        vert_coeff,
        land_mask,
    )
    below = lax.ppermute(up, "tile", [(i, i + 1) for i in range(tiles - 1)])
    above = lax.ppermute(down, "tile", [(i + 1, i) for i in range(tiles - 1)])
    slots = pl.pallas_call(
        corner_kernel,
        out_shape=jax.ShapeDtypeStruct((sources, SLOT, COLS), f32),
        in_specs=[VMEM, VMEM, VMEM, VMEM, SMEM],
        out_specs=VMEM,
        scratch_shapes=[pltpu.VMEM((SLOT, COLS), f32)],
        compiler_params=params,
        name="corners",
    )(below, above, up, edges, where)
    got = lax.all_to_all(slots, "col", split_axis=0, concat_axis=0, tiled=True)
    return pl.pallas_call(
        second_kernel,
        out_shape=tile,
        in_specs=[VMEM] * 6 + [SMEM] * 3 + [FAR] * 5,
        out_specs=FAR,
        scratch_shapes=[
            field,
            field,
            whole_mask,
            four,
            field,
            two,
            field,
            pltpu.VMEM((3 * PAD, COLS), f32),
            pltpu.VMEM((ROWS, COLS), f32),
            pltpu.VMEM((ROWS, COLS), f32),
            copies,
            copies,
        ],
        compiler_params=params,
        name="second_step",
    )(below, above, up, down, edges, got, fold_partner, fold_flip, where, part, land_mask, side_coeff, centre, vert_coeff)


def solution(mesh):
    in_specs = (
        P(None, "tile", "col"),
        P(None, "tile", "col"),
        P(None, None, "tile", "col"),
        P(None, None, "tile", "col"),
        P(None, "tile", "col"),
        P("tile", "col", None, None),
        P("tile", "col", None, None),
        P("tile", "col", None),
        P(),
        P(),
    )
    out_specs = P(None, "tile", "col")
    return jax.shard_map(body, mesh=mesh, in_specs=in_specs, out_specs=out_specs, check_vma=False)
```

```python
import functools

import jax
import jax.numpy as jnp
from jax import lax
from jax.experimental import pallas as pl
from jax.experimental.pallas import tpu as pltpu
from jax.sharding import PartitionSpec as P

LEVELS = 25
ROWS = 32
COLS = 128
CAP = 128
GROUP = 8
CHUNK = 5
PAD = 32
LINES = 4 * PAD
CORNER = 3 * LEVELS
SLOT = 80
EDGE = 32
READY = 6 * PAD + 16
OFFSET = (0, 50, 1, 51)
LIMIT = 60 * 1024 * 1024
VMEM = pl.BlockSpec(memory_space=pltpu.VMEM)
SMEM = pl.BlockSpec(memory_space=pltpu.SMEM)
FAR = pl.BlockSpec(memory_space=pltpu.HBM)


def iota(shape, dim):
    return lax.broadcasted_iota(jnp.int32, shape, dim)


def turn(x, shift, axis=1):
    shift = shift % x.shape[axis]
    return pltpu.roll(x, shift, axis) if shift else x


def terms(k, value, centre, side, vert):
    row, lane = iota((ROWS, COLS), 0), iota((ROWS, COLS), 1)
    y = value[k]
    east, west = side[0, k] * y, side[1, k] * y
    north, south = turn(side[2, k] * y, 1, 0), turn(side[3, k] * y, -1, 0)
    r = centre[k] * y
    r = r + jnp.where(lane > 0, turn(east, 1), 0.0) + jnp.where(lane < COLS - 1, turn(west, -1), 0.0)
    r = r + jnp.where(row > 0, north, 0.0) + jnp.where(row < ROWS - 1, south, 0.0)
    if k + 1 < LEVELS:
        r = r + vert[0, k + 1] * value[k + 1]
    if k > 0:
        r = r + vert[1, k - 1] * value[k - 1]
    return r, east, west, north, south


def outer(lane, last, first):
    return jnp.where(lane == COLS - 1, last, jnp.where(lane == 0, first, 0.0))


def one_hot(sources, misfit, cell, count, hot, valued, forcing):
    group = min(GROUP, sources)
    lane = iota((1, CAP), 1)
    for first in range(0, sources, group):
        for s in range(group):
            at = slice(s * CAP, (s + 1) * CAP)
            cells = cell[first + s : first + s + 1, :]
            v = jnp.where(lane < count[0, first + s], misfit[first + s : first + s + 1, :], 0.0)
            high = v.astype(jnp.bfloat16).astype(jnp.float32)
            middle = (v - high).astype(jnp.bfloat16).astype(jnp.float32)
            low = v - high - middle
            column = iota((COLS, CAP), 0) == (cells & (COLS - 1))
            for i, part in enumerate((high, middle, low)):
                valued[i * COLS : (i + 1) * COLS, at] = jnp.where(column, part, 0.0).astype(jnp.bfloat16)
            place = cells >> 7
            for k in range(LEVELS):
                match = (iota((ROWS, CAP), 0) + k * ROWS) == place
                hot[k * ROWS : (k + 1) * ROWS, at] = jnp.where(match, 1.0, 0.0).astype(jnp.bfloat16)
        part = lax.dot_general(hot[...], valued[...], (((1,), (1,)), ((), ())), preferred_element_type=jnp.float32)
        if first == 0:
            forcing[...] = part
        else:
            forcing[...] += part


def to_lanes(column, offset):
    level = iota((PAD, COLS), 0)
    spot = (iota((PAD, COLS), 1) == 2 * level + offset) & (level < LEVELS)
    return jnp.sum(jnp.where(spot, column, 0.0), axis=0, keepdims=True)


def to_rows(line, offset):
    level = iota((PAD, COLS), 0)
    spot = (iota((PAD, COLS), 1) == 2 * level + offset) & (level < LEVELS)
    return jnp.sum(jnp.where(spot, line, 0.0), axis=1, keepdims=True)


def spot_rows(first, last):
    row = iota((8, COLS), 0)
    return jnp.where(row == 0, first, 0.0) + jnp.where(row == 7, last, 0.0)


def ends(block):
    return block[:, COLS - 1 : COLS], block[:, 0:1]


def from_tiles(swapped, next_swapped, where, start):
    rows = slice(start, start + PAD)
    upward = where[4] == 0
    return (
        jnp.where(upward, next_swapped[rows, :], swapped[rows, :]),
        jnp.where(upward, swapped[rows, :], next_swapped[rows, :]),
    )


def first_kernel(sources, misfit, cell, count, where, adjoint_far, side_far, centre_far, vert_far, mask_far, out, swap, next_swap, edges, slots, hot, valued, forcing, held, adjoint, side, centre, vert, mask, part, up, down, base, arrived, sent, spread):
    loads = [
        pltpu.make_async_copy(far, near, arrived.at[i])
        for i, (far, near) in enumerate(
            ((adjoint_far, adjoint), (side_far, side), (centre_far, centre), (vert_far, vert), (mask_far, mask))
        )
    ]
    for load in loads:
        load.start()
    one_hot(sources, misfit, cell, count, hot, valued, forcing)
    for i in range(4):
        for ref in (up, down):
            ref[i * PAD + 24 : (i + 1) * PAD, :] = jnp.zeros((8, COLS), jnp.float32)
    loads[0].wait()
    for k in range(LEVELS):
        rows = slice(k * ROWS, (k + 1) * ROWS)
        f = forcing[rows, 0:COLS] + forcing[rows, COLS : 2 * COLS] + forcing[rows, 2 * COLS : 3 * COLS]
        held[k] = adjoint[k] + f
    for load in loads[1:]:
        load.wait()
    lane = iota((ROWS, COLS), 1)
    packed = [jnp.zeros((ROWS, COLS), jnp.float32)] * 3
    stores = []
    for k in range(LEVELS):
        r, east, west, north, south = terms(k, held, centre, side, vert)
        m = mask[k].astype(jnp.float32)
        part[k] = r
        sides = outer(lane, east, west)
        for ref, leaving, at, which, i in ((up, north[0:1], ROWS - 1, 2, 0), (down, south[ROWS - 1 : ROWS], 0, 3, 1)):
            ref[k : k + 1, :] = leaving
            ref[PAD + k : PAD + k + 1, :] = r[at : at + 1]
            ref[2 * PAD + k : 2 * PAD + k + 1, :] = (m * side[which, k])[at : at + 1]
            ref[3 * PAD + k : 3 * PAD + k + 1, :] = sides[at : at + 1]
        fields = (sides, outer(lane, r, r), m * outer(lane, side[0, k], side[1, k]))
        packed = [p + turn(x, 2 * k + 1) for p, x in zip(packed, fields)]
        if (k + 1) % CHUNK == 0:
            levels = pl.ds(k + 1 - CHUNK, CHUNK)
            store = pltpu.make_async_copy(part.at[levels], out.at[levels], sent.at[k // CHUNK])
            store.start()
            stores.append(store)
    for i in range(3):
        base[i * LEVELS : (i + 1) * LEVELS, :] = up[i * PAD : i * PAD + LEVELS, :]
    own_east, own_west = ends(up[3 * PAD : 4 * PAD, :])
    base[CORNER : CORNER + 1, :] = to_lanes(own_east, OFFSET[0]) + to_lanes(own_west, OFFSET[1])
    base[CORNER + 1 : SLOT, :] = jnp.zeros((SLOT - CORNER - 1, COLS), jnp.float32)
    for s in range(sources):
        store = pltpu.make_async_copy(base, slots.at[s], spread.at[s])
        store.start()
        stores.append(store)
    upward = where[4] == 0
    swap[...] = jnp.where(upward, up[...], down[...])
    next_swap[...] = jnp.where(upward, down[...], up[...])
    even = (iota((8, COLS), 1) & 1) == 0
    for i, p in enumerate(packed):
        eastward = westward = jnp.zeros((8, COLS), jnp.float32)
        for g, offset in enumerate(OFFSET):
            rows = p[8 * g : 8 * g + 8]
            eastward = eastward + turn(jnp.where(even, rows, 0.0), offset)
            westward = westward + turn(jnp.where(even, 0.0, rows), offset - 1)
        edges[8 * i : 8 * i + 8, :] = eastward
        edges[24 + 8 * i : 32 + 8 * i, :] = westward
    for store in stores:
        store.wait()


def corner_kernel(swapped, next_swapped, sent_first, sent_next, edges, where, part_far, swap, next_swap, ready, part, loaded):
    load = pltpu.make_async_copy(part_far, part, loaded)
    load.start()
    own_down, own_up = from_tiles(sent_first, sent_next, where, 0)
    below_part, above_part = from_tiles(swapped, next_swapped, where, PAD)
    below_scale, above_scale = from_tiles(swapped, next_swapped, where, 2 * PAD)
    low, high = from_tiles(swapped, next_swapped, where, 0)
    low_sides, high_sides = from_tiles(swapped, next_swapped, where, 3 * PAD)
    low_last, low_first = ends(low)
    high_last, high_first = ends(high)
    low_east, low_west = ends(low_sides)
    high_east, high_west = ends(high_sides)
    corners = (
        to_lanes(low_east, OFFSET[0]) + to_lanes(low_west, OFFSET[1]) + to_lanes(high_west, OFFSET[2]) + to_lanes(high_east, OFFSET[3])
    )
    eastward = spot_rows(to_lanes(low_last, OFFSET[0]), to_lanes(high_last, OFFSET[3]))
    westward = spot_rows(to_lanes(low_first, OFFSET[0]), to_lanes(high_first, OFFSET[3]))
    to_east = where[5] == 0
    for ref, chosen in ((swap, to_east), (next_swap, jnp.logical_not(to_east))):
        ref[0:24, :] = jnp.where(chosen, edges[0:24, :], edges[24:48, :])
        ref[8:16, :] += jnp.where(chosen, eastward, westward)
        ref[24:EDGE, :] = jnp.where(iota((EDGE - 24, COLS), 0) == 0, corners, 0.0)
    for i, rows in enumerate((low, high, below_part + own_down, above_part + own_up, below_scale, above_scale)):
        ready[i * PAD : (i + 1) * PAD, :] = rows
    ready[6 * PAD : 6 * PAD + 8, :] = edges[0:8, :]
    ready[6 * PAD + 8 : READY, :] = edges[24:32, :]
    load.wait()


def second_kernel(ready, beside, next_beside, got, partner, flip, where, part, mask, side, centre, vert, out, held, lines, near_sides, far_sides, west_side, east_side):
    sources = got.shape[0]
    below_near, above_near, sum_low, sum_high, below_scale, above_scale = (
        ready[i * PAD : (i + 1) * PAD, :] for i in range(6)
    )
    even_column = where[5] == 0
    west_side[...] = jnp.where(even_column, next_beside[...], beside[...])
    east_side[...] = jnp.where(even_column, beside[...], next_beside[...])
    column, top, left, right = where[0], where[1], where[2], where[3]
    at_top = top == 1

    def comes_from(target):
        source = 0
        for s in range(sources):
            source = jnp.where(partner[s] == target, s, source)
        return source

    def turned(rows, source):
        back = COLS - 1 - iota((PAD, COLS), 1)
        return jnp.where(flip[source] == 1, jnp.take_along_axis(rows, back, axis=1), rows)

    level_lane = iota((PAD, COLS), 1)
    source = comes_from(column)
    earlier = comes_from(source)
    before = jnp.where(source == 0, sources - 1, source - 1)
    after = jnp.where(source == sources - 1, 0, source + 1)
    corner_left = west_side[24:25, :]
    corner_right = east_side[24:25, :]
    sum_low = sum_low + jnp.where(level_lane == 0, to_rows(corner_left, OFFSET[0]), 0.0)
    sum_low = sum_low + jnp.where(level_lane == COLS - 1, to_rows(corner_right, OFFSET[1]), 0.0)
    sum_high = sum_high + jnp.where(level_lane == 0, to_rows(corner_left, OFFSET[3]), 0.0)
    sum_high = sum_high + jnp.where(level_lane == COLS - 1, to_rows(corner_right, OFFSET[2]), 0.0)
    fold_first = turned(got[source, 0:PAD, :], source)
    sum_fold = got[source, LEVELS : LEVELS + PAD, :] + turned(got[earlier, 0:PAD, :], earlier)
    cross_west = to_rows(got[before, CORNER : CORNER + 1, :], OFFSET[0])
    cross_east = to_rows(got[after, CORNER : CORNER + 1, :], OFFSET[1])
    sum_fold = sum_fold + jnp.where(level_lane == 0, cross_west, 0.0) + jnp.where(level_lane == COLS - 1, cross_east, 0.0)
    fold_second = turned(turn(got[source, SLOT - PAD : SLOT, :], SLOT - PAD - 2 * LEVELS, 0) * sum_fold, source)
    lines[0:PAD, :] = jnp.where(at_top, fold_first, above_near)
    lines[PAD : 2 * PAD, :] = below_scale * sum_low
    lines[2 * PAD : 3 * PAD, :] = jnp.where(at_top, fold_second, above_scale * sum_high)
    lines[3 * PAD : 4 * PAD, :] = below_near
    from_left = comes_from(left)
    from_right = comes_from(right)
    fold_left = turned(got[from_left, 0:PAD, :], from_left)[:, COLS - 1 : COLS]
    fold_right = turned(got[from_right, 0:PAD, :], from_right)[:, 0:1]
    fold_left = jnp.where(at_top, to_lanes(fold_left, OFFSET[3]), 0.0)
    fold_right = jnp.where(at_top, to_lanes(fold_right, OFFSET[3]), 0.0)
    near_left = west_side[0:8, :]
    near_right = east_side[0:8, :]
    next_left = west_side[16:24, :] * (west_side[8:16, :] + ready[6 * PAD + 8 : READY, :] + spot_rows(0.0, fold_left))
    next_right = east_side[16:24, :] * (east_side[8:16, :] + ready[6 * PAD : 6 * PAD + 8, :] + spot_rows(0.0, fold_right))
    even = (iota((8, COLS), 1) & 1) == 0
    for ref, from_west, from_east in ((near_sides, near_left, near_right), (far_sides, next_left, next_right)):
        for g, offset in enumerate(OFFSET):
            ref[8 * g : 8 * g + 8, :] = jnp.where(even, turn(from_west, -offset), turn(from_east, -offset - 1))

    row, lane = iota((ROWS, COLS), 0), iota((ROWS, COLS), 1)

    def joined(k, r, sides, first, last):
        r = r + jnp.where((lane == 0) | (lane == COLS - 1), turn(sides[...], -2 * k), 0.0)
        r = r + jnp.where(row == 0, first, 0.0) + jnp.where(row == ROWS - 1, last, 0.0)
        return mask[k].astype(jnp.float32) * r

    for k in range(LEVELS):
        held[k] = joined(k, part[k], near_sides, lines[3 * PAD + k : 3 * PAD + k + 1, :], lines[k : k + 1, :])
    for k in range(LEVELS):
        r = terms(k, held, centre, side, vert)[0]
        out[k] = joined(k, r, far_sides, lines[PAD + k : PAD + k + 1, :], lines[2 * PAD + k : 2 * PAD + k + 1, :])


def body(adjoint_in, centre, side_coeff, vert_coeff, land_mask, obs_misfit, obs_cell, obs_count, fold_partner, fold_flip):
    sources = obs_misfit.shape[2]
    tiles = lax.axis_size("tile")
    column, tile_row = lax.axis_index("col"), lax.axis_index("tile")
    where = jnp.stack(
        [
            column,
            (tile_row == tiles - 1).astype(jnp.int32),
            jnp.where(column == 0, sources - 1, column - 1),
            jnp.where(column == sources - 1, 0, column + 1),
            tile_row & 1,
            column & 1,
        ]
    )
    received = lax.all_to_all(obs_misfit, "col", split_axis=2, concat_axis=1, tiled=True)
    f32 = jnp.float32
    tile = jax.ShapeDtypeStruct((LEVELS, ROWS, COLS), f32)
    lines = jax.ShapeDtypeStruct((LINES, COLS), f32)
    field = pltpu.VMEM((LEVELS, ROWS, COLS), f32)
    whole_mask = pltpu.VMEM((LEVELS, ROWS, COLS), jnp.int32)
    four = pltpu.VMEM((4, LEVELS, ROWS, COLS), f32)
    two = pltpu.VMEM((2, LEVELS, ROWS, COLS), f32)
    copies = pltpu.SemaphoreType.DMA((5,))
    group = min(GROUP, sources)
    part, swap, next_swap, edges, slots = pl.pallas_call(
        functools.partial(first_kernel, sources),
        out_shape=(tile, lines, lines, jax.ShapeDtypeStruct((48, COLS), f32), jax.ShapeDtypeStruct((sources, SLOT, COLS), f32)),
        in_specs=[VMEM, VMEM, SMEM, SMEM, FAR, FAR, FAR, FAR, FAR],
        out_specs=(FAR, VMEM, VMEM, VMEM, FAR),
        scratch_shapes=[
            pltpu.VMEM((LEVELS * ROWS, group * CAP), jnp.bfloat16),
            pltpu.VMEM((3 * COLS, group * CAP), jnp.bfloat16),
            pltpu.VMEM((LEVELS * ROWS, 3 * COLS), f32),
            field,
            field,
            four,
            field,
            two,
            whole_mask,
            field,
            pltpu.VMEM((LINES, COLS), f32),
            pltpu.VMEM((LINES, COLS), f32),
            pltpu.VMEM((SLOT, COLS), f32),
            copies,
            copies,
            pltpu.SemaphoreType.DMA((sources,)),
        ],
        compiler_params=pltpu.CompilerParams(vmem_limit_bytes=LIMIT),
        name="first_step",
    )(
        received.reshape(sources, CAP),
        obs_cell.reshape(sources, CAP),
        obs_count.reshape(1, sources),
        where,
        adjoint_in,
        side_coeff,
        centre,
        vert_coeff,
        land_mask,
    )
    got = lax.all_to_all(slots, "col", split_axis=0, concat_axis=0, tiled=True)
    next_swapped = lax.ppermute(next_swap, "tile", swaps(1, tiles - 1))
    swapped = lax.ppermute(swap, "tile", swaps(0, tiles))
    edge = jax.ShapeDtypeStruct((EDGE, COLS), f32)
    beside, next_beside, ready, part = pl.pallas_call(
        corner_kernel,
        out_shape=(edge, edge, jax.ShapeDtypeStruct((READY, COLS), f32), tile),
        in_specs=[VMEM, VMEM, VMEM, VMEM, VMEM, SMEM, FAR],
        out_specs=(VMEM,) * 4,
        scratch_shapes=[pltpu.SemaphoreType.DMA],
        compiler_params=pltpu.CompilerParams(vmem_limit_bytes=4 * 1024 * 1024),
        cost_estimate=pl.CostEstimate(flops=10**6, bytes_accessed=4 * 10**6, transcendentals=0),
        name="corners",
    )(swapped, next_swapped, swap, next_swap, edges, where, part)
    round_trip = [(sources - 1, 0), (0, sources - 1)]
    next_beside = lax.ppermute(next_beside, "col", swaps(1, sources - 1) + round_trip)
    beside = lax.ppermute(beside, "col", swaps(0, sources))
    return pl.pallas_call(
        second_kernel,
        out_shape=tile,
        in_specs=[VMEM] * 4 + [SMEM] * 3 + [VMEM] * 5,
        out_specs=VMEM,
        scratch_shapes=[
            field,
            pltpu.VMEM((4 * PAD, COLS), f32),
            pltpu.VMEM((ROWS, COLS), f32),
            pltpu.VMEM((ROWS, COLS), f32),
            pltpu.VMEM((EDGE, COLS), f32),
            pltpu.VMEM((EDGE, COLS), f32),
        ],
        compiler_params=pltpu.CompilerParams(vmem_limit_bytes=8 * 1024 * 1024),
        name="second_step",
    )(
        ready,
        beside,
        next_beside,
        got,
        fold_partner,
        fold_flip,
        where,
        part,
        land_mask,
        side_coeff,
        centre,
        vert_coeff,
    )


def swaps(first, end):
    return [pair for i in range(first, end - 1, 2) for pair in ((i, i + 1), (i + 1, i))]


def solution(mesh):
    in_specs = (
        P(None, "tile", "col"),
        P(None, "tile", "col"),
        P(None, None, "tile", "col"),
        P(None, None, "tile", "col"),
        P(None, "tile", "col"),
        P("tile", "col", None, None),
        P("tile", "col", None, None),
        P("tile", "col", None),
        P(),
        P(),
    )
    out_specs = P(None, "tile", "col")
    return jax.shard_map(body, mesh=mesh, in_specs=in_specs, out_specs=out_specs, check_vma=False)
```

```python
import functools

import jax
import jax.numpy as jnp
from jax import lax
from jax.experimental import pallas as pl
from jax.experimental.pallas import tpu as pltpu
from jax.sharding import PartitionSpec as P

LEVELS = 25
ROWS = 32
COLS = 128
CAP = 128
GROUP = 8
PAD = 32
LINES = 4 * PAD
CORNER = 3 * LEVELS
SLOT = 80
EDGE = 32
OFFSET = (0, 50, 1, 51)
MIB = 1024 * 1024
VMEM = pl.BlockSpec(memory_space=pltpu.VMEM)
SMEM = pl.BlockSpec(memory_space=pltpu.SMEM)


def iota(shape, dim):
    return lax.broadcasted_iota(jnp.int32, shape, dim)


def turn(x, shift, axis=1):
    shift = shift % x.shape[axis]
    return pltpu.roll(x, shift, axis) if shift else x


def terms(k, value, centre, side, vert):
    row, lane = iota((ROWS, COLS), 0), iota((ROWS, COLS), 1)
    y = value[k]
    east, west = side[0, k] * y, side[1, k] * y
    north, south = turn(side[2, k] * y, 1, 0), turn(side[3, k] * y, -1, 0)
    r = centre[k] * y
    r = r + jnp.where(lane > 0, turn(east, 1), 0.0) + jnp.where(lane < COLS - 1, turn(west, -1), 0.0)
    r = r + jnp.where(row > 0, north, 0.0) + jnp.where(row < ROWS - 1, south, 0.0)
    if k + 1 < LEVELS:
        r = r + vert[0, k + 1] * value[k + 1]
    if k > 0:
        r = r + vert[1, k - 1] * value[k - 1]
    return r, east, west, north, south


def outer(lane, last, first):
    return jnp.where(lane == COLS - 1, last, jnp.where(lane == 0, first, 0.0))


def match_kernel(cell, hot):
    for s in range(cell.shape[0]):
        place = cell[s : s + 1, :] >> 7
        for k in range(LEVELS):
            match = (iota((ROWS, CAP), 0) + k * ROWS) == place
            hot[k * ROWS : (k + 1) * ROWS, s * CAP : (s + 1) * CAP] = jnp.where(match, 1.0, 0.0).astype(jnp.bfloat16)


def one_hot(sources, misfit, cell, count, hot, valued, forcing):
    group = min(GROUP, sources)
    lane = iota((1, CAP), 1)
    for first in range(0, sources, group):
        for s in range(group):
            at = slice(s * CAP, (s + 1) * CAP)
            cells = cell[first + s : first + s + 1, :]
            v = jnp.where(lane < count[0, first + s], misfit[first + s : first + s + 1, :], 0.0)
            high = v.astype(jnp.bfloat16).astype(jnp.float32)
            middle = (v - high).astype(jnp.bfloat16).astype(jnp.float32)
            low = v - high - middle
            column = iota((COLS, CAP), 0) == (cells & (COLS - 1))
            for i, part in enumerate((high, middle, low)):
                valued[i * COLS : (i + 1) * COLS, at] = jnp.where(column, part, 0.0).astype(jnp.bfloat16)
        matched = hot[:, first * CAP : (first + group) * CAP]
        part = lax.dot_general(matched, valued[...], (((1,), (1,)), ((), ())), preferred_element_type=jnp.float32)
        if first == 0:
            forcing[...] = part
        else:
            forcing[...] += part


def to_lanes(column, offset):
    level = iota((PAD, COLS), 0)
    spot = (iota((PAD, COLS), 1) == 2 * level + offset) & (level < LEVELS)
    return jnp.sum(jnp.where(spot, column, 0.0), axis=0, keepdims=True)


def to_rows(line, offset):
    level = iota((PAD, COLS), 0)
    spot = (iota((PAD, COLS), 1) == 2 * level + offset) & (level < LEVELS)
    return jnp.sum(jnp.where(spot, line, 0.0), axis=1, keepdims=True)


def spot_rows(first, last):
    row = iota((8, COLS), 0)
    return jnp.where(row == 0, first, 0.0) + jnp.where(row == 7, last, 0.0)


def ends(block):
    return block[:, COLS - 1 : COLS], block[:, 0:1]


def from_tiles(swapped, next_swapped, where, start):
    rows = slice(start, start + PAD)
    upward = where[4] == 0
    return (
        jnp.where(upward, next_swapped[rows, :], swapped[rows, :]),
        jnp.where(upward, swapped[rows, :], next_swapped[rows, :]),
    )


def first_kernel(sources, misfit, cell, count, where, hot, adjoint, side, centre, vert, mask, part, swap, next_swap, edges, slots, valued, forcing, held, up, down, base):
    one_hot(sources, misfit, cell, count, hot, valued, forcing)
    for i in range(4):
        for ref in (up, down):
            ref[i * PAD + 24 : (i + 1) * PAD, :] = jnp.zeros((8, COLS), jnp.float32)
    for k in range(LEVELS):
        rows = slice(k * ROWS, (k + 1) * ROWS)
        f = forcing[rows, 0:COLS] + forcing[rows, COLS : 2 * COLS] + forcing[rows, 2 * COLS : 3 * COLS]
        held[k] = adjoint[k] + f
    lane = iota((ROWS, COLS), 1)
    packed = [jnp.zeros((ROWS, COLS), jnp.float32)] * 3
    for k in range(LEVELS):
        r, east, west, north, south = terms(k, held, centre, side, vert)
        m = mask[k].astype(jnp.float32)
        part[k] = r
        sides = outer(lane, east, west)
        for ref, leaving, at, which, i in ((up, north[0:1], ROWS - 1, 2, 0), (down, south[ROWS - 1 : ROWS], 0, 3, 1)):
            ref[k : k + 1, :] = leaving
            ref[PAD + k : PAD + k + 1, :] = r[at : at + 1]
            ref[2 * PAD + k : 2 * PAD + k + 1, :] = (m * side[which, k])[at : at + 1]
            ref[3 * PAD + k : 3 * PAD + k + 1, :] = sides[at : at + 1]
        fields = (sides, outer(lane, r, r), m * outer(lane, side[0, k], side[1, k]))
        packed = [p + turn(x, 2 * k + 1) for p, x in zip(packed, fields)]
    for i in range(3):
        base[i * LEVELS : (i + 1) * LEVELS, :] = up[i * PAD : i * PAD + LEVELS, :]
    own_east, own_west = ends(up[3 * PAD : 4 * PAD, :])
    base[CORNER : CORNER + 1, :] = to_lanes(own_east, OFFSET[0]) + to_lanes(own_west, OFFSET[1])
    base[CORNER + 1 : SLOT, :] = jnp.zeros((SLOT - CORNER - 1, COLS), jnp.float32)
    for s in range(sources):
        slots[s] = base[...]
    upward = where[4] == 0
    swap[...] = jnp.where(upward, up[...], down[...])
    next_swap[...] = jnp.where(upward, down[...], up[...])
    even = (iota((8, COLS), 1) & 1) == 0
    for i, p in enumerate(packed):
        eastward = westward = jnp.zeros((8, COLS), jnp.float32)
        for g, offset in enumerate(OFFSET):
            rows = p[8 * g : 8 * g + 8]
            eastward = eastward + turn(jnp.where(even, rows, 0.0), offset)
            westward = westward + turn(jnp.where(even, 0.0, rows), offset - 1)
        edges[8 * i : 8 * i + 8, :] = eastward
        edges[24 + 8 * i : 32 + 8 * i, :] = westward


def corner_kernel(swapped, next_swapped, edges, where, swap, next_swap):
    low, high = from_tiles(swapped, next_swapped, where, 0)
    low_sides, high_sides = from_tiles(swapped, next_swapped, where, 3 * PAD)
    low_last, low_first = ends(low)
    high_last, high_first = ends(high)
    low_east, low_west = ends(low_sides)
    high_east, high_west = ends(high_sides)
    corners = (
        to_lanes(low_east, OFFSET[0]) + to_lanes(low_west, OFFSET[1]) + to_lanes(high_west, OFFSET[2]) + to_lanes(high_east, OFFSET[3])
    )
    eastward = spot_rows(to_lanes(low_last, OFFSET[0]), to_lanes(high_last, OFFSET[3]))
    westward = spot_rows(to_lanes(low_first, OFFSET[0]), to_lanes(high_first, OFFSET[3]))
    to_east = where[5] == 0
    for ref, chosen in ((swap, to_east), (next_swap, jnp.logical_not(to_east))):
        ref[0:24, :] = jnp.where(chosen, edges[0:24, :], edges[24:48, :])
        ref[8:16, :] += jnp.where(chosen, eastward, westward)
        ref[24:EDGE, :] = jnp.where(iota((EDGE - 24, COLS), 0) == 0, corners, 0.0)


def second_kernel(swapped, next_swapped, sent_first, sent_next, beside, next_beside, edges, got, partner, flip, where, part, mask, side, centre, vert, out, held, lines, near_sides, far_sides, west_side, east_side):
    sources = got.shape[0]
    below_near, above_near = from_tiles(swapped, next_swapped, where, 0)
    below_part, above_part = from_tiles(swapped, next_swapped, where, PAD)
    below_scale, above_scale = from_tiles(swapped, next_swapped, where, 2 * PAD)
    own_down, own_up = from_tiles(sent_first, sent_next, where, 0)
    sum_low, sum_high = below_part + own_down, above_part + own_up
    even_column = where[5] == 0
    west_side[...] = jnp.where(even_column, next_beside[...], beside[...])
    east_side[...] = jnp.where(even_column, beside[...], next_beside[...])
    column, top, left, right = where[0], where[1], where[2], where[3]
    at_top = top == 1

    def comes_from(target):
        source = 0
        for s in range(sources):
            source = jnp.where(partner[s] == target, s, source)
        return source

    def turned(rows, source):
        back = COLS - 1 - iota((PAD, COLS), 1)
        return jnp.where(flip[source] == 1, jnp.take_along_axis(rows, back, axis=1), rows)

    level_lane = iota((PAD, COLS), 1)
    source = comes_from(column)
    earlier = comes_from(source)
    before = jnp.where(source == 0, sources - 1, source - 1)
    after = jnp.where(source == sources - 1, 0, source + 1)
    corner_left = west_side[24:25, :]
    corner_right = east_side[24:25, :]
    sum_low = sum_low + jnp.where(level_lane == 0, to_rows(corner_left, OFFSET[0]), 0.0)
    sum_low = sum_low + jnp.where(level_lane == COLS - 1, to_rows(corner_right, OFFSET[1]), 0.0)
    sum_high = sum_high + jnp.where(level_lane == 0, to_rows(corner_left, OFFSET[3]), 0.0)
    sum_high = sum_high + jnp.where(level_lane == COLS - 1, to_rows(corner_right, OFFSET[2]), 0.0)
    fold_first = turned(got[source, 0:PAD, :], source)
    sum_fold = got[source, LEVELS : LEVELS + PAD, :] + turned(got[earlier, 0:PAD, :], earlier)
    cross_west = to_rows(got[before, CORNER : CORNER + 1, :], OFFSET[0])
    cross_east = to_rows(got[after, CORNER : CORNER + 1, :], OFFSET[1])
    sum_fold = sum_fold + jnp.where(level_lane == 0, cross_west, 0.0) + jnp.where(level_lane == COLS - 1, cross_east, 0.0)
    fold_second = turned(turn(got[source, SLOT - PAD : SLOT, :], SLOT - PAD - 2 * LEVELS, 0) * sum_fold, source)
    lines[0:PAD, :] = jnp.where(at_top, fold_first, above_near)
    lines[PAD : 2 * PAD, :] = below_scale * sum_low
    lines[2 * PAD : 3 * PAD, :] = jnp.where(at_top, fold_second, above_scale * sum_high)
    lines[3 * PAD : 4 * PAD, :] = below_near
    from_left = comes_from(left)
    from_right = comes_from(right)
    fold_left = turned(got[from_left, 0:PAD, :], from_left)[:, COLS - 1 : COLS]
    fold_right = turned(got[from_right, 0:PAD, :], from_right)[:, 0:1]
    fold_left = jnp.where(at_top, to_lanes(fold_left, OFFSET[3]), 0.0)
    fold_right = jnp.where(at_top, to_lanes(fold_right, OFFSET[3]), 0.0)
    near_left = west_side[0:8, :]
    near_right = east_side[0:8, :]
    next_left = west_side[16:24, :] * (west_side[8:16, :] + edges[24:32, :] + spot_rows(0.0, fold_left))
    next_right = east_side[16:24, :] * (east_side[8:16, :] + edges[0:8, :] + spot_rows(0.0, fold_right))
    even = (iota((8, COLS), 1) & 1) == 0
    for ref, from_west, from_east in ((near_sides, near_left, near_right), (far_sides, next_left, next_right)):
        for g, offset in enumerate(OFFSET):
            ref[8 * g : 8 * g + 8, :] = jnp.where(even, turn(from_west, -offset), turn(from_east, -offset - 1))

    row, lane = iota((ROWS, COLS), 0), iota((ROWS, COLS), 1)

    def joined(k, r, sides, first, last):
        r = r + jnp.where((lane == 0) | (lane == COLS - 1), turn(sides[...], -2 * k), 0.0)
        r = r + jnp.where(row == 0, first, 0.0) + jnp.where(row == ROWS - 1, last, 0.0)
        return mask[k].astype(jnp.float32) * r

    for k in range(LEVELS):
        held[k] = joined(k, part[k], near_sides, lines[3 * PAD + k : 3 * PAD + k + 1, :], lines[k : k + 1, :])
    for k in range(LEVELS):
        r = terms(k, held, centre, side, vert)[0]
        out[k] = joined(k, r, far_sides, lines[PAD + k : PAD + k + 1, :], lines[2 * PAD + k : 2 * PAD + k + 1, :])


def body(adjoint_in, centre, side_coeff, vert_coeff, land_mask, obs_misfit, obs_cell, obs_count, fold_partner, fold_flip):
    sources = obs_misfit.shape[2]
    tiles = lax.axis_size("tile")
    column, tile_row = lax.axis_index("col"), lax.axis_index("tile")
    where = jnp.stack(
        [
            column,
            (tile_row == tiles - 1).astype(jnp.int32),
            jnp.where(column == 0, sources - 1, column - 1),
            jnp.where(column == sources - 1, 0, column + 1),
            tile_row & 1,
            column & 1,
        ]
    )
    received = lax.all_to_all(obs_misfit, "col", split_axis=2, concat_axis=1, tiled=True)
    f32 = jnp.float32
    tile = jax.ShapeDtypeStruct((LEVELS, ROWS, COLS), f32)
    lines = jax.ShapeDtypeStruct((LINES, COLS), f32)
    field = pltpu.VMEM((LEVELS, ROWS, COLS), f32)
    group = min(GROUP, sources)
    small = sources <= GROUP
    cells = obs_cell.reshape(sources, CAP)
    hot = pl.pallas_call(
        match_kernel,
        out_shape=jax.ShapeDtypeStruct((LEVELS * ROWS, sources * CAP), jnp.bfloat16),
        in_specs=[VMEM],
        out_specs=VMEM,
        compiler_params=pltpu.CompilerParams(vmem_limit_bytes=(4 if small else 24) * MIB),
        cost_estimate=pl.CostEstimate(flops=10**10, bytes_accessed=2 * 10**8, transcendentals=0),
        name="match_rows",
    )(cells)
    part, swap, next_swap, edges, slots = pl.pallas_call(
        functools.partial(first_kernel, sources),
        out_shape=(tile, lines, lines, jax.ShapeDtypeStruct((48, COLS), f32), jax.ShapeDtypeStruct((sources, SLOT, COLS), f32)),
        in_specs=[VMEM, VMEM, SMEM, SMEM] + [VMEM] * 6,
        out_specs=(VMEM,) * 5,
        scratch_shapes=[
            pltpu.VMEM((3 * COLS, group * CAP), jnp.bfloat16),
            pltpu.VMEM((LEVELS * ROWS, 3 * COLS), f32),
            field,
            pltpu.VMEM((LINES, COLS), f32),
            pltpu.VMEM((LINES, COLS), f32),
            pltpu.VMEM((SLOT, COLS), f32),
        ],
        compiler_params=pltpu.CompilerParams(vmem_limit_bytes=(8 if small else 40) * MIB),
        name="first_step",
    )(
        received.reshape(sources, CAP),
        cells,
        obs_count.reshape(1, sources),
        where,
        hot,
        adjoint_in,
        side_coeff,
        centre,
        vert_coeff,
        land_mask,
    )
    got = lax.all_to_all(slots, "col", split_axis=0, concat_axis=0, tiled=True)
    next_swapped = lax.ppermute(next_swap, "tile", swaps(1, tiles - 1))
    swapped = lax.ppermute(swap, "tile", swaps(0, tiles))
    edge = jax.ShapeDtypeStruct((EDGE, COLS), f32)
    beside, next_beside = pl.pallas_call(
        corner_kernel,
        out_shape=(edge, edge),
        in_specs=[VMEM, VMEM, VMEM, SMEM],
        out_specs=(VMEM, VMEM),
        compiler_params=pltpu.CompilerParams(vmem_limit_bytes=4 * MIB),
        cost_estimate=pl.CostEstimate(flops=10**6, bytes_accessed=4 * 10**6, transcendentals=0),
        name="corners",
    )(swapped, next_swapped, edges, where)
    round_trip = [(sources - 1, 0), (0, sources - 1)]
    next_beside = lax.ppermute(next_beside, "col", swaps(1, sources - 1) + round_trip)
    beside = lax.ppermute(beside, "col", swaps(0, sources))
    return pl.pallas_call(
        second_kernel,
        out_shape=tile,
        in_specs=[VMEM] * 8 + [SMEM] * 3 + [VMEM] * 5,
        out_specs=VMEM,
        scratch_shapes=[
            field,
            pltpu.VMEM((4 * PAD, COLS), f32),
            pltpu.VMEM((ROWS, COLS), f32),
            pltpu.VMEM((ROWS, COLS), f32),
            pltpu.VMEM((EDGE, COLS), f32),
            pltpu.VMEM((EDGE, COLS), f32),
        ],
        compiler_params=pltpu.CompilerParams(vmem_limit_bytes=8 * MIB),
        name="second_step",
    )(
        swapped,
        next_swapped,
        swap,
        next_swap,
        beside,
        next_beside,
        edges,
        got,
        fold_partner,
        fold_flip,
        where,
        part,
        land_mask,
        side_coeff,
        centre,
        vert_coeff,
    )


def swaps(first, end):
    return [pair for i in range(first, end - 1, 2) for pair in ((i, i + 1), (i + 1, i))]


def solution(mesh):
    in_specs = (
        P(None, "tile", "col"),
        P(None, "tile", "col"),
        P(None, None, "tile", "col"),
        P(None, None, "tile", "col"),
        P(None, "tile", "col"),
        P("tile", "col", None, None),
        P("tile", "col", None, None),
        P("tile", "col", None),
        P(),
        P(),
    )
    out_specs = P(None, "tile", "col")
    return jax.shard_map(body, mesh=mesh, in_specs=in_specs, out_specs=out_specs, check_vma=False)
```

```python
import functools

import jax
import jax.numpy as jnp
from jax import lax
from jax.experimental import pallas as pl
from jax.experimental.pallas import tpu as pltpu
from jax.sharding import PartitionSpec as P

LEVELS = 25
ROWS = 32
COLS = 128
CAP = 128
GROUP = 8
PAD = 32
LINES = 4 * PAD
CORNER = 3 * LEVELS
SLOT = 80
EDGE = 32
OFFSET = (0, 50, 1, 51)
EDGES = 48 + 2 * PAD
LAND = 1e38
MIB = 1024 * 1024
VMEM = pl.BlockSpec(memory_space=pltpu.VMEM)
SMEM = pl.BlockSpec(memory_space=pltpu.SMEM)


def iota(shape, dim):
    return lax.broadcasted_iota(jnp.int32, shape, dim)


def turn(x, shift, axis=1):
    shift = shift % x.shape[axis]
    return pltpu.roll(x, shift, axis) if shift else x


def terms(k, value, centre, side, vert):
    row, lane = iota((ROWS, COLS), 0), iota((ROWS, COLS), 1)
    y = value[k]
    east, west = side[0, k] * y, side[1, k] * y
    north, south = turn(side[2, k] * y, 1, 0), turn(side[3, k] * y, -1, 0)
    r = centre[k] * y
    r = r + jnp.where(lane > 0, turn(east, 1), 0.0) + jnp.where(lane < COLS - 1, turn(west, -1), 0.0)
    r = r + jnp.where(row > 0, north, 0.0) + jnp.where(row < ROWS - 1, south, 0.0)
    if k + 1 < LEVELS:
        r = r + vert[0, k + 1] * value[k + 1]
    if k > 0:
        r = r + vert[1, k - 1] * value[k - 1]
    return r, east, west, north, south


def outer(lane, last, first):
    return jnp.where(lane == COLS - 1, last, jnp.where(lane == 0, first, 0.0))


def scale_kernel(side, mask, scales):
    lane = iota((ROWS, COLS), 1)
    packed = jnp.zeros((ROWS, COLS), jnp.float32)
    for at in (16, 16 + PAD):
        scales[at + 24 : at + PAD, :] = jnp.zeros((8, COLS), jnp.float32)
    for k in range(LEVELS):
        m = mask[k].astype(jnp.float32)
        packed = packed + turn(m * outer(lane, side[0, k], side[1, k]), 2 * k + 1)
        scales[16 + k : 17 + k, :] = (m * side[2, k])[ROWS - 1 : ROWS]
        scales[16 + PAD + k : 17 + PAD + k, :] = (m * side[3, k])[0:1]
    scales[0:8, :], scales[8:16, :] = tight(packed)


def tight(packed):
    even = (iota((8, COLS), 1) & 1) == 0
    eastward = westward = jnp.zeros((8, COLS), jnp.float32)
    for g, offset in enumerate(OFFSET):
        rows = packed[8 * g : 8 * g + 8]
        eastward = eastward + turn(jnp.where(even, rows, 0.0), offset)
        westward = westward + turn(jnp.where(even, 0.0, rows), offset - 1)
    return eastward, westward


def forcing_kernel(sources, misfit, cell, count, forcing, hot, valued):
    group = min(GROUP, sources)
    lane = iota((1, CAP), 1)
    for first in range(0, sources, group):
        for s in range(group):
            at = slice(s * CAP, (s + 1) * CAP)
            cells = cell[first + s : first + s + 1, :]
            v = jnp.where(lane < count[0, first + s], misfit[first + s : first + s + 1, :], 0.0)
            high = v.astype(jnp.bfloat16).astype(jnp.float32)
            middle = (v - high).astype(jnp.bfloat16).astype(jnp.float32)
            low = v - high - middle
            column = iota((COLS, CAP), 0) == (cells & (COLS - 1))
            for i, part in enumerate((high, middle, low)):
                valued[i * COLS : (i + 1) * COLS, at] = jnp.where(column, part, 0.0).astype(jnp.bfloat16)
            place = cells >> 7
            for k in range(LEVELS):
                match = (iota((ROWS, CAP), 0) + k * ROWS) == place
                hot[k * ROWS : (k + 1) * ROWS, at] = jnp.where(match, 1.0, 0.0).astype(jnp.bfloat16)
        part = lax.dot_general(hot[...], valued[...], (((1,), (1,)), ((), ())), preferred_element_type=jnp.float32)
        part = part[:, 0:COLS] + part[:, COLS : 2 * COLS] + part[:, 2 * COLS : 3 * COLS]
        if first == 0:
            forcing[...] = part
        else:
            forcing[...] += part


def to_lanes(column, offset):
    level = iota((PAD, COLS), 0)
    spot = (iota((PAD, COLS), 1) == 2 * level + offset) & (level < LEVELS)
    return jnp.sum(jnp.where(spot, column, 0.0), axis=0, keepdims=True)


def to_rows(line, offset):
    level = iota((PAD, COLS), 0)
    spot = (iota((PAD, COLS), 1) == 2 * level + offset) & (level < LEVELS)
    return jnp.sum(jnp.where(spot, line, 0.0), axis=1, keepdims=True)


def spot_rows(first, last):
    row = iota((8, COLS), 0)
    return jnp.where(row == 0, first, 0.0) + jnp.where(row == 7, last, 0.0)


def ends(block):
    return block[:, COLS - 1 : COLS], block[:, 0:1]


def from_tiles(swapped, next_swapped, where, start):
    rows = slice(start, start + PAD)
    upward = where[4] == 0
    return (
        jnp.where(upward, next_swapped[rows, :], swapped[rows, :]),
        jnp.where(upward, swapped[rows, :], next_swapped[rows, :]),
    )


def first_kernel(forcing, where, scales, adjoint, side, centre, vert, mask, part, swap, next_swap, edges, slots, held, up, down, base):
    for i in range(4):
        for ref in (up, down):
            ref[i * PAD + 24 : (i + 1) * PAD, :] = jnp.zeros((8, COLS), jnp.float32)
    for k in range(LEVELS):
        held[k] = adjoint[k] + forcing[k * ROWS : (k + 1) * ROWS, :]
    lane = iota((ROWS, COLS), 1)
    packed = [jnp.zeros((ROWS, COLS), jnp.float32)] * 2
    for k in range(LEVELS):
        r, east, west, north, south = terms(k, held, centre, side, vert)
        part[k] = jnp.where(mask[k] == 0, LAND, r)
        sides = outer(lane, east, west)
        for ref, leaving, at in ((up, north[0:1], ROWS - 1), (down, south[ROWS - 1 : ROWS], 0)):
            ref[k : k + 1, :] = leaving
            ref[PAD + k : PAD + k + 1, :] = r[at : at + 1]
            ref[3 * PAD + k : 3 * PAD + k + 1, :] = sides[at : at + 1]
        packed = [p + turn(x, 2 * k + 1) for p, x in zip(packed, (sides, outer(lane, r, r)))]
    up[2 * PAD : 3 * PAD, :] = scales[16 : 16 + PAD, :]
    down[2 * PAD : 3 * PAD, :] = scales[16 + PAD : 16 + 2 * PAD, :]
    for i in range(3):
        base[i * LEVELS : (i + 1) * LEVELS, :] = up[i * PAD : i * PAD + LEVELS, :]
    own_east, own_west = ends(up[3 * PAD : 4 * PAD, :])
    base[CORNER : CORNER + 1, :] = to_lanes(own_east, OFFSET[0]) + to_lanes(own_west, OFFSET[1])
    base[CORNER + 1 : SLOT, :] = jnp.zeros((SLOT - CORNER - 1, COLS), jnp.float32)
    for s in range(slots.shape[0]):
        slots[s] = base[...]
    upward = where[4] == 0
    swap[...] = jnp.where(upward, up[...], down[...])
    next_swap[...] = jnp.where(upward, down[...], up[...])
    for i, p in enumerate(packed):
        edges[8 * i : 8 * i + 8, :], edges[24 + 8 * i : 32 + 8 * i, :] = tight(p)
    edges[16:24, :] = scales[0:8, :]
    edges[40:48, :] = scales[8:16, :]
    edges[48 : 48 + PAD, :] = down[0:PAD, :]
    edges[48 + PAD : EDGES, :] = up[0:PAD, :]


def corner_kernel(swapped, next_swapped, edges, where, swap, next_swap):
    low, high = from_tiles(swapped, next_swapped, where, 0)
    low_sides, high_sides = from_tiles(swapped, next_swapped, where, 3 * PAD)
    low_last, low_first = ends(low)
    high_last, high_first = ends(high)
    low_east, low_west = ends(low_sides)
    high_east, high_west = ends(high_sides)
    corners = (
        to_lanes(low_east, OFFSET[0]) + to_lanes(low_west, OFFSET[1]) + to_lanes(high_west, OFFSET[2]) + to_lanes(high_east, OFFSET[3])
    )
    eastward = spot_rows(to_lanes(low_last, OFFSET[0]), to_lanes(high_last, OFFSET[3]))
    westward = spot_rows(to_lanes(low_first, OFFSET[0]), to_lanes(high_first, OFFSET[3]))
    to_east = where[5] == 0
    for ref, chosen in ((swap, to_east), (next_swap, jnp.logical_not(to_east))):
        ref[0:24, :] = jnp.where(chosen, edges[0:24, :], edges[24:48, :])
        ref[8:16, :] += jnp.where(chosen, eastward, westward)
        ref[24:EDGE, :] = jnp.where(iota((EDGE - 24, COLS), 0) == 0, corners, 0.0)


def second_kernel(swapped, next_swapped, beside, next_beside, edges, got, partner, flip, where, part, side, centre, vert, out, held, lines, near_sides, far_sides, west_side, east_side):
    sources = got.shape[0]
    below_near, above_near = from_tiles(swapped, next_swapped, where, 0)
    below_part, above_part = from_tiles(swapped, next_swapped, where, PAD)
    below_scale, above_scale = from_tiles(swapped, next_swapped, where, 2 * PAD)
    sum_low = below_part + edges[48 : 48 + PAD, :]
    sum_high = above_part + edges[48 + PAD : EDGES, :]
    even_column = where[5] == 0
    west_side[...] = jnp.where(even_column, next_beside[...], beside[...])
    east_side[...] = jnp.where(even_column, beside[...], next_beside[...])
    column, top, left, right = where[0], where[1], where[2], where[3]
    at_top = top == 1

    def comes_from(target):
        source = 0
        for s in range(sources):
            source = jnp.where(partner[s] == target, s, source)
        return source

    def turned(rows, source):
        back = COLS - 1 - iota((PAD, COLS), 1)
        return jnp.where(flip[source] == 1, jnp.take_along_axis(rows, back, axis=1), rows)

    level_lane = iota((PAD, COLS), 1)
    source = comes_from(column)
    earlier = comes_from(source)
    before = jnp.where(source == 0, sources - 1, source - 1)
    after = jnp.where(source == sources - 1, 0, source + 1)
    corner_left = west_side[24:25, :]
    corner_right = east_side[24:25, :]
    sum_low = sum_low + jnp.where(level_lane == 0, to_rows(corner_left, OFFSET[0]), 0.0)
    sum_low = sum_low + jnp.where(level_lane == COLS - 1, to_rows(corner_right, OFFSET[1]), 0.0)
    sum_high = sum_high + jnp.where(level_lane == 0, to_rows(corner_left, OFFSET[3]), 0.0)
    sum_high = sum_high + jnp.where(level_lane == COLS - 1, to_rows(corner_right, OFFSET[2]), 0.0)
    fold_first = turned(got[source, 0:PAD, :], source)
    sum_fold = got[source, LEVELS : LEVELS + PAD, :] + turned(got[earlier, 0:PAD, :], earlier)
    cross_west = to_rows(got[before, CORNER : CORNER + 1, :], OFFSET[0])
    cross_east = to_rows(got[after, CORNER : CORNER + 1, :], OFFSET[1])
    sum_fold = sum_fold + jnp.where(level_lane == 0, cross_west, 0.0) + jnp.where(level_lane == COLS - 1, cross_east, 0.0)
    fold_second = turned(turn(got[source, SLOT - PAD : SLOT, :], SLOT - PAD - 2 * LEVELS, 0) * sum_fold, source)
    lines[0:PAD, :] = jnp.where(at_top, fold_first, above_near)
    lines[PAD : 2 * PAD, :] = below_scale * sum_low
    lines[2 * PAD : 3 * PAD, :] = jnp.where(at_top, fold_second, above_scale * sum_high)
    lines[3 * PAD : 4 * PAD, :] = below_near
    from_left = comes_from(left)
    from_right = comes_from(right)
    fold_left = turned(got[from_left, 0:PAD, :], from_left)[:, COLS - 1 : COLS]
    fold_right = turned(got[from_right, 0:PAD, :], from_right)[:, 0:1]
    fold_left = jnp.where(at_top, to_lanes(fold_left, OFFSET[3]), 0.0)
    fold_right = jnp.where(at_top, to_lanes(fold_right, OFFSET[3]), 0.0)
    near_left = west_side[0:8, :]
    near_right = east_side[0:8, :]
    next_left = west_side[16:24, :] * (west_side[8:16, :] + edges[24:32, :] + spot_rows(0.0, fold_left))
    next_right = east_side[16:24, :] * (east_side[8:16, :] + edges[0:8, :] + spot_rows(0.0, fold_right))
    even = (iota((8, COLS), 1) & 1) == 0
    for ref, from_west, from_east in ((near_sides, near_left, near_right), (far_sides, next_left, next_right)):
        for g, offset in enumerate(OFFSET):
            ref[8 * g : 8 * g + 8, :] = jnp.where(even, turn(from_west, -offset), turn(from_east, -offset - 1))

    row, lane = iota((ROWS, COLS), 0), iota((ROWS, COLS), 1)

    def joined(k, r, sides, first, last):
        r = r + jnp.where((lane == 0) | (lane == COLS - 1), turn(sides[...], -2 * k), 0.0)
        r = r + jnp.where(row == 0, first, 0.0) + jnp.where(row == ROWS - 1, last, 0.0)
        return jnp.where(part[k] == LAND, 0.0, r)

    for k in range(LEVELS):
        held[k] = joined(k, part[k], near_sides, lines[3 * PAD + k : 3 * PAD + k + 1, :], lines[k : k + 1, :])
    for k in range(LEVELS):
        r = terms(k, held, centre, side, vert)[0]
        out[k] = joined(k, r, far_sides, lines[PAD + k : PAD + k + 1, :], lines[2 * PAD + k : 2 * PAD + k + 1, :])


def body(adjoint_in, centre, side_coeff, vert_coeff, land_mask, obs_misfit, obs_cell, obs_count, fold_partner, fold_flip):
    sources = obs_misfit.shape[2]
    tiles = lax.axis_size("tile")
    column, tile_row = lax.axis_index("col"), lax.axis_index("tile")
    where = jnp.stack(
        [
            column,
            (tile_row == tiles - 1).astype(jnp.int32),
            jnp.where(column == 0, sources - 1, column - 1),
            jnp.where(column == sources - 1, 0, column + 1),
            tile_row & 1,
            column & 1,
        ]
    )
    received = lax.all_to_all(obs_misfit, "col", split_axis=2, concat_axis=1, tiled=True)
    f32 = jnp.float32
    tile = jax.ShapeDtypeStruct((LEVELS, ROWS, COLS), f32)
    lines = jax.ShapeDtypeStruct((LINES, COLS), f32)
    field = pltpu.VMEM((LEVELS, ROWS, COLS), f32)
    group = min(GROUP, sources)
    small = sources <= GROUP
    ahead = pl.CostEstimate(flops=10**10, bytes_accessed=2 * 10**8, transcendentals=0)
    scales = pl.pallas_call(
        scale_kernel,
        out_shape=jax.ShapeDtypeStruct((16 + 2 * PAD, COLS), f32),
        in_specs=[VMEM, VMEM],
        out_specs=VMEM,
        compiler_params=pltpu.CompilerParams(vmem_limit_bytes=4 * MIB),
        cost_estimate=ahead,
        name="edge_scales",
    )(side_coeff, land_mask)
    forcing = pl.pallas_call(
        functools.partial(forcing_kernel, sources),
        out_shape=jax.ShapeDtypeStruct((LEVELS * ROWS, COLS), f32),
        in_specs=[VMEM, VMEM, SMEM],
        out_specs=VMEM,
        scratch_shapes=[
            pltpu.VMEM((LEVELS * ROWS, group * CAP), jnp.bfloat16),
            pltpu.VMEM((3 * COLS, group * CAP), jnp.bfloat16),
        ],
        compiler_params=pltpu.CompilerParams(vmem_limit_bytes=(8 if small else 24) * MIB),
        cost_estimate=pl.CostEstimate(flops=10**8, bytes_accessed=4 * 10**6, transcendentals=0),
        name="forcing",
    )(received.reshape(sources, CAP), obs_cell.reshape(sources, CAP), obs_count.reshape(1, sources))
    part, swap, next_swap, edges, slots = pl.pallas_call(
        first_kernel,
        out_shape=(tile, lines, lines, jax.ShapeDtypeStruct((EDGES, COLS), f32), jax.ShapeDtypeStruct((sources, SLOT, COLS), f32)),
        in_specs=[VMEM, SMEM] + [VMEM] * 6,
        out_specs=(VMEM,) * 5,
        scratch_shapes=[
            field,
            pltpu.VMEM((LINES, COLS), f32),
            pltpu.VMEM((LINES, COLS), f32),
            pltpu.VMEM((SLOT, COLS), f32),
        ],
        compiler_params=pltpu.CompilerParams(vmem_limit_bytes=(8 if small else 24) * MIB),
        name="first_step",
    )(forcing, where, scales, adjoint_in, side_coeff, centre, vert_coeff, land_mask)
    got = lax.all_to_all(slots, "col", split_axis=0, concat_axis=0, tiled=True)
    next_swapped = lax.ppermute(next_swap, "tile", swaps(1, tiles - 1))
    swapped = lax.ppermute(swap, "tile", swaps(0, tiles))
    edge = jax.ShapeDtypeStruct((EDGE, COLS), f32)
    beside, next_beside = pl.pallas_call(
        corner_kernel,
        out_shape=(edge, edge),
        in_specs=[VMEM, VMEM, VMEM, SMEM],
        out_specs=(VMEM, VMEM),
        compiler_params=pltpu.CompilerParams(vmem_limit_bytes=4 * MIB),
        cost_estimate=pl.CostEstimate(flops=10**6, bytes_accessed=4 * 10**6, transcendentals=0),
        name="corners",
    )(swapped, next_swapped, edges, where)
    round_trip = [(sources - 1, 0), (0, sources - 1)]
    next_beside = lax.ppermute(next_beside, "col", swaps(1, sources - 1) + round_trip)
    beside = lax.ppermute(beside, "col", swaps(0, sources))
    return pl.pallas_call(
        second_kernel,
        out_shape=tile,
        in_specs=[VMEM] * 6 + [SMEM] * 3 + [VMEM] * 4,
        out_specs=VMEM,
        scratch_shapes=[
            field,
            pltpu.VMEM((4 * PAD, COLS), f32),
            pltpu.VMEM((ROWS, COLS), f32),
            pltpu.VMEM((ROWS, COLS), f32),
            pltpu.VMEM((EDGE, COLS), f32),
            pltpu.VMEM((EDGE, COLS), f32),
        ],
        compiler_params=pltpu.CompilerParams(vmem_limit_bytes=8 * MIB),
        name="second_step",
    )(
        swapped,
        next_swapped,
        beside,
        next_beside,
        edges,
        got,
        fold_partner,
        fold_flip,
        where,
        part,
        side_coeff,
        centre,
        vert_coeff,
    )


def swaps(first, end):
    return [pair for i in range(first, end - 1, 2) for pair in ((i, i + 1), (i + 1, i))]


def solution(mesh):
    in_specs = (
        P(None, "tile", "col"),
        P(None, "tile", "col"),
        P(None, None, "tile", "col"),
        P(None, None, "tile", "col"),
        P(None, "tile", "col"),
        P("tile", "col", None, None),
        P("tile", "col", None, None),
        P("tile", "col", None),
        P(),
        P(),
    )
    out_specs = P(None, "tile", "col")
    return jax.shard_map(body, mesh=mesh, in_specs=in_specs, out_specs=out_specs, check_vma=False)
```

```python
import functools

import jax
import jax.numpy as jnp
from jax import lax
from jax.experimental import pallas as pl
from jax.experimental.pallas import tpu as pltpu
from jax.sharding import PartitionSpec as P

LEVELS = 25
ROWS = 32
COLS = 128
CAP = 128
GROUP = 8
PAD = 32
LINES = 4 * PAD
CORNER = 3 * LEVELS
SLOT = 80
EDGE = 32
OFFSET = (0, 50, 1, 51)
EDGES = 48 + 2 * PAD
LAND = 1e38
MIB = 1024 * 1024
VMEM = pl.BlockSpec(memory_space=pltpu.VMEM)
SMEM = pl.BlockSpec(memory_space=pltpu.SMEM)


def iota(shape, dim):
    return lax.broadcasted_iota(jnp.int32, shape, dim)


def turn(x, shift, axis=1):
    shift = shift % x.shape[axis]
    return pltpu.roll(x, shift, axis) if shift else x


def terms(k, value, centre, side, vert):
    row, lane = iota((ROWS, COLS), 0), iota((ROWS, COLS), 1)
    y = value[k]
    east, west = side[0, k] * y, side[1, k] * y
    north, south = turn(side[2, k] * y, 1, 0), turn(side[3, k] * y, -1, 0)
    r = centre[k] * y
    r = r + jnp.where(lane > 0, turn(east, 1), 0.0) + jnp.where(lane < COLS - 1, turn(west, -1), 0.0)
    r = r + jnp.where(row > 0, north, 0.0) + jnp.where(row < ROWS - 1, south, 0.0)
    if k + 1 < LEVELS:
        r = r + vert[0, k + 1] * value[k + 1]
    if k > 0:
        r = r + vert[1, k - 1] * value[k - 1]
    return r, east, west, north, south


def outer(lane, last, first):
    return jnp.where(lane == COLS - 1, last, jnp.where(lane == 0, first, 0.0))


def scale_kernel(side, mask, scales):
    lane = iota((ROWS, COLS), 1)
    packed = jnp.zeros((ROWS, COLS), jnp.float32)
    for at in (16, 16 + PAD):
        scales[at + 24 : at + PAD, :] = jnp.zeros((8, COLS), jnp.float32)
    for k in range(LEVELS):
        m = mask[k].astype(jnp.float32)
        packed = packed + turn(m * outer(lane, side[0, k], side[1, k]), 2 * k + 1)
        scales[16 + k : 17 + k, :] = (m * side[2, k])[ROWS - 1 : ROWS]
        scales[16 + PAD + k : 17 + PAD + k, :] = (m * side[3, k])[0:1]
    scales[0:8, :], scales[8:16, :] = tight(packed)


def tight(packed):
    even = (iota((8, COLS), 1) & 1) == 0
    eastward = westward = jnp.zeros((8, COLS), jnp.float32)
    for g, offset in enumerate(OFFSET):
        rows = packed[8 * g : 8 * g + 8]
        eastward = eastward + turn(jnp.where(even, rows, 0.0), offset)
        westward = westward + turn(jnp.where(even, 0.0, rows), offset - 1)
    return eastward, westward


def forcing_kernel(sources, own_core, other_core, cell, count, where, forcing, hot, valued):
    group = min(GROUP, sources)
    lane = iota((1, CAP), 1)
    for first in range(0, sources, group):
        for s in range(group):
            at = slice(s * CAP, (s + 1) * CAP)
            cells = cell[first + s : first + s + 1, :]
            core = (first + s) & 1
            spot = pl.ds(first + s - core + where[5], 1)
            sent = jnp.where(where[5] == core, own_core[spot, :], other_core[spot, :])
            v = jnp.where(lane < count[0, first + s], sent, 0.0)
            high = v.astype(jnp.bfloat16).astype(jnp.float32)
            middle = (v - high).astype(jnp.bfloat16).astype(jnp.float32)
            low = v - high - middle
            column = iota((COLS, CAP), 0) == (cells & (COLS - 1))
            for i, part in enumerate((high, middle, low)):
                valued[i * COLS : (i + 1) * COLS, at] = jnp.where(column, part, 0.0).astype(jnp.bfloat16)
            place = cells >> 7
            for k in range(LEVELS):
                match = (iota((ROWS, CAP), 0) + k * ROWS) == place
                hot[k * ROWS : (k + 1) * ROWS, at] = jnp.where(match, 1.0, 0.0).astype(jnp.bfloat16)
        part = lax.dot_general(hot[...], valued[...], (((1,), (1,)), ((), ())), preferred_element_type=jnp.float32)
        part = part[:, 0:COLS] + part[:, COLS : 2 * COLS] + part[:, 2 * COLS : 3 * COLS]
        if first == 0:
            forcing[...] = part
        else:
            forcing[...] += part


def to_lanes(column, offset):
    level = iota((PAD, COLS), 0)
    spot = (iota((PAD, COLS), 1) == 2 * level + offset) & (level < LEVELS)
    return jnp.sum(jnp.where(spot, column, 0.0), axis=0, keepdims=True)


def to_rows(line, offset):
    level = iota((PAD, COLS), 0)
    spot = (iota((PAD, COLS), 1) == 2 * level + offset) & (level < LEVELS)
    return jnp.sum(jnp.where(spot, line, 0.0), axis=1, keepdims=True)


def spot_rows(first, last):
    row = iota((8, COLS), 0)
    return jnp.where(row == 0, first, 0.0) + jnp.where(row == 7, last, 0.0)


def ends(block):
    return block[:, COLS - 1 : COLS], block[:, 0:1]


def from_tiles(swapped, next_swapped, where, start):
    rows = slice(start, start + PAD)
    upward = where[4] == 0
    return (
        jnp.where(upward, next_swapped[rows, :], swapped[rows, :]),
        jnp.where(upward, swapped[rows, :], next_swapped[rows, :]),
    )


def first_kernel(forcing, where, scales, adjoint, side, centre, vert, mask, part, swap, next_swap, edges, slots, held, up, down, base):
    for i in range(4):
        for ref in (up, down):
            ref[i * PAD + 24 : (i + 1) * PAD, :] = jnp.zeros((8, COLS), jnp.float32)
    for k in range(LEVELS):
        held[k] = adjoint[k] + forcing[k * ROWS : (k + 1) * ROWS, :]
    lane = iota((ROWS, COLS), 1)
    packed = [jnp.zeros((ROWS, COLS), jnp.float32)] * 2
    for k in range(LEVELS):
        r, east, west, north, south = terms(k, held, centre, side, vert)
        part[k] = jnp.where(mask[k] == 0, LAND, r)
        sides = outer(lane, east, west)
        for ref, leaving, at in ((up, north[0:1], ROWS - 1), (down, south[ROWS - 1 : ROWS], 0)):
            ref[k : k + 1, :] = leaving
            ref[PAD + k : PAD + k + 1, :] = r[at : at + 1]
            ref[3 * PAD + k : 3 * PAD + k + 1, :] = sides[at : at + 1]
        packed = [p + turn(x, 2 * k + 1) for p, x in zip(packed, (sides, outer(lane, r, r)))]
    up[2 * PAD : 3 * PAD, :] = scales[16 : 16 + PAD, :]
    down[2 * PAD : 3 * PAD, :] = scales[16 + PAD : 16 + 2 * PAD, :]
    for i in range(3):
        base[i * LEVELS : (i + 1) * LEVELS, :] = up[i * PAD : i * PAD + LEVELS, :]
    own_east, own_west = ends(up[3 * PAD : 4 * PAD, :])
    base[CORNER : CORNER + 1, :] = to_lanes(own_east, OFFSET[0]) + to_lanes(own_west, OFFSET[1])
    base[CORNER + 1 : SLOT, :] = jnp.zeros((SLOT - CORNER - 1, COLS), jnp.float32)
    for s in range(slots.shape[0]):
        slots[s] = base[...]
    upward = where[4] == 0
    swap[...] = jnp.where(upward, up[...], down[...])
    next_swap[...] = jnp.where(upward, down[...], up[...])
    for i, p in enumerate(packed):
        edges[8 * i : 8 * i + 8, :], edges[24 + 8 * i : 32 + 8 * i, :] = tight(p)
    edges[16:24, :] = scales[0:8, :]
    edges[40:48, :] = scales[8:16, :]
    edges[48 : 48 + PAD, :] = down[0:PAD, :]
    edges[48 + PAD : EDGES, :] = up[0:PAD, :]


def corner_kernel(swapped, next_swapped, edges, where, swap, next_swap):
    low, high = from_tiles(swapped, next_swapped, where, 0)
    low_sides, high_sides = from_tiles(swapped, next_swapped, where, 3 * PAD)
    low_last, low_first = ends(low)
    high_last, high_first = ends(high)
    low_east, low_west = ends(low_sides)
    high_east, high_west = ends(high_sides)
    corners = (
        to_lanes(low_east, OFFSET[0]) + to_lanes(low_west, OFFSET[1]) + to_lanes(high_west, OFFSET[2]) + to_lanes(high_east, OFFSET[3])
    )
    eastward = spot_rows(to_lanes(low_last, OFFSET[0]), to_lanes(high_last, OFFSET[3]))
    westward = spot_rows(to_lanes(low_first, OFFSET[0]), to_lanes(high_first, OFFSET[3]))
    to_east = where[5] == 0
    for ref, chosen in ((swap, to_east), (next_swap, jnp.logical_not(to_east))):
        ref[0:24, :] = jnp.where(chosen, edges[0:24, :], edges[24:48, :])
        ref[8:16, :] += jnp.where(chosen, eastward, westward)
        ref[24:EDGE, :] = jnp.where(iota((EDGE - 24, COLS), 0) == 0, corners, 0.0)


def second_kernel(swapped, next_swapped, beside, next_beside, edges, got_own, got_other, partner, flip, where, part, side, centre, vert, out, held, lines, near_sides, far_sides, west_side, east_side):
    sources = 2 * got_own.shape[0]

    def got(s, rows):
        return jnp.where((s & 1) == where[5], got_own[s >> 1, rows, :], got_other[s >> 1, rows, :])

    below_near, above_near = from_tiles(swapped, next_swapped, where, 0)
    below_part, above_part = from_tiles(swapped, next_swapped, where, PAD)
    below_scale, above_scale = from_tiles(swapped, next_swapped, where, 2 * PAD)
    sum_low = below_part + edges[48 : 48 + PAD, :]
    sum_high = above_part + edges[48 + PAD : EDGES, :]
    even_column = where[5] == 0
    west_side[...] = jnp.where(even_column, next_beside[...], beside[...])
    east_side[...] = jnp.where(even_column, beside[...], next_beside[...])
    column, top, left, right = where[0], where[1], where[2], where[3]
    at_top = top == 1

    def comes_from(target):
        source = 0
        for s in range(sources):
            source = jnp.where(partner[s] == target, s, source)
        return source

    def turned(rows, source):
        back = COLS - 1 - iota((PAD, COLS), 1)
        return jnp.where(flip[source] == 1, jnp.take_along_axis(rows, back, axis=1), rows)

    level_lane = iota((PAD, COLS), 1)
    source = comes_from(column)
    earlier = comes_from(source)
    before = jnp.where(source == 0, sources - 1, source - 1)
    after = jnp.where(source == sources - 1, 0, source + 1)
    corner_left = west_side[24:25, :]
    corner_right = east_side[24:25, :]
    sum_low = sum_low + jnp.where(level_lane == 0, to_rows(corner_left, OFFSET[0]), 0.0)
    sum_low = sum_low + jnp.where(level_lane == COLS - 1, to_rows(corner_right, OFFSET[1]), 0.0)
    sum_high = sum_high + jnp.where(level_lane == 0, to_rows(corner_left, OFFSET[3]), 0.0)
    sum_high = sum_high + jnp.where(level_lane == COLS - 1, to_rows(corner_right, OFFSET[2]), 0.0)
    fold_first = turned(got(source, slice(0, PAD)), source)
    sum_fold = got(source, slice(LEVELS, LEVELS + PAD)) + turned(got(earlier, slice(0, PAD)), earlier)
    cross_west = to_rows(got(before, slice(CORNER, CORNER + 1)), OFFSET[0])
    cross_east = to_rows(got(after, slice(CORNER, CORNER + 1)), OFFSET[1])
    sum_fold = sum_fold + jnp.where(level_lane == 0, cross_west, 0.0) + jnp.where(level_lane == COLS - 1, cross_east, 0.0)
    fold_second = turned(turn(got(source, slice(SLOT - PAD, SLOT)), SLOT - PAD - 2 * LEVELS, 0) * sum_fold, source)
    lines[0:PAD, :] = jnp.where(at_top, fold_first, above_near)
    lines[PAD : 2 * PAD, :] = below_scale * sum_low
    lines[2 * PAD : 3 * PAD, :] = jnp.where(at_top, fold_second, above_scale * sum_high)
    lines[3 * PAD : 4 * PAD, :] = below_near
    from_left = comes_from(left)
    from_right = comes_from(right)
    fold_left = turned(got(from_left, slice(0, PAD)), from_left)[:, COLS - 1 : COLS]
    fold_right = turned(got(from_right, slice(0, PAD)), from_right)[:, 0:1]
    fold_left = jnp.where(at_top, to_lanes(fold_left, OFFSET[3]), 0.0)
    fold_right = jnp.where(at_top, to_lanes(fold_right, OFFSET[3]), 0.0)
    near_left = west_side[0:8, :]
    near_right = east_side[0:8, :]
    next_left = west_side[16:24, :] * (west_side[8:16, :] + edges[24:32, :] + spot_rows(0.0, fold_left))
    next_right = east_side[16:24, :] * (east_side[8:16, :] + edges[0:8, :] + spot_rows(0.0, fold_right))
    even = (iota((8, COLS), 1) & 1) == 0
    for ref, from_west, from_east in ((near_sides, near_left, near_right), (far_sides, next_left, next_right)):
        for g, offset in enumerate(OFFSET):
            ref[8 * g : 8 * g + 8, :] = jnp.where(even, turn(from_west, -offset), turn(from_east, -offset - 1))

    row, lane = iota((ROWS, COLS), 0), iota((ROWS, COLS), 1)

    def joined(k, r, sides, first, last):
        r = r + jnp.where((lane == 0) | (lane == COLS - 1), turn(sides[...], -2 * k), 0.0)
        r = r + jnp.where(row == 0, first, 0.0) + jnp.where(row == ROWS - 1, last, 0.0)
        return jnp.where(part[k] == LAND, 0.0, r)

    for k in range(LEVELS):
        held[k] = joined(k, part[k], near_sides, lines[3 * PAD + k : 3 * PAD + k + 1, :], lines[k : k + 1, :])
    for k in range(LEVELS):
        r = terms(k, held, centre, side, vert)[0]
        out[k] = joined(k, r, far_sides, lines[PAD + k : PAD + k + 1, :], lines[2 * PAD + k : 2 * PAD + k + 1, :])


def body(adjoint_in, centre, side_coeff, vert_coeff, land_mask, obs_misfit, obs_cell, obs_count, fold_partner, fold_flip):
    sources = obs_misfit.shape[2]
    tiles = lax.axis_size("tile")
    column, tile_row = lax.axis_index("col"), lax.axis_index("tile")
    where = jnp.stack(
        [
            column,
            (tile_row == tiles - 1).astype(jnp.int32),
            jnp.where(column == 0, sources - 1, column - 1),
            jnp.where(column == sources - 1, 0, column + 1),
            tile_row & 1,
            column & 1,
        ]
    )
    chips = sources // 2
    same_core = [list(range(core, sources, 2)) for core in range(2)]

    def between_chips(slots):
        return lax.all_to_all(slots, "col", split_axis=0, concat_axis=0, tiled=True, axis_index_groups=same_core)

    def between_cores(block):
        return lax.ppermute(block, "col", swaps(0, sources))

    own_core = between_chips(obs_misfit.reshape(chips, 2, CAP)).reshape(sources, CAP)
    other_core = between_cores(own_core)
    f32 = jnp.float32
    tile = jax.ShapeDtypeStruct((LEVELS, ROWS, COLS), f32)
    lines = jax.ShapeDtypeStruct((LINES, COLS), f32)
    field = pltpu.VMEM((LEVELS, ROWS, COLS), f32)
    group = min(GROUP, sources)
    small = sources <= GROUP
    ahead = pl.CostEstimate(flops=10**10, bytes_accessed=2 * 10**8, transcendentals=0)
    scales = pl.pallas_call(
        scale_kernel,
        out_shape=jax.ShapeDtypeStruct((16 + 2 * PAD, COLS), f32),
        in_specs=[VMEM, VMEM],
        out_specs=VMEM,
        compiler_params=pltpu.CompilerParams(vmem_limit_bytes=4 * MIB),
        cost_estimate=ahead,
        name="edge_scales",
    )(side_coeff, land_mask)
    forcing = pl.pallas_call(
        functools.partial(forcing_kernel, sources),
        out_shape=jax.ShapeDtypeStruct((LEVELS * ROWS, COLS), f32),
        in_specs=[VMEM, VMEM, VMEM, SMEM, SMEM],
        out_specs=VMEM,
        scratch_shapes=[
            pltpu.VMEM((LEVELS * ROWS, group * CAP), jnp.bfloat16),
            pltpu.VMEM((3 * COLS, group * CAP), jnp.bfloat16),
        ],
        compiler_params=pltpu.CompilerParams(vmem_limit_bytes=(8 if small else 24) * MIB),
        cost_estimate=pl.CostEstimate(flops=10**8, bytes_accessed=4 * 10**6, transcendentals=0),
        name="forcing",
    )(own_core, other_core, obs_cell.reshape(sources, CAP), obs_count.reshape(1, sources), where)
    part, swap, next_swap, edges, slots = pl.pallas_call(
        first_kernel,
        out_shape=(tile, lines, lines, jax.ShapeDtypeStruct((EDGES, COLS), f32), jax.ShapeDtypeStruct((chips, SLOT, COLS), f32)),
        in_specs=[VMEM, SMEM] + [VMEM] * 6,
        out_specs=(VMEM,) * 5,
        scratch_shapes=[
            field,
            pltpu.VMEM((LINES, COLS), f32),
            pltpu.VMEM((LINES, COLS), f32),
            pltpu.VMEM((SLOT, COLS), f32),
        ],
        compiler_params=pltpu.CompilerParams(vmem_limit_bytes=(8 if small else 24) * MIB),
        name="first_step",
    )(forcing, where, scales, adjoint_in, side_coeff, centre, vert_coeff, land_mask)
    got = between_chips(slots)
    next_swapped = lax.ppermute(next_swap, "tile", swaps(1, tiles - 1))
    swapped = lax.ppermute(swap, "tile", swaps(0, tiles))
    edge = jax.ShapeDtypeStruct((EDGE, COLS), f32)
    beside, next_beside = pl.pallas_call(
        corner_kernel,
        out_shape=(edge, edge),
        in_specs=[VMEM, VMEM, VMEM, SMEM],
        out_specs=(VMEM, VMEM),
        compiler_params=pltpu.CompilerParams(vmem_limit_bytes=4 * MIB),
        cost_estimate=pl.CostEstimate(flops=10**6, bytes_accessed=4 * 10**6, transcendentals=0),
        name="corners",
    )(swapped, next_swapped, edges, where)
    round_trip = [(sources - 1, 0), (0, sources - 1)]
    next_beside = lax.ppermute(next_beside, "col", swaps(1, sources - 1) + round_trip)
    got, beside = lax.optimization_barrier((got, beside))
    beside = between_cores(beside)
    got_other = between_cores(got)
    return pl.pallas_call(
        second_kernel,
        out_shape=tile,
        in_specs=[VMEM] * 7 + [SMEM] * 3 + [VMEM] * 4,
        out_specs=VMEM,
        scratch_shapes=[
            field,
            pltpu.VMEM((4 * PAD, COLS), f32),
            pltpu.VMEM((ROWS, COLS), f32),
            pltpu.VMEM((ROWS, COLS), f32),
            pltpu.VMEM((EDGE, COLS), f32),
            pltpu.VMEM((EDGE, COLS), f32),
        ],
        compiler_params=pltpu.CompilerParams(vmem_limit_bytes=8 * MIB),
        name="second_step",
    )(
        swapped,
        next_swapped,
        beside,
        next_beside,
        edges,
        got,
        got_other,
        fold_partner,
        fold_flip,
        where,
        part,
        side_coeff,
        centre,
        vert_coeff,
    )


def swaps(first, end):
    return [pair for i in range(first, end - 1, 2) for pair in ((i, i + 1), (i + 1, i))]


def solution(mesh):
    in_specs = (
        P(None, "tile", "col"),
        P(None, "tile", "col"),
        P(None, None, "tile", "col"),
        P(None, None, "tile", "col"),
        P(None, "tile", "col"),
        P("tile", "col", None, None),
        P("tile", "col", None, None),
        P("tile", "col", None),
        P(),
        P(),
    )
    out_specs = P(None, "tile", "col")
    return jax.shard_map(body, mesh=mesh, in_specs=in_specs, out_specs=out_specs, check_vma=False)
```

```python
import functools

import jax
import jax.numpy as jnp
from jax import lax
from jax.experimental import pallas as pl
from jax.experimental.pallas import tpu as pltpu
from jax.sharding import PartitionSpec as P

LEVELS = 25
ROWS = 32
COLS = 128
CAP = 128
GROUP = 8
CHUNK = 5
PAD = 32
LINES = 4 * PAD
CORNER = 3 * LEVELS
SLOT = 80
EDGE = 32
OFFSET = (0, 50, 1, 51)
EDGES = 48 + 2 * PAD
LAND = 1e38
MIB = 1024 * 1024
VMEM = pl.BlockSpec(memory_space=pltpu.VMEM)
FAR = pl.BlockSpec(memory_space=pltpu.HBM)
SMEM = pl.BlockSpec(memory_space=pltpu.SMEM)


def iota(shape, dim):
    return lax.broadcasted_iota(jnp.int32, shape, dim)


def turn(x, shift, axis=1):
    shift = shift % x.shape[axis]
    return pltpu.roll(x, shift, axis) if shift else x


def terms(k, value, centre, side, vert):
    row, lane = iota((ROWS, COLS), 0), iota((ROWS, COLS), 1)
    y = value[k]
    east, west = side[0, k] * y, side[1, k] * y
    north, south = turn(side[2, k] * y, 1, 0), turn(side[3, k] * y, -1, 0)
    r = centre[k] * y
    r = r + jnp.where(lane > 0, turn(east, 1), 0.0) + jnp.where(lane < COLS - 1, turn(west, -1), 0.0)
    r = r + jnp.where(row > 0, north, 0.0) + jnp.where(row < ROWS - 1, south, 0.0)
    if k + 1 < LEVELS:
        r = r + vert[0, k + 1] * value[k + 1]
    if k > 0:
        r = r + vert[1, k - 1] * value[k - 1]
    return r, east, west, north, south


def outer(lane, last, first):
    return jnp.where(lane == COLS - 1, last, jnp.where(lane == 0, first, 0.0))


def scale_kernel(side, mask, scales):
    lane = iota((ROWS, COLS), 1)
    packed = jnp.zeros((ROWS, COLS), jnp.float32)
    for at in (16, 16 + PAD):
        scales[at + 24 : at + PAD, :] = jnp.zeros((8, COLS), jnp.float32)
    for k in range(LEVELS):
        m = mask[k].astype(jnp.float32)
        packed = packed + turn(m * outer(lane, side[0, k], side[1, k]), 2 * k + 1)
        scales[16 + k : 17 + k, :] = (m * side[2, k])[ROWS - 1 : ROWS]
        scales[16 + PAD + k : 17 + PAD + k, :] = (m * side[3, k])[0:1]
    scales[0:8, :], scales[8:16, :] = tight(packed)


def tight(packed):
    even = (iota((8, COLS), 1) & 1) == 0
    eastward = westward = jnp.zeros((8, COLS), jnp.float32)
    for g, offset in enumerate(OFFSET):
        rows = packed[8 * g : 8 * g + 8]
        eastward = eastward + turn(jnp.where(even, rows, 0.0), offset)
        westward = westward + turn(jnp.where(even, 0.0, rows), offset - 1)
    return eastward, westward


def forcing_kernel(sources, misfit, cell, count, forcing, hot, valued):
    group = min(GROUP, sources)
    lane = iota((1, CAP), 1)
    for first in range(0, sources, group):
        for s in range(group):
            at = slice(s * CAP, (s + 1) * CAP)
            cells = cell[first + s : first + s + 1, :]
            v = jnp.where(lane < count[0, first + s], misfit[first + s : first + s + 1, :], 0.0)
            high = v.astype(jnp.bfloat16).astype(jnp.float32)
            middle = (v - high).astype(jnp.bfloat16).astype(jnp.float32)
            low = v - high - middle
            column = iota((COLS, CAP), 0) == (cells & (COLS - 1))
            for i, part in enumerate((high, middle, low)):
                valued[i * COLS : (i + 1) * COLS, at] = jnp.where(column, part, 0.0).astype(jnp.bfloat16)
            place = cells >> 7
            for k in range(LEVELS):
                match = (iota((ROWS, CAP), 0) + k * ROWS) == place
                hot[k * ROWS : (k + 1) * ROWS, at] = jnp.where(match, 1.0, 0.0).astype(jnp.bfloat16)
        part = lax.dot_general(hot[...], valued[...], (((1,), (1,)), ((), ())), preferred_element_type=jnp.float32)
        part = part[:, 0:COLS] + part[:, COLS : 2 * COLS] + part[:, 2 * COLS : 3 * COLS]
        if first == 0:
            forcing[...] = part
        else:
            forcing[...] += part


def to_lanes(column, offset):
    level = iota((PAD, COLS), 0)
    spot = (iota((PAD, COLS), 1) == 2 * level + offset) & (level < LEVELS)
    return jnp.sum(jnp.where(spot, column, 0.0), axis=0, keepdims=True)


def to_rows(line, offset):
    level = iota((PAD, COLS), 0)
    spot = (iota((PAD, COLS), 1) == 2 * level + offset) & (level < LEVELS)
    return jnp.sum(jnp.where(spot, line, 0.0), axis=1, keepdims=True)


def spot_rows(first, last):
    row = iota((8, COLS), 0)
    return jnp.where(row == 0, first, 0.0) + jnp.where(row == 7, last, 0.0)


def ends(block):
    return block[:, COLS - 1 : COLS], block[:, 0:1]


def from_tiles(swapped, next_swapped, where, start):
    rows = slice(start, start + PAD)
    upward = where[4] == 0
    return (
        jnp.where(upward, next_swapped[rows, :], swapped[rows, :]),
        jnp.where(upward, swapped[rows, :], next_swapped[rows, :]),
    )


def chunk(source, target, semaphores, i):
    levels = pl.ds(i * CHUNK, CHUNK)
    return pltpu.make_async_copy(source.at[levels], target.at[levels], semaphores.at[i])


def first_kernel(forcing, where, scales, adjoint, side, centre, vert, mask, part_far, swap, next_swap, edges, slots, held, part, up, down, base, sent):
    for i in range(4):
        for ref in (up, down):
            ref[i * PAD + 24 : (i + 1) * PAD, :] = jnp.zeros((8, COLS), jnp.float32)
    for k in range(LEVELS):
        held[k] = adjoint[k] + forcing[k * ROWS : (k + 1) * ROWS, :]
    lane = iota((ROWS, COLS), 1)
    packed = [jnp.zeros((ROWS, COLS), jnp.float32)] * 2
    for k in range(LEVELS):
        r, east, west, north, south = terms(k, held, centre, side, vert)
        part[k] = jnp.where(mask[k] == 0, LAND, r)
        sides = outer(lane, east, west)
        for ref, leaving, at in ((up, north[0:1], ROWS - 1), (down, south[ROWS - 1 : ROWS], 0)):
            ref[k : k + 1, :] = leaving
            ref[PAD + k : PAD + k + 1, :] = r[at : at + 1]
            ref[3 * PAD + k : 3 * PAD + k + 1, :] = sides[at : at + 1]
        packed = [p + turn(x, 2 * k + 1) for p, x in zip(packed, (sides, outer(lane, r, r)))]
        if (k + 1) % CHUNK == 0:
            chunk(part, part_far, sent, k // CHUNK).start()
    up[2 * PAD : 3 * PAD, :] = scales[16 : 16 + PAD, :]
    down[2 * PAD : 3 * PAD, :] = scales[16 + PAD : 16 + 2 * PAD, :]
    for i in range(3):
        base[i * LEVELS : (i + 1) * LEVELS, :] = up[i * PAD : i * PAD + LEVELS, :]
    own_east, own_west = ends(up[3 * PAD : 4 * PAD, :])
    base[CORNER : CORNER + 1, :] = to_lanes(own_east, OFFSET[0]) + to_lanes(own_west, OFFSET[1])
    base[CORNER + 1 : SLOT, :] = jnp.zeros((SLOT - CORNER - 1, COLS), jnp.float32)
    for s in range(slots.shape[0]):
        slots[s] = base[...]
    upward = where[4] == 0
    swap[...] = jnp.where(upward, up[...], down[...])
    next_swap[...] = jnp.where(upward, down[...], up[...])
    for i, p in enumerate(packed):
        edges[8 * i : 8 * i + 8, :], edges[24 + 8 * i : 32 + 8 * i, :] = tight(p)
    edges[16:24, :] = scales[0:8, :]
    edges[40:48, :] = scales[8:16, :]
    edges[48 : 48 + PAD, :] = down[0:PAD, :]
    edges[48 + PAD : EDGES, :] = up[0:PAD, :]
    for i in range(LEVELS // CHUNK):
        chunk(part, part_far, sent, i).wait()


def corner_kernel(swapped, next_swapped, edges, where, swap, next_swap):
    low, high = from_tiles(swapped, next_swapped, where, 0)
    low_sides, high_sides = from_tiles(swapped, next_swapped, where, 3 * PAD)
    low_last, low_first = ends(low)
    high_last, high_first = ends(high)
    low_east, low_west = ends(low_sides)
    high_east, high_west = ends(high_sides)
    corners = (
        to_lanes(low_east, OFFSET[0]) + to_lanes(low_west, OFFSET[1]) + to_lanes(high_west, OFFSET[2]) + to_lanes(high_east, OFFSET[3])
    )
    eastward = spot_rows(to_lanes(low_last, OFFSET[0]), to_lanes(high_last, OFFSET[3]))
    westward = spot_rows(to_lanes(low_first, OFFSET[0]), to_lanes(high_first, OFFSET[3]))
    to_east = where[5] == 0
    for ref, chosen in ((swap, to_east), (next_swap, jnp.logical_not(to_east))):
        ref[0:24, :] = jnp.where(chosen, edges[0:24, :], edges[24:48, :])
        ref[8:16, :] += jnp.where(chosen, eastward, westward)
        ref[24:EDGE, :] = jnp.where(iota((EDGE - 24, COLS), 0) == 0, corners, 0.0)


def second_kernel(swapped, next_swapped, beside, next_beside, edges, got, partner, flip, where, part_far, side, centre, vert, out, held, part, result, lines, near_sides, far_sides, west_side, east_side, loaded, sent):
    for i in range(LEVELS // CHUNK):
        chunk(part_far, part, loaded, i).start()
    sources = got.shape[0]
    below_near, above_near = from_tiles(swapped, next_swapped, where, 0)
    below_part, above_part = from_tiles(swapped, next_swapped, where, PAD)
    below_scale, above_scale = from_tiles(swapped, next_swapped, where, 2 * PAD)
    sum_low = below_part + edges[48 : 48 + PAD, :]
    sum_high = above_part + edges[48 + PAD : EDGES, :]
    even_column = where[5] == 0
    west_side[...] = jnp.where(even_column, next_beside[...], beside[...])
    east_side[...] = jnp.where(even_column, beside[...], next_beside[...])
    column, top, left, right = where[0], where[1], where[2], where[3]
    at_top = top == 1

    def comes_from(target):
        source = 0
        for s in range(sources):
            source = jnp.where(partner[s] == target, s, source)
        return source

    def turned(rows, source):
        back = COLS - 1 - iota((PAD, COLS), 1)
        return jnp.where(flip[source] == 1, jnp.take_along_axis(rows, back, axis=1), rows)

    level_lane = iota((PAD, COLS), 1)
    source = comes_from(column)
    earlier = comes_from(source)
    before = jnp.where(source == 0, sources - 1, source - 1)
    after = jnp.where(source == sources - 1, 0, source + 1)
    corner_left = west_side[24:25, :]
    corner_right = east_side[24:25, :]
    sum_low = sum_low + jnp.where(level_lane == 0, to_rows(corner_left, OFFSET[0]), 0.0)
    sum_low = sum_low + jnp.where(level_lane == COLS - 1, to_rows(corner_right, OFFSET[1]), 0.0)
    sum_high = sum_high + jnp.where(level_lane == 0, to_rows(corner_left, OFFSET[3]), 0.0)
    sum_high = sum_high + jnp.where(level_lane == COLS - 1, to_rows(corner_right, OFFSET[2]), 0.0)
    fold_first = turned(got[source, 0:PAD, :], source)
    sum_fold = got[source, LEVELS : LEVELS + PAD, :] + turned(got[earlier, 0:PAD, :], earlier)
    cross_west = to_rows(got[before, CORNER : CORNER + 1, :], OFFSET[0])
    cross_east = to_rows(got[after, CORNER : CORNER + 1, :], OFFSET[1])
    sum_fold = sum_fold + jnp.where(level_lane == 0, cross_west, 0.0) + jnp.where(level_lane == COLS - 1, cross_east, 0.0)
    fold_second = turned(turn(got[source, SLOT - PAD : SLOT, :], SLOT - PAD - 2 * LEVELS, 0) * sum_fold, source)
    lines[0:PAD, :] = jnp.where(at_top, fold_first, above_near)
    lines[PAD : 2 * PAD, :] = below_scale * sum_low
    lines[2 * PAD : 3 * PAD, :] = jnp.where(at_top, fold_second, above_scale * sum_high)
    lines[3 * PAD : 4 * PAD, :] = below_near
    from_left = comes_from(left)
    from_right = comes_from(right)
    fold_left = turned(got[from_left, 0:PAD, :], from_left)[:, COLS - 1 : COLS]
    fold_right = turned(got[from_right, 0:PAD, :], from_right)[:, 0:1]
    fold_left = jnp.where(at_top, to_lanes(fold_left, OFFSET[3]), 0.0)
    fold_right = jnp.where(at_top, to_lanes(fold_right, OFFSET[3]), 0.0)
    near_left = west_side[0:8, :]
    near_right = east_side[0:8, :]
    next_left = west_side[16:24, :] * (west_side[8:16, :] + edges[24:32, :] + spot_rows(0.0, fold_left))
    next_right = east_side[16:24, :] * (east_side[8:16, :] + edges[0:8, :] + spot_rows(0.0, fold_right))
    even = (iota((8, COLS), 1) & 1) == 0
    for ref, from_west, from_east in ((near_sides, near_left, near_right), (far_sides, next_left, next_right)):
        for g, offset in enumerate(OFFSET):
            ref[8 * g : 8 * g + 8, :] = jnp.where(even, turn(from_west, -offset), turn(from_east, -offset - 1))

    row, lane = iota((ROWS, COLS), 0), iota((ROWS, COLS), 1)

    def joined(k, r, sides, first, last):
        r = r + jnp.where((lane == 0) | (lane == COLS - 1), turn(sides[...], -2 * k), 0.0)
        r = r + jnp.where(row == 0, first, 0.0) + jnp.where(row == ROWS - 1, last, 0.0)
        return jnp.where(part[k] == LAND, 0.0, r)

    for k in range(LEVELS):
        if k % CHUNK == 0:
            chunk(part_far, part, loaded, k // CHUNK).wait()
        held[k] = joined(k, part[k], near_sides, lines[3 * PAD + k : 3 * PAD + k + 1, :], lines[k : k + 1, :])
    for k in range(LEVELS):
        r = terms(k, held, centre, side, vert)[0]
        result[k] = joined(k, r, far_sides, lines[PAD + k : PAD + k + 1, :], lines[2 * PAD + k : 2 * PAD + k + 1, :])
        if (k + 1) % CHUNK == 0:
            chunk(result, out, sent, k // CHUNK).start()
    for i in range(LEVELS // CHUNK):
        chunk(result, out, sent, i).wait()


def body(adjoint_in, centre, side_coeff, vert_coeff, land_mask, obs_misfit, obs_cell, obs_count, fold_partner, fold_flip):
    sources = obs_misfit.shape[2]
    tiles = lax.axis_size("tile")
    column, tile_row = lax.axis_index("col"), lax.axis_index("tile")
    where = jnp.stack(
        [
            column,
            (tile_row == tiles - 1).astype(jnp.int32),
            jnp.where(column == 0, sources - 1, column - 1),
            jnp.where(column == sources - 1, 0, column + 1),
            tile_row & 1,
            column & 1,
        ]
    )
    received = lax.all_to_all(obs_misfit, "col", split_axis=2, concat_axis=1, tiled=True)
    f32 = jnp.float32
    tile = jax.ShapeDtypeStruct((LEVELS, ROWS, COLS), f32)
    lines = jax.ShapeDtypeStruct((LINES, COLS), f32)
    field = pltpu.VMEM((LEVELS, ROWS, COLS), f32)
    chunks = pltpu.SemaphoreType.DMA((LEVELS // CHUNK,))
    group = min(GROUP, sources)
    small = sources <= GROUP
    ahead = pl.CostEstimate(flops=10**10, bytes_accessed=2 * 10**8, transcendentals=0)
    scales = pl.pallas_call(
        scale_kernel,
        out_shape=jax.ShapeDtypeStruct((16 + 2 * PAD, COLS), f32),
        in_specs=[VMEM, VMEM],
        out_specs=VMEM,
        compiler_params=pltpu.CompilerParams(vmem_limit_bytes=4 * MIB),
        cost_estimate=ahead,
        name="edge_scales",
    )(side_coeff, land_mask)
    forcing = pl.pallas_call(
        functools.partial(forcing_kernel, sources),
        out_shape=jax.ShapeDtypeStruct((LEVELS * ROWS, COLS), f32),
        in_specs=[VMEM, VMEM, SMEM],
        out_specs=VMEM,
        scratch_shapes=[
            pltpu.VMEM((LEVELS * ROWS, group * CAP), jnp.bfloat16),
            pltpu.VMEM((3 * COLS, group * CAP), jnp.bfloat16),
        ],
        compiler_params=pltpu.CompilerParams(vmem_limit_bytes=(8 if small else 24) * MIB),
        cost_estimate=pl.CostEstimate(flops=10**8, bytes_accessed=8 * 10**6, transcendentals=0),
        name="forcing",
    )(received.reshape(sources, CAP), obs_cell.reshape(sources, CAP), obs_count.reshape(1, sources))
    part, swap, next_swap, edges, slots = pl.pallas_call(
        first_kernel,
        out_shape=(tile, lines, lines, jax.ShapeDtypeStruct((EDGES, COLS), f32), jax.ShapeDtypeStruct((sources, SLOT, COLS), f32)),
        in_specs=[VMEM, SMEM] + [VMEM] * 6,
        out_specs=(FAR,) + (VMEM,) * 4,
        scratch_shapes=[
            field,
            field,
            pltpu.VMEM((LINES, COLS), f32),
            pltpu.VMEM((LINES, COLS), f32),
            pltpu.VMEM((SLOT, COLS), f32),
            chunks,
        ],
        compiler_params=pltpu.CompilerParams(vmem_limit_bytes=(8 if small else 24) * MIB),
        name="first_step",
    )(forcing, where, scales, adjoint_in, side_coeff, centre, vert_coeff, land_mask)
    got = lax.all_to_all(slots, "col", split_axis=0, concat_axis=0, tiled=True)
    next_swapped = lax.ppermute(next_swap, "tile", swaps(1, tiles - 1))
    swapped = lax.ppermute(swap, "tile", swaps(0, tiles))
    edge = jax.ShapeDtypeStruct((EDGE, COLS), f32)
    beside, next_beside = pl.pallas_call(
        corner_kernel,
        out_shape=(edge, edge),
        in_specs=[VMEM, VMEM, VMEM, SMEM],
        out_specs=(VMEM, VMEM),
        compiler_params=pltpu.CompilerParams(vmem_limit_bytes=4 * MIB),
        cost_estimate=pl.CostEstimate(flops=10**6, bytes_accessed=4 * 10**6, transcendentals=0),
        name="corners",
    )(swapped, next_swapped, edges, where)
    round_trip = [(sources - 1, 0), (0, sources - 1)]
    next_beside = lax.ppermute(next_beside, "col", swaps(1, sources - 1) + round_trip)
    beside = lax.ppermute(beside, "col", swaps(0, sources))
    return pl.pallas_call(
        second_kernel,
        out_shape=tile,
        in_specs=[VMEM] * 6 + [SMEM] * 3 + [FAR] + [VMEM] * 3,
        out_specs=FAR,
        input_output_aliases={9: 0},
        scratch_shapes=[
            field,
            field,
            field,
            pltpu.VMEM((4 * PAD, COLS), f32),
            pltpu.VMEM((ROWS, COLS), f32),
            pltpu.VMEM((ROWS, COLS), f32),
            pltpu.VMEM((EDGE, COLS), f32),
            pltpu.VMEM((EDGE, COLS), f32),
            chunks,
            chunks,
        ],
        compiler_params=pltpu.CompilerParams(vmem_limit_bytes=8 * MIB),
        name="second_step",
    )(
        swapped,
        next_swapped,
        beside,
        next_beside,
        edges,
        got,
        fold_partner,
        fold_flip,
        where,
        part,
        side_coeff,
        centre,
        vert_coeff,
    )


def swaps(first, end):
    return [pair for i in range(first, end - 1, 2) for pair in ((i, i + 1), (i + 1, i))]


def solution(mesh):
    in_specs = (
        P(None, "tile", "col"),
        P(None, "tile", "col"),
        P(None, None, "tile", "col"),
        P(None, None, "tile", "col"),
        P(None, "tile", "col"),
        P("tile", "col", None, None),
        P("tile", "col", None, None),
        P("tile", "col", None),
        P(),
        P(),
    )
    out_specs = P(None, "tile", "col")
    return jax.shard_map(body, mesh=mesh, in_specs=in_specs, out_specs=out_specs, check_vma=False)
```

```python
import functools

import jax
import jax.numpy as jnp
from jax import lax
from jax.experimental import pallas as pl
from jax.experimental.pallas import tpu as pltpu
from jax.sharding import PartitionSpec as P

LEVELS = 25
ROWS = 32
COLS = 128
CAP = 128
GROUP = 8
CHUNK = 5
PAD = 32
LINES = 4 * PAD
CORNER = 3 * LEVELS
SLOT = 80
EDGE = 32
OFFSET = (0, 50, 1, 51)
EDGES = 48 + 2 * PAD
LAND = 1e38
MIB = 1024 * 1024
VMEM = pl.BlockSpec(memory_space=pltpu.VMEM)
FAR = pl.BlockSpec(memory_space=pltpu.HBM)
SMEM = pl.BlockSpec(memory_space=pltpu.SMEM)


def iota(shape, dim):
    return lax.broadcasted_iota(jnp.int32, shape, dim)


def turn(x, shift, axis=1):
    shift = shift % x.shape[axis]
    return pltpu.roll(x, shift, axis) if shift else x


def terms(k, value, centre, side, vert):
    row, lane = iota((ROWS, COLS), 0), iota((ROWS, COLS), 1)
    y = value[k]
    east, west = side[0, k] * y, side[1, k] * y
    north, south = turn(side[2, k] * y, 1, 0), turn(side[3, k] * y, -1, 0)
    r = centre[k] * y
    r = r + jnp.where(lane > 0, turn(east, 1), 0.0) + jnp.where(lane < COLS - 1, turn(west, -1), 0.0)
    r = r + jnp.where(row > 0, north, 0.0) + jnp.where(row < ROWS - 1, south, 0.0)
    if k + 1 < LEVELS:
        r = r + vert[0, k + 1] * value[k + 1]
    if k > 0:
        r = r + vert[1, k - 1] * value[k - 1]
    return r, east, west, north, south


def outer(lane, last, first):
    return jnp.where(lane == COLS - 1, last, jnp.where(lane == 0, first, 0.0))


def scale_kernel(side, mask, scales):
    lane = iota((ROWS, COLS), 1)
    packed = jnp.zeros((ROWS, COLS), jnp.float32)
    for at in (16, 16 + PAD):
        scales[at + 24 : at + PAD, :] = jnp.zeros((8, COLS), jnp.float32)
    for k in range(LEVELS):
        m = mask[k].astype(jnp.float32)
        packed = packed + turn(m * outer(lane, side[0, k], side[1, k]), 2 * k + 1)
        scales[16 + k : 17 + k, :] = (m * side[2, k])[ROWS - 1 : ROWS]
        scales[16 + PAD + k : 17 + PAD + k, :] = (m * side[3, k])[0:1]
    scales[0:8, :], scales[8:16, :] = tight(packed)


def tight(packed):
    even = (iota((8, COLS), 1) & 1) == 0
    eastward = westward = jnp.zeros((8, COLS), jnp.float32)
    for g, offset in enumerate(OFFSET):
        rows = packed[8 * g : 8 * g + 8]
        eastward = eastward + turn(jnp.where(even, rows, 0.0), offset)
        westward = westward + turn(jnp.where(even, 0.0, rows), offset - 1)
    return eastward, westward


def forcing_kernel(sources, misfit, cell, count, adjoint_far, start, hot, valued, forcing, adjoint, arrived):
    load = pltpu.make_async_copy(adjoint_far, adjoint, arrived)
    load.start()
    group = min(GROUP, sources)
    lane = iota((1, CAP), 1)
    for first in range(0, sources, group):
        for s in range(group):
            at = slice(s * CAP, (s + 1) * CAP)
            cells = cell[first + s : first + s + 1, :]
            v = jnp.where(lane < count[0, first + s], misfit[first + s : first + s + 1, :], 0.0)
            high = v.astype(jnp.bfloat16).astype(jnp.float32)
            middle = (v - high).astype(jnp.bfloat16).astype(jnp.float32)
            low = v - high - middle
            column = iota((COLS, CAP), 0) == (cells & (COLS - 1))
            for i, part in enumerate((high, middle, low)):
                valued[i * COLS : (i + 1) * COLS, at] = jnp.where(column, part, 0.0).astype(jnp.bfloat16)
            place = cells >> 7
            for k in range(LEVELS):
                match = (iota((ROWS, CAP), 0) + k * ROWS) == place
                hot[k * ROWS : (k + 1) * ROWS, at] = jnp.where(match, 1.0, 0.0).astype(jnp.bfloat16)
        part = lax.dot_general(hot[...], valued[...], (((1,), (1,)), ((), ())), preferred_element_type=jnp.float32)
        part = part[:, 0:COLS] + part[:, COLS : 2 * COLS] + part[:, 2 * COLS : 3 * COLS]
        if first == 0:
            forcing[...] = part
        else:
            forcing[...] += part
    load.wait()
    for k in range(LEVELS):
        start[k] = adjoint[k] + forcing[k * ROWS : (k + 1) * ROWS, :]


def to_lanes(column, offset):
    level = iota((PAD, COLS), 0)
    spot = (iota((PAD, COLS), 1) == 2 * level + offset) & (level < LEVELS)
    return jnp.sum(jnp.where(spot, column, 0.0), axis=0, keepdims=True)


def to_rows(line, offset):
    level = iota((PAD, COLS), 0)
    spot = (iota((PAD, COLS), 1) == 2 * level + offset) & (level < LEVELS)
    return jnp.sum(jnp.where(spot, line, 0.0), axis=1, keepdims=True)


def spot_rows(first, last):
    row = iota((8, COLS), 0)
    return jnp.where(row == 0, first, 0.0) + jnp.where(row == 7, last, 0.0)


def ends(block):
    return block[:, COLS - 1 : COLS], block[:, 0:1]


def from_tiles(swapped, next_swapped, where, start):
    rows = slice(start, start + PAD)
    upward = where[4] == 0
    return (
        jnp.where(upward, next_swapped[rows, :], swapped[rows, :]),
        jnp.where(upward, swapped[rows, :], next_swapped[rows, :]),
    )


def chunk(source, target, semaphores, i):
    levels = pl.ds(i * CHUNK, CHUNK)
    return pltpu.make_async_copy(source.at[levels], target.at[levels], semaphores.at[i])


def first_kernel(held, where, scales, side, centre, vert, mask, part_far, swap, next_swap, edges, slots, part, up, down, base, sent, posted):
    for i in range(4):
        for ref in (up, down):
            ref[i * PAD + 24 : (i + 1) * PAD, :] = jnp.zeros((8, COLS), jnp.float32)
    lane = iota((ROWS, COLS), 1)
    packed = [jnp.zeros((ROWS, COLS), jnp.float32)] * 2
    for k in range(LEVELS):
        r, east, west, north, south = terms(k, held, centre, side, vert)
        part[k] = jnp.where(mask[k] == 0, LAND, r)
        sides = outer(lane, east, west)
        for ref, leaving, at in ((up, north[0:1], ROWS - 1), (down, south[ROWS - 1 : ROWS], 0)):
            ref[k : k + 1, :] = leaving
            ref[PAD + k : PAD + k + 1, :] = r[at : at + 1]
            ref[3 * PAD + k : 3 * PAD + k + 1, :] = sides[at : at + 1]
        packed = [p + turn(x, 2 * k + 1) for p, x in zip(packed, (sides, outer(lane, r, r)))]
        if (k + 1) % CHUNK == 0:
            chunk(part, part_far, sent, k // CHUNK).start()
    up[2 * PAD : 3 * PAD, :] = scales[16 : 16 + PAD, :]
    down[2 * PAD : 3 * PAD, :] = scales[16 + PAD : 16 + 2 * PAD, :]
    for i in range(3):
        base[i * LEVELS : (i + 1) * LEVELS, :] = up[i * PAD : i * PAD + LEVELS, :]
    own_east, own_west = ends(up[3 * PAD : 4 * PAD, :])
    base[CORNER : CORNER + 1, :] = to_lanes(own_east, OFFSET[0]) + to_lanes(own_west, OFFSET[1])
    base[CORNER + 1 : SLOT, :] = jnp.zeros((SLOT - CORNER - 1, COLS), jnp.float32)
    spread = [pltpu.make_async_copy(base, slots.at[s], posted.at[s]) for s in range(slots.shape[0])]
    for copy in spread:
        copy.start()
    upward = where[4] == 0
    swap[...] = jnp.where(upward, up[...], down[...])
    next_swap[...] = jnp.where(upward, down[...], up[...])
    for i, p in enumerate(packed):
        edges[8 * i : 8 * i + 8, :], edges[24 + 8 * i : 32 + 8 * i, :] = tight(p)
    edges[16:24, :] = scales[0:8, :]
    edges[40:48, :] = scales[8:16, :]
    edges[48 : 48 + PAD, :] = down[0:PAD, :]
    edges[48 + PAD : EDGES, :] = up[0:PAD, :]
    for i in range(LEVELS // CHUNK):
        chunk(part, part_far, sent, i).wait()
    for copy in spread:
        copy.wait()


def corner_kernel(swapped, next_swapped, edges, where, swap, next_swap):
    low, high = from_tiles(swapped, next_swapped, where, 0)
    low_sides, high_sides = from_tiles(swapped, next_swapped, where, 3 * PAD)
    low_last, low_first = ends(low)
    high_last, high_first = ends(high)
    low_east, low_west = ends(low_sides)
    high_east, high_west = ends(high_sides)
    corners = (
        to_lanes(low_east, OFFSET[0]) + to_lanes(low_west, OFFSET[1]) + to_lanes(high_west, OFFSET[2]) + to_lanes(high_east, OFFSET[3])
    )
    eastward = spot_rows(to_lanes(low_last, OFFSET[0]), to_lanes(high_last, OFFSET[3]))
    westward = spot_rows(to_lanes(low_first, OFFSET[0]), to_lanes(high_first, OFFSET[3]))
    to_east = where[5] == 0
    for ref, chosen in ((swap, to_east), (next_swap, jnp.logical_not(to_east))):
        ref[0:24, :] = jnp.where(chosen, edges[0:24, :], edges[24:48, :])
        ref[8:16, :] += jnp.where(chosen, eastward, westward)
        ref[24:EDGE, :] = jnp.where(iota((EDGE - 24, COLS), 0) == 0, corners, 0.0)


def second_kernel(swapped, next_swapped, beside, next_beside, edges, got, partner, flip, where, part_far, side, centre, vert, out, held, part, result, lines, near_sides, far_sides, west_side, east_side, loaded, sent):
    for i in range(LEVELS // CHUNK):
        chunk(part_far, part, loaded, i).start()
    sources = got.shape[0]
    below_near, above_near = from_tiles(swapped, next_swapped, where, 0)
    below_part, above_part = from_tiles(swapped, next_swapped, where, PAD)
    below_scale, above_scale = from_tiles(swapped, next_swapped, where, 2 * PAD)
    sum_low = below_part + edges[48 : 48 + PAD, :]
    sum_high = above_part + edges[48 + PAD : EDGES, :]
    even_column = where[5] == 0
    west_side[...] = jnp.where(even_column, next_beside[...], beside[...])
    east_side[...] = jnp.where(even_column, beside[...], next_beside[...])
    column, top, left, right = where[0], where[1], where[2], where[3]
    at_top = top == 1

    def comes_from(target):
        source = 0
        for s in range(sources):
            source = jnp.where(partner[s] == target, s, source)
        return source

    def turned(rows, source):
        back = COLS - 1 - iota((PAD, COLS), 1)
        return jnp.where(flip[source] == 1, jnp.take_along_axis(rows, back, axis=1), rows)

    level_lane = iota((PAD, COLS), 1)
    source = comes_from(column)
    earlier = comes_from(source)
    before = jnp.where(source == 0, sources - 1, source - 1)
    after = jnp.where(source == sources - 1, 0, source + 1)
    corner_left = west_side[24:25, :]
    corner_right = east_side[24:25, :]
    sum_low = sum_low + jnp.where(level_lane == 0, to_rows(corner_left, OFFSET[0]), 0.0)
    sum_low = sum_low + jnp.where(level_lane == COLS - 1, to_rows(corner_right, OFFSET[1]), 0.0)
    sum_high = sum_high + jnp.where(level_lane == 0, to_rows(corner_left, OFFSET[3]), 0.0)
    sum_high = sum_high + jnp.where(level_lane == COLS - 1, to_rows(corner_right, OFFSET[2]), 0.0)
    fold_first = turned(got[source, 0:PAD, :], source)
    sum_fold = got[source, LEVELS : LEVELS + PAD, :] + turned(got[earlier, 0:PAD, :], earlier)
    cross_west = to_rows(got[before, CORNER : CORNER + 1, :], OFFSET[0])
    cross_east = to_rows(got[after, CORNER : CORNER + 1, :], OFFSET[1])
    sum_fold = sum_fold + jnp.where(level_lane == 0, cross_west, 0.0) + jnp.where(level_lane == COLS - 1, cross_east, 0.0)
    fold_second = turned(turn(got[source, SLOT - PAD : SLOT, :], SLOT - PAD - 2 * LEVELS, 0) * sum_fold, source)
    lines[0:PAD, :] = jnp.where(at_top, fold_first, above_near)
    lines[PAD : 2 * PAD, :] = below_scale * sum_low
    lines[2 * PAD : 3 * PAD, :] = jnp.where(at_top, fold_second, above_scale * sum_high)
    lines[3 * PAD : 4 * PAD, :] = below_near
    from_left = comes_from(left)
    from_right = comes_from(right)
    fold_left = turned(got[from_left, 0:PAD, :], from_left)[:, COLS - 1 : COLS]
    fold_right = turned(got[from_right, 0:PAD, :], from_right)[:, 0:1]
    fold_left = jnp.where(at_top, to_lanes(fold_left, OFFSET[3]), 0.0)
    fold_right = jnp.where(at_top, to_lanes(fold_right, OFFSET[3]), 0.0)
    near_left = west_side[0:8, :]
    near_right = east_side[0:8, :]
    next_left = west_side[16:24, :] * (west_side[8:16, :] + edges[24:32, :] + spot_rows(0.0, fold_left))
    next_right = east_side[16:24, :] * (east_side[8:16, :] + edges[0:8, :] + spot_rows(0.0, fold_right))
    even = (iota((8, COLS), 1) & 1) == 0
    for ref, from_west, from_east in ((near_sides, near_left, near_right), (far_sides, next_left, next_right)):
        for g, offset in enumerate(OFFSET):
            ref[8 * g : 8 * g + 8, :] = jnp.where(even, turn(from_west, -offset), turn(from_east, -offset - 1))

    row, lane = iota((ROWS, COLS), 0), iota((ROWS, COLS), 1)

    def joined(k, r, sides, first, last):
        r = r + jnp.where((lane == 0) | (lane == COLS - 1), turn(sides[...], -2 * k), 0.0)
        r = r + jnp.where(row == 0, first, 0.0) + jnp.where(row == ROWS - 1, last, 0.0)
        return jnp.where(part[k] == LAND, 0.0, r)

    for k in range(LEVELS):
        if k % CHUNK == 0:
            chunk(part_far, part, loaded, k // CHUNK).wait()
        held[k] = joined(k, part[k], near_sides, lines[3 * PAD + k : 3 * PAD + k + 1, :], lines[k : k + 1, :])
    for k in range(LEVELS):
        r = terms(k, held, centre, side, vert)[0]
        result[k] = joined(k, r, far_sides, lines[PAD + k : PAD + k + 1, :], lines[2 * PAD + k : 2 * PAD + k + 1, :])
        if (k + 1) % CHUNK == 0:
            chunk(result, out, sent, k // CHUNK).start()
    for i in range(LEVELS // CHUNK):
        chunk(result, out, sent, i).wait()


def body(adjoint_in, centre, side_coeff, vert_coeff, land_mask, obs_misfit, obs_cell, obs_count, fold_partner, fold_flip):
    sources = obs_misfit.shape[2]
    tiles = lax.axis_size("tile")
    column, tile_row = lax.axis_index("col"), lax.axis_index("tile")
    where = jnp.stack(
        [
            column,
            (tile_row == tiles - 1).astype(jnp.int32),
            jnp.where(column == 0, sources - 1, column - 1),
            jnp.where(column == sources - 1, 0, column + 1),
            tile_row & 1,
            column & 1,
        ]
    )
    received = lax.all_to_all(obs_misfit, "col", split_axis=2, concat_axis=1, tiled=True)
    f32 = jnp.float32
    tile = jax.ShapeDtypeStruct((LEVELS, ROWS, COLS), f32)
    lines = jax.ShapeDtypeStruct((LINES, COLS), f32)
    field = pltpu.VMEM((LEVELS, ROWS, COLS), f32)
    chunks = pltpu.SemaphoreType.DMA((LEVELS // CHUNK,))
    group = min(GROUP, sources)
    small = sources <= GROUP
    ahead = pl.CostEstimate(flops=10**10, bytes_accessed=2 * 10**8, transcendentals=0)
    scales = pl.pallas_call(
        scale_kernel,
        out_shape=jax.ShapeDtypeStruct((16 + 2 * PAD, COLS), f32),
        in_specs=[VMEM, VMEM],
        out_specs=VMEM,
        compiler_params=pltpu.CompilerParams(vmem_limit_bytes=4 * MIB),
        cost_estimate=ahead,
        name="edge_scales",
    )(side_coeff, land_mask)
    start = pl.pallas_call(
        functools.partial(forcing_kernel, sources),
        out_shape=tile,
        in_specs=[VMEM, VMEM, SMEM, FAR],
        out_specs=VMEM,
        scratch_shapes=[
            pltpu.VMEM((LEVELS * ROWS, group * CAP), jnp.bfloat16),
            pltpu.VMEM((3 * COLS, group * CAP), jnp.bfloat16),
            pltpu.VMEM((LEVELS * ROWS, COLS), f32),
            field,
            pltpu.SemaphoreType.DMA,
        ],
        compiler_params=pltpu.CompilerParams(vmem_limit_bytes=(8 if small else 24) * MIB),
        cost_estimate=pl.CostEstimate(flops=10**8, bytes_accessed=8 * 10**6, transcendentals=0),
        name="forcing",
    )(received.reshape(sources, CAP), obs_cell.reshape(sources, CAP), obs_count.reshape(1, sources), pltpu.with_memory_space_constraint(adjoint_in, pltpu.HBM))
    part, swap, next_swap, edges, slots = pl.pallas_call(
        first_kernel,
        out_shape=(tile, lines, lines, jax.ShapeDtypeStruct((EDGES, COLS), f32), pltpu.HBM((sources, SLOT, COLS), f32)),
        in_specs=[VMEM, SMEM] + [VMEM] * 5,
        out_specs=(FAR,) + (VMEM,) * 3 + (FAR,),
        scratch_shapes=[
            field,
            pltpu.VMEM((LINES, COLS), f32),
            pltpu.VMEM((LINES, COLS), f32),
            pltpu.VMEM((SLOT, COLS), f32),
            chunks,
            pltpu.SemaphoreType.DMA((sources,)),
        ],
        compiler_params=pltpu.CompilerParams(vmem_limit_bytes=(8 if small else 24) * MIB),
        name="first_step",
    )(start, where, scales, side_coeff, centre, vert_coeff, land_mask)
    got = lax.all_to_all(slots, "col", split_axis=0, concat_axis=0, tiled=True)
    next_swapped = lax.ppermute(next_swap, "tile", swaps(1, tiles - 1))
    swapped = lax.ppermute(swap, "tile", swaps(0, tiles))
    edge = jax.ShapeDtypeStruct((EDGE, COLS), f32)
    beside, next_beside = pl.pallas_call(
        corner_kernel,
        out_shape=(edge, edge),
        in_specs=[VMEM, VMEM, VMEM, SMEM],
        out_specs=(VMEM, VMEM),
        compiler_params=pltpu.CompilerParams(vmem_limit_bytes=4 * MIB),
        cost_estimate=pl.CostEstimate(flops=10**6, bytes_accessed=4 * 10**6, transcendentals=0),
        name="corners",
    )(swapped, next_swapped, edges, where)
    round_trip = [(sources - 1, 0), (0, sources - 1)]
    next_beside = lax.ppermute(next_beside, "col", swaps(1, sources - 1) + round_trip)
    beside = lax.ppermute(beside, "col", swaps(0, sources))
    return pl.pallas_call(
        second_kernel,
        out_shape=tile,
        in_specs=[VMEM] * 6 + [SMEM] * 3 + [FAR] + [VMEM] * 3,
        out_specs=FAR,
        input_output_aliases={9: 0},
        scratch_shapes=[
            field,
            field,
            field,
            pltpu.VMEM((4 * PAD, COLS), f32),
            pltpu.VMEM((ROWS, COLS), f32),
            pltpu.VMEM((ROWS, COLS), f32),
            pltpu.VMEM((EDGE, COLS), f32),
            pltpu.VMEM((EDGE, COLS), f32),
            chunks,
            chunks,
        ],
        compiler_params=pltpu.CompilerParams(vmem_limit_bytes=8 * MIB),
        name="second_step",
    )(
        swapped,
        next_swapped,
        beside,
        next_beside,
        edges,
        got,
        fold_partner,
        fold_flip,
        where,
        part,
        side_coeff,
        centre,
        vert_coeff,
    )


def swaps(first, end):
    return [pair for i in range(first, end - 1, 2) for pair in ((i, i + 1), (i + 1, i))]


def solution(mesh):
    in_specs = (
        P(None, "tile", "col"),
        P(None, "tile", "col"),
        P(None, None, "tile", "col"),
        P(None, None, "tile", "col"),
        P(None, "tile", "col"),
        P("tile", "col", None, None),
        P("tile", "col", None, None),
        P("tile", "col", None),
        P(),
        P(),
    )
    out_specs = P(None, "tile", "col")
    return jax.shard_map(body, mesh=mesh, in_specs=in_specs, out_specs=out_specs, check_vma=False)
```

```python
import functools

import jax
import jax.numpy as jnp
from jax import lax
from jax.experimental import pallas as pl
from jax.experimental.pallas import tpu as pltpu
from jax.sharding import PartitionSpec as P

LEVELS = 25
ROWS = 32
COLS = 128
CAP = 128
GROUP = 8
CHUNK = 5
PAD = 32
LINES = 4 * PAD
CORNER = 3 * LEVELS
SLOT = 80
EDGE = 32
OFFSET = (0, 50, 1, 51)
EDGES = 48 + 2 * PAD
LAND = 1e38
MIB = 1024 * 1024
VMEM = pl.BlockSpec(memory_space=pltpu.VMEM)
FAR = pl.BlockSpec(memory_space=pltpu.HBM)
SMEM = pl.BlockSpec(memory_space=pltpu.SMEM)


def iota(shape, dim):
    return lax.broadcasted_iota(jnp.int32, shape, dim)


def turn(x, shift, axis=1):
    shift = shift % x.shape[axis]
    return pltpu.roll(x, shift, axis) if shift else x


def terms(k, value, centre, side, vert):
    row, lane = iota((ROWS, COLS), 0), iota((ROWS, COLS), 1)
    y = value[k]
    east, west = side[0, k] * y, side[1, k] * y
    north, south = turn(side[2, k] * y, 1, 0), turn(side[3, k] * y, -1, 0)
    r = centre[k] * y
    r = r + jnp.where(lane > 0, turn(east, 1), 0.0) + jnp.where(lane < COLS - 1, turn(west, -1), 0.0)
    r = r + jnp.where(row > 0, north, 0.0) + jnp.where(row < ROWS - 1, south, 0.0)
    if k + 1 < LEVELS:
        r = r + vert[0, k + 1] * value[k + 1]
    if k > 0:
        r = r + vert[1, k - 1] * value[k - 1]
    return r, east, west, north, south


def outer(lane, last, first):
    return jnp.where(lane == COLS - 1, last, jnp.where(lane == 0, first, 0.0))


def scale_kernel(side, mask, scales):
    lane = iota((ROWS, COLS), 1)
    packed = jnp.zeros((ROWS, COLS), jnp.float32)
    for at in (16, 16 + PAD):
        scales[at + 24 : at + PAD, :] = jnp.zeros((8, COLS), jnp.float32)
    for k in range(LEVELS):
        m = mask[k].astype(jnp.float32)
        packed = packed + turn(m * outer(lane, side[0, k], side[1, k]), 2 * k + 1)
        scales[16 + k : 17 + k, :] = (m * side[2, k])[ROWS - 1 : ROWS]
        scales[16 + PAD + k : 17 + PAD + k, :] = (m * side[3, k])[0:1]
    scales[0:8, :], scales[8:16, :] = tight(packed)


def tight(packed):
    even = (iota((8, COLS), 1) & 1) == 0
    eastward = westward = jnp.zeros((8, COLS), jnp.float32)
    for g, offset in enumerate(OFFSET):
        rows = packed[8 * g : 8 * g + 8]
        eastward = eastward + turn(jnp.where(even, rows, 0.0), offset)
        westward = westward + turn(jnp.where(even, 0.0, rows), offset - 1)
    return eastward, westward


def forcing_kernel(sources, misfit, cell, count, adjoint_far, start, hot, valued, adjoint, arrived):
    load = pltpu.make_async_copy(adjoint_far, adjoint, arrived)
    load.start()
    group = min(GROUP, sources)
    lane = iota((1, CAP), 1)
    for first in range(0, sources, group):
        for s in range(group):
            at = slice(s * CAP, (s + 1) * CAP)
            cells = cell[first + s : first + s + 1, :]
            v = jnp.where(lane < count[0, first + s], misfit[first + s : first + s + 1, :], 0.0)
            high = v.astype(jnp.bfloat16).astype(jnp.float32)
            middle = (v - high).astype(jnp.bfloat16).astype(jnp.float32)
            low = v - high - middle
            column = iota((COLS, CAP), 0) == (cells & (COLS - 1))
            for i, part in enumerate((high, middle, low)):
                valued[i * COLS : (i + 1) * COLS, at] = jnp.where(column, part, 0.0).astype(jnp.bfloat16)
            place = cells >> 7
            for k in range(LEVELS):
                match = (iota((ROWS, CAP), 0) + k * ROWS) == place
                hot[k * ROWS : (k + 1) * ROWS, at] = jnp.where(match, 1.0, 0.0).astype(jnp.bfloat16)
        part = lax.dot_general(hot[...], valued[...], (((1,), (1,)), ((), ())), preferred_element_type=jnp.float32)
        part = part[:, 0:COLS] + part[:, COLS : 2 * COLS] + part[:, 2 * COLS : 3 * COLS]
        if first == 0:
            load.wait()
        held = adjoint if first == 0 else start
        for k in range(LEVELS):
            start[k] = held[k] + part[k * ROWS : (k + 1) * ROWS, :]


def to_lanes(column, offset):
    level = iota((PAD, COLS), 0)
    spot = (iota((PAD, COLS), 1) == 2 * level + offset) & (level < LEVELS)
    return jnp.sum(jnp.where(spot, column, 0.0), axis=0, keepdims=True)


def to_rows(line, offset):
    level = iota((PAD, COLS), 0)
    spot = (iota((PAD, COLS), 1) == 2 * level + offset) & (level < LEVELS)
    return jnp.sum(jnp.where(spot, line, 0.0), axis=1, keepdims=True)


def spot_rows(first, last):
    row = iota((8, COLS), 0)
    return jnp.where(row == 0, first, 0.0) + jnp.where(row == 7, last, 0.0)


def ends(block):
    return block[:, COLS - 1 : COLS], block[:, 0:1]


def from_tiles(swapped, next_swapped, where, start):
    rows = slice(start, start + PAD)
    upward = where[4] == 0
    return (
        jnp.where(upward, next_swapped[rows, :], swapped[rows, :]),
        jnp.where(upward, swapped[rows, :], next_swapped[rows, :]),
    )


def chunk(source, target, semaphores, i):
    levels = pl.ds(i * CHUNK, CHUNK)
    return pltpu.make_async_copy(source.at[levels], target.at[levels], semaphores.at[i])


def first_kernel(held, where, scales, side, centre, vert, mask, part_far, swap, next_swap, edges, slots, part, up, down, base, picked, next_picked, sent, posted):
    for i in range(4):
        for ref in (up, down):
            ref[i * PAD + 24 : (i + 1) * PAD, :] = jnp.zeros((8, COLS), jnp.float32)
    lane = iota((ROWS, COLS), 1)
    packed = [jnp.zeros((ROWS, COLS), jnp.float32)] * 2
    for k in range(LEVELS):
        r, east, west, north, south = terms(k, held, centre, side, vert)
        part[k] = jnp.where(mask[k] == 0, LAND, r)
        sides = outer(lane, east, west)
        for ref, leaving, at in ((up, north[0:1], ROWS - 1), (down, south[ROWS - 1 : ROWS], 0)):
            ref[k : k + 1, :] = leaving
            ref[PAD + k : PAD + k + 1, :] = r[at : at + 1]
            ref[3 * PAD + k : 3 * PAD + k + 1, :] = sides[at : at + 1]
        packed = [p + turn(x, 2 * k + 1) for p, x in zip(packed, (sides, outer(lane, r, r)))]
        if (k + 1) % CHUNK == 0:
            chunk(part, part_far, sent, k // CHUNK).start()
    up[2 * PAD : 3 * PAD, :] = scales[16 : 16 + PAD, :]
    down[2 * PAD : 3 * PAD, :] = scales[16 + PAD : 16 + 2 * PAD, :]
    for i in range(3):
        base[i * LEVELS : (i + 1) * LEVELS, :] = up[i * PAD : i * PAD + LEVELS, :]
    own_east, own_west = ends(up[3 * PAD : 4 * PAD, :])
    base[CORNER : CORNER + 1, :] = to_lanes(own_east, OFFSET[0]) + to_lanes(own_west, OFFSET[1])
    base[CORNER + 1 : SLOT, :] = jnp.zeros((SLOT - CORNER - 1, COLS), jnp.float32)
    spread = [pltpu.make_async_copy(base, slots.at[s], posted.at[s]) for s in range(slots.shape[0])]
    for copy in spread:
        copy.start()
    upward = where[4] == 0
    picked[...] = jnp.where(upward, up[...], down[...])
    next_picked[...] = jnp.where(upward, down[...], up[...])
    spread.append(pltpu.make_async_copy(picked, swap, posted.at[slots.shape[0]]))
    spread.append(pltpu.make_async_copy(next_picked, next_swap, posted.at[slots.shape[0] + 1]))
    for copy in spread[-2:]:
        copy.start()
    for i, p in enumerate(packed):
        edges[8 * i : 8 * i + 8, :], edges[24 + 8 * i : 32 + 8 * i, :] = tight(p)
    edges[16:24, :] = scales[0:8, :]
    edges[40:48, :] = scales[8:16, :]
    edges[48 : 48 + PAD, :] = down[0:PAD, :]
    edges[48 + PAD : EDGES, :] = up[0:PAD, :]
    for i in range(LEVELS // CHUNK):
        chunk(part, part_far, sent, i).wait()
    for copy in spread:
        copy.wait()


def corner_kernel(swapped, next_swapped, edges, where, swap, next_swap):
    low, high = from_tiles(swapped, next_swapped, where, 0)
    low_sides, high_sides = from_tiles(swapped, next_swapped, where, 3 * PAD)
    low_last, low_first = ends(low)
    high_last, high_first = ends(high)
    low_east, low_west = ends(low_sides)
    high_east, high_west = ends(high_sides)
    corners = (
        to_lanes(low_east, OFFSET[0]) + to_lanes(low_west, OFFSET[1]) + to_lanes(high_west, OFFSET[2]) + to_lanes(high_east, OFFSET[3])
    )
    eastward = spot_rows(to_lanes(low_last, OFFSET[0]), to_lanes(high_last, OFFSET[3]))
    westward = spot_rows(to_lanes(low_first, OFFSET[0]), to_lanes(high_first, OFFSET[3]))
    to_east = where[5] == 0
    for ref, chosen in ((swap, to_east), (next_swap, jnp.logical_not(to_east))):
        ref[0:24, :] = jnp.where(chosen, edges[0:24, :], edges[24:48, :])
        ref[8:16, :] += jnp.where(chosen, eastward, westward)
        ref[24:EDGE, :] = jnp.where(iota((EDGE - 24, COLS), 0) == 0, corners, 0.0)


def second_kernel(swapped, next_swapped, beside, next_beside, edges, got_far, partner, flip, where, part_far, side, centre, vert, out, held, part, result, lines, near_sides, far_sides, west_side, east_side, got, loaded, sent, gathered):
    gather = pltpu.make_async_copy(got_far, got, gathered)
    gather.start()
    for i in range(LEVELS // CHUNK):
        chunk(part_far, part, loaded, i).start()
    sources = got.shape[0]
    below_near, above_near = from_tiles(swapped, next_swapped, where, 0)
    below_part, above_part = from_tiles(swapped, next_swapped, where, PAD)
    below_scale, above_scale = from_tiles(swapped, next_swapped, where, 2 * PAD)
    sum_low = below_part + edges[48 : 48 + PAD, :]
    sum_high = above_part + edges[48 + PAD : EDGES, :]
    even_column = where[5] == 0
    west_side[...] = jnp.where(even_column, next_beside[...], beside[...])
    east_side[...] = jnp.where(even_column, beside[...], next_beside[...])
    column, top, left, right = where[0], where[1], where[2], where[3]
    at_top = top == 1

    def comes_from(target):
        source = 0
        for s in range(sources):
            source = jnp.where(partner[s] == target, s, source)
        return source

    def turned(rows, source):
        back = COLS - 1 - iota((PAD, COLS), 1)
        return jnp.where(flip[source] == 1, jnp.take_along_axis(rows, back, axis=1), rows)

    level_lane = iota((PAD, COLS), 1)
    gather.wait()
    source = comes_from(column)
    earlier = comes_from(source)
    before = jnp.where(source == 0, sources - 1, source - 1)
    after = jnp.where(source == sources - 1, 0, source + 1)
    corner_left = west_side[24:25, :]
    corner_right = east_side[24:25, :]
    sum_low = sum_low + jnp.where(level_lane == 0, to_rows(corner_left, OFFSET[0]), 0.0)
    sum_low = sum_low + jnp.where(level_lane == COLS - 1, to_rows(corner_right, OFFSET[1]), 0.0)
    sum_high = sum_high + jnp.where(level_lane == 0, to_rows(corner_left, OFFSET[3]), 0.0)
    sum_high = sum_high + jnp.where(level_lane == COLS - 1, to_rows(corner_right, OFFSET[2]), 0.0)
    fold_first = turned(got[source, 0:PAD, :], source)
    sum_fold = got[source, LEVELS : LEVELS + PAD, :] + turned(got[earlier, 0:PAD, :], earlier)
    cross_west = to_rows(got[before, CORNER : CORNER + 1, :], OFFSET[0])
    cross_east = to_rows(got[after, CORNER : CORNER + 1, :], OFFSET[1])
    sum_fold = sum_fold + jnp.where(level_lane == 0, cross_west, 0.0) + jnp.where(level_lane == COLS - 1, cross_east, 0.0)
    fold_second = turned(turn(got[source, SLOT - PAD : SLOT, :], SLOT - PAD - 2 * LEVELS, 0) * sum_fold, source)
    lines[0:PAD, :] = jnp.where(at_top, fold_first, above_near)
    lines[PAD : 2 * PAD, :] = below_scale * sum_low
    lines[2 * PAD : 3 * PAD, :] = jnp.where(at_top, fold_second, above_scale * sum_high)
    lines[3 * PAD : 4 * PAD, :] = below_near
    from_left = comes_from(left)
    from_right = comes_from(right)
    fold_left = turned(got[from_left, 0:PAD, :], from_left)[:, COLS - 1 : COLS]
    fold_right = turned(got[from_right, 0:PAD, :], from_right)[:, 0:1]
    fold_left = jnp.where(at_top, to_lanes(fold_left, OFFSET[3]), 0.0)
    fold_right = jnp.where(at_top, to_lanes(fold_right, OFFSET[3]), 0.0)
    near_left = west_side[0:8, :]
    near_right = east_side[0:8, :]
    next_left = west_side[16:24, :] * (west_side[8:16, :] + edges[24:32, :] + spot_rows(0.0, fold_left))
    next_right = east_side[16:24, :] * (east_side[8:16, :] + edges[0:8, :] + spot_rows(0.0, fold_right))
    even = (iota((8, COLS), 1) & 1) == 0
    for ref, from_west, from_east in ((near_sides, near_left, near_right), (far_sides, next_left, next_right)):
        for g, offset in enumerate(OFFSET):
            ref[8 * g : 8 * g + 8, :] = jnp.where(even, turn(from_west, -offset), turn(from_east, -offset - 1))

    row, lane = iota((ROWS, COLS), 0), iota((ROWS, COLS), 1)

    def joined(k, r, sides, first, last):
        r = r + jnp.where((lane == 0) | (lane == COLS - 1), turn(sides[...], -2 * k), 0.0)
        r = r + jnp.where(row == 0, first, 0.0) + jnp.where(row == ROWS - 1, last, 0.0)
        return jnp.where(part[k] == LAND, 0.0, r)

    for k in range(LEVELS):
        if k % CHUNK == 0:
            chunk(part_far, part, loaded, k // CHUNK).wait()
        held[k] = joined(k, part[k], near_sides, lines[3 * PAD + k : 3 * PAD + k + 1, :], lines[k : k + 1, :])
    for k in range(LEVELS):
        r = terms(k, held, centre, side, vert)[0]
        result[k] = joined(k, r, far_sides, lines[PAD + k : PAD + k + 1, :], lines[2 * PAD + k : 2 * PAD + k + 1, :])
        if (k + 1) % CHUNK == 0:
            chunk(result, out, sent, k // CHUNK).start()
    for i in range(LEVELS // CHUNK):
        chunk(result, out, sent, i).wait()


def body(adjoint_in, centre, side_coeff, vert_coeff, land_mask, obs_misfit, obs_cell, obs_count, fold_partner, fold_flip):
    sources = obs_misfit.shape[2]
    tiles = lax.axis_size("tile")
    column, tile_row = lax.axis_index("col"), lax.axis_index("tile")
    where = jnp.stack(
        [
            column,
            (tile_row == tiles - 1).astype(jnp.int32),
            jnp.where(column == 0, sources - 1, column - 1),
            jnp.where(column == sources - 1, 0, column + 1),
            tile_row & 1,
            column & 1,
        ]
    )
    received = lax.all_to_all(obs_misfit, "col", split_axis=2, concat_axis=1, tiled=True)
    f32 = jnp.float32
    tile = jax.ShapeDtypeStruct((LEVELS, ROWS, COLS), f32)
    lines = pltpu.HBM((LINES, COLS), f32)
    field = pltpu.VMEM((LEVELS, ROWS, COLS), f32)
    chunks = pltpu.SemaphoreType.DMA((LEVELS // CHUNK,))
    group = min(GROUP, sources)
    small = sources <= GROUP
    ahead = pl.CostEstimate(flops=10**10, bytes_accessed=2 * 10**8, transcendentals=0)
    scales = pl.pallas_call(
        scale_kernel,
        out_shape=jax.ShapeDtypeStruct((16 + 2 * PAD, COLS), f32),
        in_specs=[VMEM, VMEM],
        out_specs=VMEM,
        compiler_params=pltpu.CompilerParams(vmem_limit_bytes=4 * MIB),
        cost_estimate=ahead,
        name="edge_scales",
    )(side_coeff, land_mask)
    start = pl.pallas_call(
        functools.partial(forcing_kernel, sources),
        out_shape=tile,
        in_specs=[VMEM, VMEM, SMEM, FAR],
        out_specs=VMEM,
        scratch_shapes=[
            pltpu.VMEM((LEVELS * ROWS, group * CAP), jnp.bfloat16),
            pltpu.VMEM((3 * COLS, group * CAP), jnp.bfloat16),
            field,
            pltpu.SemaphoreType.DMA,
        ],
        compiler_params=pltpu.CompilerParams(vmem_limit_bytes=(8 if small else 24) * MIB),
        cost_estimate=pl.CostEstimate(flops=10**8, bytes_accessed=8 * 10**6, transcendentals=0),
        name="forcing",
    )(received.reshape(sources, CAP), obs_cell.reshape(sources, CAP), obs_count.reshape(1, sources), pltpu.with_memory_space_constraint(adjoint_in, pltpu.HBM))
    part, swap, next_swap, edges, slots = pl.pallas_call(
        first_kernel,
        out_shape=(tile, lines, lines, jax.ShapeDtypeStruct((EDGES, COLS), f32), pltpu.HBM((sources, SLOT, COLS), f32)),
        in_specs=[VMEM, SMEM] + [VMEM] * 5,
        out_specs=(FAR, FAR, FAR, VMEM, FAR),
        scratch_shapes=[
            field,
            pltpu.VMEM((LINES, COLS), f32),
            pltpu.VMEM((LINES, COLS), f32),
            pltpu.VMEM((SLOT, COLS), f32),
            pltpu.VMEM((LINES, COLS), f32),
            pltpu.VMEM((LINES, COLS), f32),
            chunks,
            pltpu.SemaphoreType.DMA((sources + 2,)),
        ],
        compiler_params=pltpu.CompilerParams(vmem_limit_bytes=(8 if small else 24) * MIB),
        name="first_step",
    )(start, where, scales, side_coeff, centre, vert_coeff, land_mask)
    got = lax.all_to_all(slots, "col", split_axis=0, concat_axis=0, tiled=True)
    next_swapped = lax.ppermute(next_swap, "tile", swaps(1, tiles - 1))
    swapped = lax.ppermute(swap, "tile", swaps(0, tiles))
    edge = jax.ShapeDtypeStruct((EDGE, COLS), f32)
    beside, next_beside = pl.pallas_call(
        corner_kernel,
        out_shape=(edge, edge),
        in_specs=[VMEM, VMEM, VMEM, SMEM],
        out_specs=(VMEM, VMEM),
        compiler_params=pltpu.CompilerParams(vmem_limit_bytes=4 * MIB),
        cost_estimate=pl.CostEstimate(flops=10**6, bytes_accessed=4 * 10**6, transcendentals=0),
        name="corners",
    )(swapped, next_swapped, edges, where)
    round_trip = [(sources - 1, 0), (0, sources - 1)]
    next_beside = lax.ppermute(next_beside, "col", swaps(1, sources - 1) + round_trip)
    beside = lax.ppermute(beside, "col", swaps(0, sources))
    return pl.pallas_call(
        second_kernel,
        out_shape=tile,
        in_specs=[VMEM] * 5 + [FAR] + [SMEM] * 3 + [FAR] + [VMEM] * 3,
        out_specs=FAR,
        input_output_aliases={9: 0},
        scratch_shapes=[
            field,
            field,
            field,
            pltpu.VMEM((4 * PAD, COLS), f32),
            pltpu.VMEM((ROWS, COLS), f32),
            pltpu.VMEM((ROWS, COLS), f32),
            pltpu.VMEM((EDGE, COLS), f32),
            pltpu.VMEM((EDGE, COLS), f32),
            pltpu.VMEM((sources, SLOT, COLS), f32),
            chunks,
            chunks,
            pltpu.SemaphoreType.DMA,
        ],
        compiler_params=pltpu.CompilerParams(vmem_limit_bytes=(8 if small else 24) * MIB),
        name="second_step",
    )(
        swapped,
        next_swapped,
        beside,
        next_beside,
        edges,
        got,
        fold_partner,
        fold_flip,
        where,
        part,
        side_coeff,
        centre,
        vert_coeff,
    )


def swaps(first, end):
    return [pair for i in range(first, end - 1, 2) for pair in ((i, i + 1), (i + 1, i))]


def solution(mesh):
    in_specs = (
        P(None, "tile", "col"),
        P(None, "tile", "col"),
        P(None, None, "tile", "col"),
        P(None, None, "tile", "col"),
        P(None, "tile", "col"),
        P("tile", "col", None, None),
        P("tile", "col", None, None),
        P("tile", "col", None),
        P(),
        P(),
    )
    out_specs = P(None, "tile", "col")
    return jax.shard_map(body, mesh=mesh, in_specs=in_specs, out_specs=out_specs, check_vma=False)
```

```python
import functools

import jax
import jax.numpy as jnp
from jax import lax
from jax.experimental import pallas as pl
from jax.experimental.pallas import tpu as pltpu
from jax.sharding import PartitionSpec as P

LEVELS = 25
ROWS = 32
COLS = 128
CAP = 128
GROUP = 8
CHUNK = 5
PAD = 32
LINES = 4 * PAD
CORNER = 3 * LEVELS
SLOT = 80
EDGE = 32
OFFSET = (0, 50, 1, 51)
EDGES = 48 + 2 * PAD
LAND = 1e38
MIB = 1024 * 1024
VMEM = pl.BlockSpec(memory_space=pltpu.VMEM)
FAR = pl.BlockSpec(memory_space=pltpu.HBM)
SMEM = pl.BlockSpec(memory_space=pltpu.SMEM)


def iota(shape, dim):
    return lax.broadcasted_iota(jnp.int32, shape, dim)


def turn(x, shift, axis=1):
    shift = shift % x.shape[axis]
    return pltpu.roll(x, shift, axis) if shift else x


def terms(k, value, centre, side, vert):
    row, lane = iota((ROWS, COLS), 0), iota((ROWS, COLS), 1)
    y = value[k]
    east, west = side[0, k] * y, side[1, k] * y
    north, south = turn(side[2, k] * y, 1, 0), turn(side[3, k] * y, -1, 0)
    r = centre[k] * y
    r = r + jnp.where(lane > 0, turn(east, 1), 0.0) + jnp.where(lane < COLS - 1, turn(west, -1), 0.0)
    r = r + jnp.where(row > 0, north, 0.0) + jnp.where(row < ROWS - 1, south, 0.0)
    if k + 1 < LEVELS:
        r = r + vert[0, k + 1] * value[k + 1]
    if k > 0:
        r = r + vert[1, k - 1] * value[k - 1]
    return r, east, west, north, south


def outer(lane, last, first):
    return jnp.where(lane == COLS - 1, last, jnp.where(lane == 0, first, 0.0))


def scale_kernel(side, mask, scales):
    lane = iota((ROWS, COLS), 1)
    packed = jnp.zeros((ROWS, COLS), jnp.float32)
    for at in (16, 16 + PAD):
        scales[at + 24 : at + PAD, :] = jnp.zeros((8, COLS), jnp.float32)
    for k in range(LEVELS):
        m = mask[k].astype(jnp.float32)
        packed = packed + turn(m * outer(lane, side[0, k], side[1, k]), 2 * k + 1)
        scales[16 + k : 17 + k, :] = (m * side[2, k])[ROWS - 1 : ROWS]
        scales[16 + PAD + k : 17 + PAD + k, :] = (m * side[3, k])[0:1]
    scales[0:8, :], scales[8:16, :] = tight(packed)


def tight(packed):
    even = (iota((8, COLS), 1) & 1) == 0
    eastward = westward = jnp.zeros((8, COLS), jnp.float32)
    for g, offset in enumerate(OFFSET):
        rows = packed[8 * g : 8 * g + 8]
        eastward = eastward + turn(jnp.where(even, rows, 0.0), offset)
        westward = westward + turn(jnp.where(even, 0.0, rows), offset - 1)
    return eastward, westward


def forcing_kernel(sources, misfit, cell, count, adjoint_far, start, hot, valued, adjoint, arrived):
    load = pltpu.make_async_copy(adjoint_far, adjoint, arrived)
    load.start()
    group = min(GROUP, sources)
    lane = iota((1, CAP), 1)
    for first in range(0, sources, group):
        for s in range(group):
            at = slice(s * CAP, (s + 1) * CAP)
            cells = cell[first + s : first + s + 1, :]
            v = jnp.where(lane < count[0, first + s], misfit[first + s : first + s + 1, :], 0.0)
            high = v.astype(jnp.bfloat16).astype(jnp.float32)
            middle = (v - high).astype(jnp.bfloat16).astype(jnp.float32)
            low = v - high - middle
            column = iota((COLS, CAP), 0) == (cells & (COLS - 1))
            for i, part in enumerate((high, middle, low)):
                valued[i * COLS : (i + 1) * COLS, at] = jnp.where(column, part, 0.0).astype(jnp.bfloat16)
            place = cells >> 7
            for k in range(LEVELS):
                match = (iota((ROWS, CAP), 0) + k * ROWS) == place
                hot[k * ROWS : (k + 1) * ROWS, at] = jnp.where(match, 1.0, 0.0).astype(jnp.bfloat16)
        part = lax.dot_general(hot[...], valued[...], (((1,), (1,)), ((), ())), preferred_element_type=jnp.float32)
        part = part[:, 0:COLS] + part[:, COLS : 2 * COLS] + part[:, 2 * COLS : 3 * COLS]
        if first == 0:
            load.wait()
        held = adjoint if first == 0 else start
        for k in range(LEVELS):
            start[k] = held[k] + part[k * ROWS : (k + 1) * ROWS, :]


def to_lanes(column, offset):
    level = iota((PAD, COLS), 0)
    spot = (iota((PAD, COLS), 1) == 2 * level + offset) & (level < LEVELS)
    return jnp.sum(jnp.where(spot, column, 0.0), axis=0, keepdims=True)


def to_rows(line, offset):
    level = iota((PAD, COLS), 0)
    spot = (iota((PAD, COLS), 1) == 2 * level + offset) & (level < LEVELS)
    return jnp.sum(jnp.where(spot, line, 0.0), axis=1, keepdims=True)


def spot_rows(first, last):
    row = iota((8, COLS), 0)
    return jnp.where(row == 0, first, 0.0) + jnp.where(row == 7, last, 0.0)


def ends(block):
    return block[:, COLS - 1 : COLS], block[:, 0:1]


def from_tiles(swapped, next_swapped, where, start):
    rows = slice(start, start + PAD)
    upward = where[4] == 0
    return (
        jnp.where(upward, next_swapped[rows, :], swapped[rows, :]),
        jnp.where(upward, swapped[rows, :], next_swapped[rows, :]),
    )


def chunk(source, target, semaphores, i):
    levels = pl.ds(i * CHUNK, CHUNK)
    return pltpu.make_async_copy(source.at[levels], target.at[levels], semaphores.at[i])


def first_kernel(held, where, scales, side, centre, vert, mask, part, next_swap, swap, edges, slots, up, down, base, picked, next_picked, posted):
    for i in range(4):
        for ref in (up, down):
            ref[i * PAD + 24 : (i + 1) * PAD, :] = jnp.zeros((8, COLS), jnp.float32)
    lane = iota((ROWS, COLS), 1)
    packed = [jnp.zeros((ROWS, COLS), jnp.float32)] * 2
    for k in range(LEVELS):
        r, east, west, north, south = terms(k, held, centre, side, vert)
        part[k] = jnp.where(mask[k] == 0, LAND, r)
        sides = outer(lane, east, west)
        for ref, leaving, at in ((up, north[0:1], ROWS - 1), (down, south[ROWS - 1 : ROWS], 0)):
            ref[k : k + 1, :] = leaving
            ref[PAD + k : PAD + k + 1, :] = r[at : at + 1]
            ref[3 * PAD + k : 3 * PAD + k + 1, :] = sides[at : at + 1]
        packed = [p + turn(x, 2 * k + 1) for p, x in zip(packed, (sides, outer(lane, r, r)))]
    up[2 * PAD : 3 * PAD, :] = scales[16 : 16 + PAD, :]
    down[2 * PAD : 3 * PAD, :] = scales[16 + PAD : 16 + 2 * PAD, :]
    for i in range(3):
        base[i * LEVELS : (i + 1) * LEVELS, :] = up[i * PAD : i * PAD + LEVELS, :]
    own_east, own_west = ends(up[3 * PAD : 4 * PAD, :])
    base[CORNER : CORNER + 1, :] = to_lanes(own_east, OFFSET[0]) + to_lanes(own_west, OFFSET[1])
    base[CORNER + 1 : SLOT, :] = jnp.zeros((SLOT - CORNER - 1, COLS), jnp.float32)
    spread = [pltpu.make_async_copy(base, slots.at[s], posted.at[s]) for s in range(slots.shape[0])]
    for copy in spread:
        copy.start()
    upward = where[4] == 0
    picked[...] = jnp.where(upward, up[...], down[...])
    next_picked[...] = jnp.where(upward, down[...], up[...])
    spread.append(pltpu.make_async_copy(picked, swap, posted.at[slots.shape[0]]))
    spread.append(pltpu.make_async_copy(next_picked, next_swap, posted.at[slots.shape[0] + 1]))
    for copy in spread[-2:]:
        copy.start()
    for i, p in enumerate(packed):
        edges[8 * i : 8 * i + 8, :], edges[24 + 8 * i : 32 + 8 * i, :] = tight(p)
    edges[16:24, :] = scales[0:8, :]
    edges[40:48, :] = scales[8:16, :]
    edges[48 : 48 + PAD, :] = down[0:PAD, :]
    edges[48 + PAD : EDGES, :] = up[0:PAD, :]
    for copy in spread:
        copy.wait()


def corner_kernel(swapped, next_swapped, edges, where, next_swap, swap):
    low, high = from_tiles(swapped, next_swapped, where, 0)
    low_sides, high_sides = from_tiles(swapped, next_swapped, where, 3 * PAD)
    low_last, low_first = ends(low)
    high_last, high_first = ends(high)
    low_east, low_west = ends(low_sides)
    high_east, high_west = ends(high_sides)
    corners = (
        to_lanes(low_east, OFFSET[0]) + to_lanes(low_west, OFFSET[1]) + to_lanes(high_west, OFFSET[2]) + to_lanes(high_east, OFFSET[3])
    )
    eastward = spot_rows(to_lanes(low_last, OFFSET[0]), to_lanes(high_last, OFFSET[3]))
    westward = spot_rows(to_lanes(low_first, OFFSET[0]), to_lanes(high_first, OFFSET[3]))
    to_east = where[5] == 0
    for ref, chosen in ((swap, to_east), (next_swap, jnp.logical_not(to_east))):
        ref[0:24, :] = jnp.where(chosen, edges[0:24, :], edges[24:48, :])
        ref[8:16, :] += jnp.where(chosen, eastward, westward)
        ref[24:EDGE, :] = jnp.where(iota((EDGE - 24, COLS), 0) == 0, corners, 0.0)


def second_kernel(swapped, next_swapped, beside, next_beside, edges, got_far, partner, flip, where, part, side, centre, vert, out, held, result, lines, near_sides, far_sides, west_side, east_side, got, sent, gathered):
    gather = pltpu.make_async_copy(got_far, got, gathered)
    gather.start()
    sources = got.shape[0]
    below_near, above_near = from_tiles(swapped, next_swapped, where, 0)
    below_part, above_part = from_tiles(swapped, next_swapped, where, PAD)
    below_scale, above_scale = from_tiles(swapped, next_swapped, where, 2 * PAD)
    sum_low = below_part + edges[48 : 48 + PAD, :]
    sum_high = above_part + edges[48 + PAD : EDGES, :]
    even_column = where[5] == 0
    west_side[...] = jnp.where(even_column, next_beside[...], beside[...])
    east_side[...] = jnp.where(even_column, beside[...], next_beside[...])
    column, top, left, right = where[0], where[1], where[2], where[3]
    at_top = top == 1

    def comes_from(target):
        source = 0
        for s in range(sources):
            source = jnp.where(partner[s] == target, s, source)
        return source

    def turned(rows, source):
        back = COLS - 1 - iota((PAD, COLS), 1)
        return jnp.where(flip[source] == 1, jnp.take_along_axis(rows, back, axis=1), rows)

    level_lane = iota((PAD, COLS), 1)
    gather.wait()
    source = comes_from(column)
    earlier = comes_from(source)
    before = jnp.where(source == 0, sources - 1, source - 1)
    after = jnp.where(source == sources - 1, 0, source + 1)
    corner_left = west_side[24:25, :]
    corner_right = east_side[24:25, :]
    sum_low = sum_low + jnp.where(level_lane == 0, to_rows(corner_left, OFFSET[0]), 0.0)
    sum_low = sum_low + jnp.where(level_lane == COLS - 1, to_rows(corner_right, OFFSET[1]), 0.0)
    sum_high = sum_high + jnp.where(level_lane == 0, to_rows(corner_left, OFFSET[3]), 0.0)
    sum_high = sum_high + jnp.where(level_lane == COLS - 1, to_rows(corner_right, OFFSET[2]), 0.0)
    fold_first = turned(got[source, 0:PAD, :], source)
    sum_fold = got[source, LEVELS : LEVELS + PAD, :] + turned(got[earlier, 0:PAD, :], earlier)
    cross_west = to_rows(got[before, CORNER : CORNER + 1, :], OFFSET[0])
    cross_east = to_rows(got[after, CORNER : CORNER + 1, :], OFFSET[1])
    sum_fold = sum_fold + jnp.where(level_lane == 0, cross_west, 0.0) + jnp.where(level_lane == COLS - 1, cross_east, 0.0)
    fold_second = turned(turn(got[source, SLOT - PAD : SLOT, :], SLOT - PAD - 2 * LEVELS, 0) * sum_fold, source)
    lines[0:PAD, :] = jnp.where(at_top, fold_first, above_near)
    lines[PAD : 2 * PAD, :] = below_scale * sum_low
    lines[2 * PAD : 3 * PAD, :] = jnp.where(at_top, fold_second, above_scale * sum_high)
    lines[3 * PAD : 4 * PAD, :] = below_near
    from_left = comes_from(left)
    from_right = comes_from(right)
    fold_left = turned(got[from_left, 0:PAD, :], from_left)[:, COLS - 1 : COLS]
    fold_right = turned(got[from_right, 0:PAD, :], from_right)[:, 0:1]
    fold_left = jnp.where(at_top, to_lanes(fold_left, OFFSET[3]), 0.0)
    fold_right = jnp.where(at_top, to_lanes(fold_right, OFFSET[3]), 0.0)
    near_left = west_side[0:8, :]
    near_right = east_side[0:8, :]
    next_left = west_side[16:24, :] * (west_side[8:16, :] + edges[24:32, :] + spot_rows(0.0, fold_left))
    next_right = east_side[16:24, :] * (east_side[8:16, :] + edges[0:8, :] + spot_rows(0.0, fold_right))
    even = (iota((8, COLS), 1) & 1) == 0
    for ref, from_west, from_east in ((near_sides, near_left, near_right), (far_sides, next_left, next_right)):
        for g, offset in enumerate(OFFSET):
            ref[8 * g : 8 * g + 8, :] = jnp.where(even, turn(from_west, -offset), turn(from_east, -offset - 1))

    row, lane = iota((ROWS, COLS), 0), iota((ROWS, COLS), 1)

    def joined(k, r, sides, first, last):
        r = r + jnp.where((lane == 0) | (lane == COLS - 1), turn(sides[...], -2 * k), 0.0)
        r = r + jnp.where(row == 0, first, 0.0) + jnp.where(row == ROWS - 1, last, 0.0)
        return jnp.where(part[k] == LAND, 0.0, r)

    for k in range(LEVELS):
        held[k] = joined(k, part[k], near_sides, lines[3 * PAD + k : 3 * PAD + k + 1, :], lines[k : k + 1, :])
    for k in range(LEVELS):
        r = terms(k, held, centre, side, vert)[0]
        result[k] = joined(k, r, far_sides, lines[PAD + k : PAD + k + 1, :], lines[2 * PAD + k : 2 * PAD + k + 1, :])
        if (k + 1) % CHUNK == 0:
            chunk(result, out, sent, k // CHUNK).start()
    for i in range(LEVELS // CHUNK):
        chunk(result, out, sent, i).wait()


def body(adjoint_in, centre, side_coeff, vert_coeff, land_mask, obs_misfit, obs_cell, obs_count, fold_partner, fold_flip):
    sources = obs_misfit.shape[2]
    tiles = lax.axis_size("tile")
    column, tile_row = lax.axis_index("col"), lax.axis_index("tile")
    where = jnp.stack(
        [
            column,
            (tile_row == tiles - 1).astype(jnp.int32),
            jnp.where(column == 0, sources - 1, column - 1),
            jnp.where(column == sources - 1, 0, column + 1),
            tile_row & 1,
            column & 1,
        ]
    )
    received = lax.all_to_all(obs_misfit, "col", split_axis=2, concat_axis=1, tiled=True)
    f32 = jnp.float32
    tile = jax.ShapeDtypeStruct((LEVELS, ROWS, COLS), f32)
    lines = pltpu.HBM((LINES, COLS), f32)
    field = pltpu.VMEM((LEVELS, ROWS, COLS), f32)
    chunks = pltpu.SemaphoreType.DMA((LEVELS // CHUNK,))
    group = min(GROUP, sources)
    small = sources <= GROUP
    ahead = pl.CostEstimate(flops=10**10, bytes_accessed=2 * 10**8, transcendentals=0)
    scales = pl.pallas_call(
        scale_kernel,
        out_shape=jax.ShapeDtypeStruct((16 + 2 * PAD, COLS), f32),
        in_specs=[VMEM, VMEM],
        out_specs=VMEM,
        compiler_params=pltpu.CompilerParams(vmem_limit_bytes=4 * MIB),
        cost_estimate=ahead,
        name="edge_scales",
    )(side_coeff, land_mask)
    start = pl.pallas_call(
        functools.partial(forcing_kernel, sources),
        out_shape=tile,
        in_specs=[VMEM, VMEM, SMEM, FAR],
        out_specs=VMEM,
        scratch_shapes=[
            pltpu.VMEM((LEVELS * ROWS, group * CAP), jnp.bfloat16),
            pltpu.VMEM((3 * COLS, group * CAP), jnp.bfloat16),
            field,
            pltpu.SemaphoreType.DMA,
        ],
        compiler_params=pltpu.CompilerParams(vmem_limit_bytes=(8 if small else 24) * MIB),
        cost_estimate=pl.CostEstimate(flops=10**8, bytes_accessed=8 * 10**6, transcendentals=0),
        name="forcing",
    )(received.reshape(sources, CAP), obs_cell.reshape(sources, CAP), obs_count.reshape(1, sources), pltpu.with_memory_space_constraint(adjoint_in, pltpu.HBM))
    part, next_swap, swap, edges, slots = pl.pallas_call(
        first_kernel,
        out_shape=(pltpu.VMEM((LEVELS, ROWS, COLS), f32), lines, lines, jax.ShapeDtypeStruct((EDGES, COLS), f32), pltpu.HBM((sources, SLOT, COLS), f32)),
        in_specs=[VMEM, SMEM] + [VMEM] * 5,
        out_specs=(VMEM, FAR, FAR, VMEM, FAR),
        scratch_shapes=[
            pltpu.VMEM((LINES, COLS), f32),
            pltpu.VMEM((LINES, COLS), f32),
            pltpu.VMEM((SLOT, COLS), f32),
            pltpu.VMEM((LINES, COLS), f32),
            pltpu.VMEM((LINES, COLS), f32),
            pltpu.SemaphoreType.DMA((sources + 2,)),
        ],
        compiler_params=pltpu.CompilerParams(vmem_limit_bytes=(8 if small else 24) * MIB),
        name="first_step",
    )(start, where, scales, side_coeff, centre, vert_coeff, land_mask)
    got = lax.all_to_all(slots, "col", split_axis=0, concat_axis=0, tiled=True)
    swapped = lax.ppermute(swap, "tile", swaps(0, tiles))
    next_swapped = lax.ppermute(next_swap, "tile", swaps(1, tiles - 1))
    edge = jax.ShapeDtypeStruct((EDGE, COLS), f32)
    next_beside, beside = pl.pallas_call(
        corner_kernel,
        out_shape=(edge, edge),
        in_specs=[VMEM, VMEM, VMEM, SMEM],
        out_specs=(VMEM, VMEM),
        compiler_params=pltpu.CompilerParams(vmem_limit_bytes=4 * MIB),
        cost_estimate=pl.CostEstimate(flops=10**6, bytes_accessed=4 * 10**6, transcendentals=0),
        name="corners",
    )(swapped, next_swapped, edges, where)
    round_trip = [(sources - 1, 0), (0, sources - 1)]
    next_beside = lax.ppermute(next_beside, "col", swaps(1, sources - 1) + round_trip)
    beside = lax.ppermute(beside, "col", swaps(0, sources))
    return pl.pallas_call(
        second_kernel,
        out_shape=tile,
        in_specs=[VMEM] * 5 + [FAR] + [SMEM] * 3 + [VMEM] * 4,
        out_specs=FAR,
        scratch_shapes=[
            field,
            field,
            pltpu.VMEM((4 * PAD, COLS), f32),
            pltpu.VMEM((ROWS, COLS), f32),
            pltpu.VMEM((ROWS, COLS), f32),
            pltpu.VMEM((EDGE, COLS), f32),
            pltpu.VMEM((EDGE, COLS), f32),
            pltpu.VMEM((sources, SLOT, COLS), f32),
            chunks,
            pltpu.SemaphoreType.DMA,
        ],
        compiler_params=pltpu.CompilerParams(vmem_limit_bytes=(8 if small else 24) * MIB),
        name="second_step",
    )(
        swapped,
        next_swapped,
        beside,
        next_beside,
        edges,
        got,
        fold_partner,
        fold_flip,
        where,
        pltpu.with_memory_space_constraint(part, pltpu.VMEM),
        side_coeff,
        centre,
        vert_coeff,
    )


def swaps(first, end):
    return [pair for i in range(first, end - 1, 2) for pair in ((i, i + 1), (i + 1, i))]


def solution(mesh):
    in_specs = (
        P(None, "tile", "col"),
        P(None, "tile", "col"),
        P(None, None, "tile", "col"),
        P(None, None, "tile", "col"),
        P(None, "tile", "col"),
        P("tile", "col", None, None),
        P("tile", "col", None, None),
        P("tile", "col", None),
        P(),
        P(),
    )
    out_specs = P(None, "tile", "col")
    return jax.shard_map(body, mesh=mesh, in_specs=in_specs, out_specs=out_specs, check_vma=False)
```

```python
import functools

import jax
import jax.numpy as jnp
from jax import lax
from jax.experimental import pallas as pl
from jax.experimental.pallas import tpu as pltpu
from jax.sharding import PartitionSpec as P

LEVELS = 25
ROWS = 32
COLS = 128
CAP = 128
GROUP = 8
CHUNK = 5
PAD = 32
CORNER = 3 * LEVELS
SLOT = 80
EDGE = 32
OFFSET = (0, 50, 1, 51)
EDGES = 48 + 2 * PAD
LAND = 1e38
MIB = 1024 * 1024
VMEM = pl.BlockSpec(memory_space=pltpu.VMEM)
FAR = pl.BlockSpec(memory_space=pltpu.HBM)
SMEM = pl.BlockSpec(memory_space=pltpu.SMEM)


def iota(shape, dim):
    return lax.broadcasted_iota(jnp.int32, shape, dim)


def turn(x, shift, axis=1):
    shift = shift % x.shape[axis]
    return pltpu.roll(x, shift, axis) if shift else x


def terms(k, value, centre, side, vert):
    row, lane = iota((ROWS, COLS), 0), iota((ROWS, COLS), 1)
    y = value[k]
    east, west = side[0, k] * y, side[1, k] * y
    north, south = turn(side[2, k] * y, 1, 0), turn(side[3, k] * y, -1, 0)
    r = centre[k] * y
    r = r + jnp.where(lane > 0, turn(east, 1), 0.0) + jnp.where(lane < COLS - 1, turn(west, -1), 0.0)
    r = r + jnp.where(row > 0, north, 0.0) + jnp.where(row < ROWS - 1, south, 0.0)
    if k + 1 < LEVELS:
        r = r + vert[0, k + 1] * value[k + 1]
    if k > 0:
        r = r + vert[1, k - 1] * value[k - 1]
    return r, east, west, north, south


def outer(lane, last, first):
    return jnp.where(lane == COLS - 1, last, jnp.where(lane == 0, first, 0.0))


def scale_kernel(side, mask, scales):
    lane = iota((ROWS, COLS), 1)
    packed = jnp.zeros((ROWS, COLS), jnp.float32)
    for at in (16, 16 + PAD):
        scales[at + 24 : at + PAD, :] = jnp.zeros((8, COLS), jnp.float32)
    for k in range(LEVELS):
        m = mask[k].astype(jnp.float32)
        packed = packed + turn(m * outer(lane, side[0, k], side[1, k]), 2 * k + 1)
        scales[16 + k : 17 + k, :] = (m * side[2, k])[ROWS - 1 : ROWS]
        scales[16 + PAD + k : 17 + PAD + k, :] = (m * side[3, k])[0:1]
    scales[0:8, :], scales[8:16, :] = tight(packed)


def tight(packed):
    even = (iota((8, COLS), 1) & 1) == 0
    eastward = westward = jnp.zeros((8, COLS), jnp.float32)
    for g, offset in enumerate(OFFSET):
        rows = packed[8 * g : 8 * g + 8]
        eastward = eastward + turn(jnp.where(even, rows, 0.0), offset)
        westward = westward + turn(jnp.where(even, 0.0, rows), offset - 1)
    return eastward, westward


def forcing_kernel(sources, misfit, cell, count, adjoint_far, start, hot, valued, adjoint, arrived):
    load = pltpu.make_async_copy(adjoint_far, adjoint, arrived)
    load.start()
    group = min(GROUP, sources)
    lane = iota((1, CAP), 1)
    for first in range(0, sources, group):
        for s in range(group):
            at = slice(s * CAP, (s + 1) * CAP)
            cells = cell[first + s : first + s + 1, :]
            v = jnp.where(lane < count[0, first + s], misfit[first + s : first + s + 1, :], 0.0)
            high = v.astype(jnp.bfloat16).astype(jnp.float32)
            low = v - high
            column = iota((COLS, CAP), 0) == (cells & (COLS - 1))
            for i, part in enumerate((high, low)):
                valued[i * COLS : (i + 1) * COLS, at] = jnp.where(column, part, 0.0).astype(jnp.bfloat16)
            place = cells >> 7
            for k in range(LEVELS):
                match = (iota((ROWS, CAP), 0) + k * ROWS) == place
                hot[k * ROWS : (k + 1) * ROWS, at] = jnp.where(match, 1.0, 0.0).astype(jnp.bfloat16)
        part = lax.dot_general(hot[...], valued[...], (((1,), (1,)), ((), ())), preferred_element_type=jnp.float32)
        part = part[:, 0:COLS] + part[:, COLS : 2 * COLS]
        if first == 0:
            load.wait()
        held = adjoint if first == 0 else start
        for k in range(LEVELS):
            start[k] = held[k] + part[k * ROWS : (k + 1) * ROWS, :]


def to_lanes(column, offset):
    level = iota((PAD, COLS), 0)
    spot = (iota((PAD, COLS), 1) == 2 * level + offset) & (level < LEVELS)
    return jnp.sum(jnp.where(spot, column, 0.0), axis=0, keepdims=True)


def to_rows(line, offset):
    level = iota((PAD, COLS), 0)
    spot = (iota((PAD, COLS), 1) == 2 * level + offset) & (level < LEVELS)
    return jnp.sum(jnp.where(spot, line, 0.0), axis=1, keepdims=True)


def spot_rows(first, last):
    row = iota((8, COLS), 0)
    return jnp.where(row == 0, first, 0.0) + jnp.where(row == 7, last, 0.0)


def ends(block):
    return block[:, COLS - 1 : COLS], block[:, 0:1]


def from_tiles(swapped, next_swapped, where, rows):
    upward = where[4] == 0
    first, second = swapped[rows, :], next_swapped[rows, :]
    return jnp.where(upward, second, first), jnp.where(upward, first, second)


def chunk(source, target, semaphores, i):
    levels = pl.ds(i * CHUNK, CHUNK)
    return pltpu.make_async_copy(source.at[levels], target.at[levels], semaphores.at[i])


def first_kernel(held, where, scales, side, centre, vert, mask, part_far, swap, next_swap, edges, slots, part, up, down, tips, picked, next_picked, sent, posted):
    for ref in (up, down):
        ref[CORNER + 1 : SLOT, :] = jnp.zeros((SLOT - CORNER - 1, COLS), jnp.float32)
    for i in range(2):
        tips[i * PAD + 24 : (i + 1) * PAD, :] = jnp.zeros((8, COLS), jnp.float32)
    lane = iota((ROWS, COLS), 1)
    packed = [jnp.zeros((ROWS, COLS), jnp.float32)] * 2
    for k in range(LEVELS):
        r, east, west, north, south = terms(k, held, centre, side, vert)
        part[k] = jnp.where(mask[k] == 0, LAND, r)
        sides = outer(lane, east, west)
        for i, (ref, leaving, at) in enumerate(((up, north[0:1], ROWS - 1), (down, south[ROWS - 1 : ROWS], 0))):
            ref[k : k + 1, :] = leaving
            ref[LEVELS + k : LEVELS + k + 1, :] = r[at : at + 1]
            tips[i * PAD + k : i * PAD + k + 1, :] = sides[at : at + 1]
        packed = [p + turn(x, 2 * k + 1) for p, x in zip(packed, (sides, outer(lane, r, r)))]
        if (k + 1) % CHUNK == 0:
            chunk(part, part_far, sent, k // CHUNK).start()
    for i, ref in enumerate((up, down)):
        ref[2 * LEVELS : 3 * LEVELS, :] = scales[16 + i * PAD : 16 + i * PAD + LEVELS, :]
        east, west = ends(tips[i * PAD : (i + 1) * PAD, :])
        ref[CORNER : CORNER + 1, :] = to_lanes(east, OFFSET[0]) + to_lanes(west, OFFSET[1])
    spread = [pltpu.make_async_copy(up, slots.at[s], posted.at[s]) for s in range(slots.shape[0])]
    for copy in spread:
        copy.start()
    upward = where[4] == 0
    picked[...] = jnp.where(upward, up[...], down[...])
    next_picked[...] = jnp.where(upward, down[...], up[...])
    spread.append(pltpu.make_async_copy(picked, swap, posted.at[slots.shape[0]]))
    spread.append(pltpu.make_async_copy(next_picked, next_swap, posted.at[slots.shape[0] + 1]))
    for copy in spread[-2:]:
        copy.start()
    for i, p in enumerate(packed):
        edges[8 * i : 8 * i + 8, :], edges[24 + 8 * i : 32 + 8 * i, :] = tight(p)
    edges[16:24, :] = scales[0:8, :]
    edges[40:48, :] = scales[8:16, :]
    edges[48 : 48 + PAD, :] = down[0:PAD, :]
    edges[48 + PAD : EDGES, :] = up[0:PAD, :]
    for i in range(LEVELS // CHUNK):
        chunk(part, part_far, sent, i).wait()
    for copy in spread:
        copy.wait()


def corner_kernel(swapped, next_swapped, edges, where, swap, next_swap):
    low, high = from_tiles(swapped, next_swapped, where, slice(0, PAD))
    low_tips, high_tips = from_tiles(swapped, next_swapped, where, slice(CORNER, CORNER + 1))
    low_last, low_first = ends(low)
    high_last, high_first = ends(high)
    eastern = iota((1, COLS), 1) < OFFSET[1]
    corners = low_tips + turn(jnp.where(eastern, high_tips, 0.0), OFFSET[3] - OFFSET[0])
    corners = corners + turn(jnp.where(eastern, 0.0, high_tips), OFFSET[2] - OFFSET[1])
    eastward = spot_rows(to_lanes(low_last, OFFSET[0]), to_lanes(high_last, OFFSET[3]))
    westward = spot_rows(to_lanes(low_first, OFFSET[0]), to_lanes(high_first, OFFSET[3]))
    to_east = where[5] == 0
    for ref, chosen in ((swap, to_east), (next_swap, jnp.logical_not(to_east))):
        ref[0:24, :] = jnp.where(chosen, edges[0:24, :], edges[24:48, :])
        ref[8:16, :] += jnp.where(chosen, eastward, westward)
        ref[24:EDGE, :] = jnp.where(iota((EDGE - 24, COLS), 0) == 0, corners, 0.0)


def second_kernel(swapped, next_swapped, beside, next_beside, edges, got_far, partner, flip, where, part_far, side, centre, vert, out, held, part, result, lines, near_sides, far_sides, west_side, east_side, got, loaded, sent, gathered):
    gather = pltpu.make_async_copy(got_far, got, gathered)
    gather.start()
    for i in range(LEVELS // CHUNK):
        chunk(part_far, part, loaded, i).start()
    sources = got.shape[0]
    below_near, above_near = from_tiles(swapped, next_swapped, where, slice(0, PAD))
    below_part, above_part = from_tiles(swapped, next_swapped, where, slice(LEVELS, LEVELS + PAD))
    below_scale, above_scale = (
        turn(rows, SLOT - PAD - 2 * LEVELS, 0)
        for rows in from_tiles(swapped, next_swapped, where, slice(SLOT - PAD, SLOT))
    )
    sum_low = below_part + edges[48 : 48 + PAD, :]
    sum_high = above_part + edges[48 + PAD : EDGES, :]
    even_column = where[5] == 0
    west_side[...] = jnp.where(even_column, next_beside[...], beside[...])
    east_side[...] = jnp.where(even_column, beside[...], next_beside[...])
    column, top, left, right = where[0], where[1], where[2], where[3]
    at_top = top == 1

    def comes_from(target):
        source = 0
        for s in range(sources):
            source = jnp.where(partner[s] == target, s, source)
        return source

    def turned(rows, source):
        back = COLS - 1 - iota((PAD, COLS), 1)
        return jnp.where(flip[source] == 1, jnp.take_along_axis(rows, back, axis=1), rows)

    level_lane = iota((PAD, COLS), 1)
    gather.wait()
    source = comes_from(column)
    earlier = comes_from(source)
    before = jnp.where(source == 0, sources - 1, source - 1)
    after = jnp.where(source == sources - 1, 0, source + 1)
    corner_left = west_side[24:25, :]
    corner_right = east_side[24:25, :]
    sum_low = sum_low + jnp.where(level_lane == 0, to_rows(corner_left, OFFSET[0]), 0.0)
    sum_low = sum_low + jnp.where(level_lane == COLS - 1, to_rows(corner_right, OFFSET[1]), 0.0)
    sum_high = sum_high + jnp.where(level_lane == 0, to_rows(corner_left, OFFSET[3]), 0.0)
    sum_high = sum_high + jnp.where(level_lane == COLS - 1, to_rows(corner_right, OFFSET[2]), 0.0)
    fold_first = turned(got[source, 0:PAD, :], source)
    sum_fold = got[source, LEVELS : LEVELS + PAD, :] + turned(got[earlier, 0:PAD, :], earlier)
    cross_west = to_rows(got[before, CORNER : CORNER + 1, :], OFFSET[0])
    cross_east = to_rows(got[after, CORNER : CORNER + 1, :], OFFSET[1])
    sum_fold = sum_fold + jnp.where(level_lane == 0, cross_west, 0.0) + jnp.where(level_lane == COLS - 1, cross_east, 0.0)
    fold_second = turned(turn(got[source, SLOT - PAD : SLOT, :], SLOT - PAD - 2 * LEVELS, 0) * sum_fold, source)
    lines[0:PAD, :] = jnp.where(at_top, fold_first, above_near)
    lines[PAD : 2 * PAD, :] = below_scale * sum_low
    lines[2 * PAD : 3 * PAD, :] = jnp.where(at_top, fold_second, above_scale * sum_high)
    lines[3 * PAD : 4 * PAD, :] = below_near
    from_left = comes_from(left)
    from_right = comes_from(right)
    fold_left = turned(got[from_left, 0:PAD, :], from_left)[:, COLS - 1 : COLS]
    fold_right = turned(got[from_right, 0:PAD, :], from_right)[:, 0:1]
    fold_left = jnp.where(at_top, to_lanes(fold_left, OFFSET[3]), 0.0)
    fold_right = jnp.where(at_top, to_lanes(fold_right, OFFSET[3]), 0.0)
    near_left = west_side[0:8, :]
    near_right = east_side[0:8, :]
    next_left = west_side[16:24, :] * (west_side[8:16, :] + edges[24:32, :] + spot_rows(0.0, fold_left))
    next_right = east_side[16:24, :] * (east_side[8:16, :] + edges[0:8, :] + spot_rows(0.0, fold_right))
    even = (iota((8, COLS), 1) & 1) == 0
    for ref, from_west, from_east in ((near_sides, near_left, near_right), (far_sides, next_left, next_right)):
        for g, offset in enumerate(OFFSET):
            ref[8 * g : 8 * g + 8, :] = jnp.where(even, turn(from_west, -offset), turn(from_east, -offset - 1))

    row, lane = iota((ROWS, COLS), 0), iota((ROWS, COLS), 1)

    def joined(k, r, sides, first, last):
        r = r + jnp.where((lane == 0) | (lane == COLS - 1), turn(sides[...], -2 * k), 0.0)
        r = r + jnp.where(row == 0, first, 0.0) + jnp.where(row == ROWS - 1, last, 0.0)
        return jnp.where(part[k] == LAND, 0.0, r)

    for k in range(LEVELS):
        if k % CHUNK == 0:
            chunk(part_far, part, loaded, k // CHUNK).wait()
        held[k] = joined(k, part[k], near_sides, lines[3 * PAD + k : 3 * PAD + k + 1, :], lines[k : k + 1, :])
    for k in range(LEVELS):
        r = terms(k, held, centre, side, vert)[0]
        result[k] = joined(k, r, far_sides, lines[PAD + k : PAD + k + 1, :], lines[2 * PAD + k : 2 * PAD + k + 1, :])
        if (k + 1) % CHUNK == 0:
            chunk(result, out, sent, k // CHUNK).start()
    for i in range(LEVELS // CHUNK):
        chunk(result, out, sent, i).wait()


def body(adjoint_in, centre, side_coeff, vert_coeff, land_mask, obs_misfit, obs_cell, obs_count, fold_partner, fold_flip):
    sources = obs_misfit.shape[2]
    tiles = lax.axis_size("tile")
    column, tile_row = lax.axis_index("col"), lax.axis_index("tile")
    where = jnp.stack(
        [
            column,
            (tile_row == tiles - 1).astype(jnp.int32),
            jnp.where(column == 0, sources - 1, column - 1),
            jnp.where(column == sources - 1, 0, column + 1),
            tile_row & 1,
            column & 1,
        ]
    )
    received = lax.all_to_all(obs_misfit, "col", split_axis=2, concat_axis=1, tiled=True)
    f32 = jnp.float32
    tile = jax.ShapeDtypeStruct((LEVELS, ROWS, COLS), f32)
    lines = pltpu.HBM((SLOT, COLS), f32)
    field = pltpu.VMEM((LEVELS, ROWS, COLS), f32)
    chunks = pltpu.SemaphoreType.DMA((LEVELS // CHUNK,))
    group = min(GROUP, sources)
    small = sources <= GROUP
    ahead = pl.CostEstimate(flops=10**10, bytes_accessed=2 * 10**8, transcendentals=0)
    scales = pl.pallas_call(
        scale_kernel,
        out_shape=jax.ShapeDtypeStruct((16 + 2 * PAD, COLS), f32),
        in_specs=[VMEM, VMEM],
        out_specs=VMEM,
        compiler_params=pltpu.CompilerParams(vmem_limit_bytes=4 * MIB),
        cost_estimate=ahead,
        name="edge_scales",
    )(side_coeff, land_mask)
    start = pl.pallas_call(
        functools.partial(forcing_kernel, sources),
        out_shape=tile,
        in_specs=[VMEM, VMEM, SMEM, FAR],
        out_specs=VMEM,
        scratch_shapes=[
            pltpu.VMEM((LEVELS * ROWS, group * CAP), jnp.bfloat16),
            pltpu.VMEM((2 * COLS, group * CAP), jnp.bfloat16),
            field,
            pltpu.SemaphoreType.DMA,
        ],
        compiler_params=pltpu.CompilerParams(vmem_limit_bytes=(8 if small else 24) * MIB),
        cost_estimate=pl.CostEstimate(flops=10**8, bytes_accessed=8 * 10**6, transcendentals=0),
        name="forcing",
    )(received.reshape(sources, CAP), obs_cell.reshape(sources, CAP), obs_count.reshape(1, sources), pltpu.with_memory_space_constraint(adjoint_in, pltpu.HBM))
    part, swap, next_swap, edges, slots = pl.pallas_call(
        first_kernel,
        out_shape=(tile, lines, lines, jax.ShapeDtypeStruct((EDGES, COLS), f32), pltpu.HBM((sources, SLOT, COLS), f32)),
        in_specs=[VMEM, SMEM] + [VMEM] * 5,
        out_specs=(FAR, FAR, FAR, VMEM, FAR),
        scratch_shapes=[
            field,
            pltpu.VMEM((SLOT, COLS), f32),
            pltpu.VMEM((SLOT, COLS), f32),
            pltpu.VMEM((2 * PAD, COLS), f32),
            pltpu.VMEM((SLOT, COLS), f32),
            pltpu.VMEM((SLOT, COLS), f32),
            chunks,
            pltpu.SemaphoreType.DMA((sources + 2,)),
        ],
        compiler_params=pltpu.CompilerParams(vmem_limit_bytes=(8 if small else 24) * MIB),
        name="first_step",
    )(start, where, scales, side_coeff, centre, vert_coeff, land_mask)
    got = lax.all_to_all(slots, "col", split_axis=0, concat_axis=0, tiled=True)
    next_swapped = lax.ppermute(next_swap, "tile", swaps(1, tiles - 1))
    swapped = lax.ppermute(swap, "tile", swaps(0, tiles))
    edge = jax.ShapeDtypeStruct((EDGE, COLS), f32)
    beside, next_beside = pl.pallas_call(
        corner_kernel,
        out_shape=(edge, edge),
        in_specs=[VMEM, VMEM, VMEM, SMEM],
        out_specs=(VMEM, VMEM),
        compiler_params=pltpu.CompilerParams(vmem_limit_bytes=4 * MIB),
        cost_estimate=pl.CostEstimate(flops=10**6, bytes_accessed=4 * 10**6, transcendentals=0),
        name="corners",
    )(swapped, next_swapped, edges, where)
    round_trip = [(sources - 1, 0), (0, sources - 1)]
    next_beside = lax.ppermute(next_beside, "col", swaps(1, sources - 1) + round_trip)
    beside = lax.ppermute(beside, "col", swaps(0, sources))
    return pl.pallas_call(
        second_kernel,
        out_shape=tile,
        in_specs=[VMEM] * 5 + [FAR] + [SMEM] * 3 + [FAR] + [VMEM] * 3,
        out_specs=FAR,
        input_output_aliases={9: 0},
        scratch_shapes=[
            field,
            field,
            field,
            pltpu.VMEM((4 * PAD, COLS), f32),
            pltpu.VMEM((ROWS, COLS), f32),
            pltpu.VMEM((ROWS, COLS), f32),
            pltpu.VMEM((EDGE, COLS), f32),
            pltpu.VMEM((EDGE, COLS), f32),
            pltpu.VMEM((sources, SLOT, COLS), f32),
            chunks,
            chunks,
            pltpu.SemaphoreType.DMA,
        ],
        compiler_params=pltpu.CompilerParams(vmem_limit_bytes=(8 if small else 24) * MIB),
        name="second_step",
    )(
        swapped,
        next_swapped,
        beside,
        next_beside,
        edges,
        got,
        fold_partner,
        fold_flip,
        where,
        part,
        side_coeff,
        centre,
        vert_coeff,
    )


def swaps(first, end):
    return [pair for i in range(first, end - 1, 2) for pair in ((i, i + 1), (i + 1, i))]


def solution(mesh):
    in_specs = (
        P(None, "tile", "col"),
        P(None, "tile", "col"),
        P(None, None, "tile", "col"),
        P(None, None, "tile", "col"),
        P(None, "tile", "col"),
        P("tile", "col", None, None),
        P("tile", "col", None, None),
        P("tile", "col", None),
        P(),
        P(),
    )
    out_specs = P(None, "tile", "col")
    return jax.shard_map(body, mesh=mesh, in_specs=in_specs, out_specs=out_specs, check_vma=False)
```

```python
import functools

import jax
import jax.numpy as jnp
from jax import lax
from jax.experimental import pallas as pl
from jax.experimental.pallas import tpu as pltpu
from jax.sharding import PartitionSpec as P

LEVELS = 25
ROWS = 32
COLS = 128
CAP = 128
GROUP = 8
CHUNK = 5
PAD = 32
CORNER = 3 * LEVELS
SLOT = 80
EDGE = 32
OFFSET = (0, 50, 1, 51)
EDGES = 48 + 2 * PAD
LAND = 1e38
MIB = 1024 * 1024
VMEM = pl.BlockSpec(memory_space=pltpu.VMEM)
FAR = pl.BlockSpec(memory_space=pltpu.HBM)
SMEM = pl.BlockSpec(memory_space=pltpu.SMEM)


def iota(shape, dim):
    return lax.broadcasted_iota(jnp.int32, shape, dim)


def turn(x, shift, axis=1):
    shift = shift % x.shape[axis]
    return pltpu.roll(x, shift, axis) if shift else x


def terms(k, value, centre, side, vert):
    row, lane = iota((ROWS, COLS), 0), iota((ROWS, COLS), 1)
    y = value[k]
    east, west = side[0, k] * y, side[1, k] * y
    north, south = turn(side[2, k] * y, 1, 0), turn(side[3, k] * y, -1, 0)
    r = centre[k] * y
    r = r + jnp.where(lane > 0, turn(east, 1), 0.0) + jnp.where(lane < COLS - 1, turn(west, -1), 0.0)
    r = r + jnp.where(row > 0, north, 0.0) + jnp.where(row < ROWS - 1, south, 0.0)
    if k + 1 < LEVELS:
        r = r + vert[0, k + 1] * value[k + 1]
    if k > 0:
        r = r + vert[1, k - 1] * value[k - 1]
    return r, east, west, north, south


def outer(lane, last, first):
    return jnp.where(lane == COLS - 1, last, jnp.where(lane == 0, first, 0.0))


def scale_kernel(side, mask, scales):
    lane = iota((ROWS, COLS), 1)
    packed = jnp.zeros((ROWS, COLS), jnp.float32)
    for at in (16, 16 + PAD):
        scales[at + 24 : at + PAD, :] = jnp.zeros((8, COLS), jnp.float32)
    for k in range(LEVELS):
        m = mask[k].astype(jnp.float32)
        packed = packed + turn(m * outer(lane, side[0, k], side[1, k]), 2 * k + 1)
        scales[16 + k : 17 + k, :] = (m * side[2, k])[ROWS - 1 : ROWS]
        scales[16 + PAD + k : 17 + PAD + k, :] = (m * side[3, k])[0:1]
    scales[0:8, :], scales[8:16, :] = tight(packed)


def tight(packed):
    even = (iota((8, COLS), 1) & 1) == 0
    eastward = westward = jnp.zeros((8, COLS), jnp.float32)
    for g, offset in enumerate(OFFSET):
        rows = packed[8 * g : 8 * g + 8]
        eastward = eastward + turn(jnp.where(even, rows, 0.0), offset)
        westward = westward + turn(jnp.where(even, 0.0, rows), offset - 1)
    return eastward, westward


def forced(sources, misfit, cell, count, adjoint_far, start, hot, valued, adjoint, arrived):
    load = pltpu.make_async_copy(adjoint_far, adjoint, arrived)
    load.start()
    group = min(GROUP, sources)
    lane = iota((1, CAP), 1)
    for first in range(0, sources, group):
        for s in range(group):
            at = slice(s * CAP, (s + 1) * CAP)
            cells = cell[first + s : first + s + 1, :]
            v = jnp.where(lane < count[0, first + s], misfit[first + s : first + s + 1, :], 0.0)
            high = v.astype(jnp.bfloat16).astype(jnp.float32)
            low = v - high
            column = iota((COLS, CAP), 0) == (cells & (COLS - 1))
            for i, part in enumerate((high, low)):
                valued[i * COLS : (i + 1) * COLS, at] = jnp.where(column, part, 0.0).astype(jnp.bfloat16)
            place = cells >> 7
            for k in range(LEVELS):
                match = (iota((ROWS, CAP), 0) + k * ROWS) == place
                hot[k * ROWS : (k + 1) * ROWS, at] = jnp.where(match, 1.0, 0.0).astype(jnp.bfloat16)
        part = lax.dot_general(hot[...], valued[...], (((1,), (1,)), ((), ())), preferred_element_type=jnp.float32)
        part = part[:, 0:COLS] + part[:, COLS : 2 * COLS]
        if first == 0:
            load.wait()
        held = adjoint if first == 0 else start
        for k in range(LEVELS):
            start[k] = held[k] + part[k * ROWS : (k + 1) * ROWS, :]


def to_lanes(column, offset):
    level = iota((PAD, COLS), 0)
    spot = (iota((PAD, COLS), 1) == 2 * level + offset) & (level < LEVELS)
    return jnp.sum(jnp.where(spot, column, 0.0), axis=0, keepdims=True)


def to_rows(line, offset):
    level = iota((PAD, COLS), 0)
    spot = (iota((PAD, COLS), 1) == 2 * level + offset) & (level < LEVELS)
    return jnp.sum(jnp.where(spot, line, 0.0), axis=1, keepdims=True)


def spot_rows(first, last):
    row = iota((8, COLS), 0)
    return jnp.where(row == 0, first, 0.0) + jnp.where(row == 7, last, 0.0)


def ends(block):
    return block[:, COLS - 1 : COLS], block[:, 0:1]


def from_tiles(swapped, next_swapped, where, rows):
    upward = where[4] == 0
    first, second = swapped[rows, :], next_swapped[rows, :]
    return jnp.where(upward, second, first), jnp.where(upward, first, second)


def chunk(source, target, semaphores, i):
    levels = pl.ds(i * CHUNK, CHUNK)
    return pltpu.make_async_copy(source.at[levels], target.at[levels], semaphores.at[i])


def first_kernel(sources, misfit, cell, count, adjoint_far, where, scales, side, centre, vert, mask, part_far, swap, next_swap, edges, slots, hot, valued, adjoint, held, part, up, down, tips, picked, next_picked, sent, posted, arrived):
    forced(sources, misfit, cell, count, adjoint_far, held, hot, valued, adjoint, arrived)
    for ref in (up, down):
        ref[CORNER + 1 : SLOT, :] = jnp.zeros((SLOT - CORNER - 1, COLS), jnp.float32)
    for i in range(2):
        tips[i * PAD + 24 : (i + 1) * PAD, :] = jnp.zeros((8, COLS), jnp.float32)
    lane = iota((ROWS, COLS), 1)
    packed = [jnp.zeros((ROWS, COLS), jnp.float32)] * 2
    for k in range(LEVELS):
        r, east, west, north, south = terms(k, held, centre, side, vert)
        part[k] = jnp.where(mask[k] == 0, LAND, r)
        sides = outer(lane, east, west)
        for i, (ref, leaving, at) in enumerate(((up, north[0:1], ROWS - 1), (down, south[ROWS - 1 : ROWS], 0))):
            ref[k : k + 1, :] = leaving
            ref[LEVELS + k : LEVELS + k + 1, :] = r[at : at + 1]
            tips[i * PAD + k : i * PAD + k + 1, :] = sides[at : at + 1]
        packed = [p + turn(x, 2 * k + 1) for p, x in zip(packed, (sides, outer(lane, r, r)))]
        if (k + 1) % CHUNK == 0:
            chunk(part, part_far, sent, k // CHUNK).start()
    for i, ref in enumerate((up, down)):
        ref[2 * LEVELS : 3 * LEVELS, :] = scales[16 + i * PAD : 16 + i * PAD + LEVELS, :]
        east, west = ends(tips[i * PAD : (i + 1) * PAD, :])
        ref[CORNER : CORNER + 1, :] = to_lanes(east, OFFSET[0]) + to_lanes(west, OFFSET[1])
    spread = [pltpu.make_async_copy(up, slots.at[s], posted.at[s]) for s in range(slots.shape[0])]
    for copy in spread:
        copy.start()
    upward = where[4] == 0
    picked[...] = jnp.where(upward, up[...], down[...])
    next_picked[...] = jnp.where(upward, down[...], up[...])
    spread.append(pltpu.make_async_copy(picked, swap, posted.at[slots.shape[0]]))
    spread.append(pltpu.make_async_copy(next_picked, next_swap, posted.at[slots.shape[0] + 1]))
    for copy in spread[-2:]:
        copy.start()
    for i, p in enumerate(packed):
        edges[8 * i : 8 * i + 8, :], edges[24 + 8 * i : 32 + 8 * i, :] = tight(p)
    edges[16:24, :] = scales[0:8, :]
    edges[40:48, :] = scales[8:16, :]
    edges[48 : 48 + PAD, :] = down[0:PAD, :]
    edges[48 + PAD : EDGES, :] = up[0:PAD, :]
    for i in range(LEVELS // CHUNK):
        chunk(part, part_far, sent, i).wait()
    for copy in spread:
        copy.wait()


def corner_kernel(swapped, next_swapped, edges, where, swap, next_swap):
    low, high = from_tiles(swapped, next_swapped, where, slice(0, PAD))
    low_tips, high_tips = from_tiles(swapped, next_swapped, where, slice(CORNER, CORNER + 1))
    low_last, low_first = ends(low)
    high_last, high_first = ends(high)
    eastern = iota((1, COLS), 1) < OFFSET[1]
    corners = low_tips + turn(jnp.where(eastern, high_tips, 0.0), OFFSET[3] - OFFSET[0])
    corners = corners + turn(jnp.where(eastern, 0.0, high_tips), OFFSET[2] - OFFSET[1])
    eastward = spot_rows(to_lanes(low_last, OFFSET[0]), to_lanes(high_last, OFFSET[3]))
    westward = spot_rows(to_lanes(low_first, OFFSET[0]), to_lanes(high_first, OFFSET[3]))
    to_east = where[5] == 0
    for ref, chosen in ((swap, to_east), (next_swap, jnp.logical_not(to_east))):
        ref[0:24, :] = jnp.where(chosen, edges[0:24, :], edges[24:48, :])
        ref[8:16, :] += jnp.where(chosen, eastward, westward)
        ref[24:EDGE, :] = jnp.where(iota((EDGE - 24, COLS), 0) == 0, corners, 0.0)


def second_kernel(swapped, next_swapped, beside, next_beside, edges, got, partner, flip, where, part_far, side, centre, vert, out, held, part, result, lines, near_sides, far_sides, west_side, east_side, loaded, sent):
    for i in range(LEVELS // CHUNK):
        chunk(part_far, part, loaded, i).start()
    sources = got.shape[0]
    below_near, above_near = from_tiles(swapped, next_swapped, where, slice(0, PAD))
    below_part, above_part = from_tiles(swapped, next_swapped, where, slice(LEVELS, LEVELS + PAD))
    below_scale, above_scale = (
        turn(rows, SLOT - PAD - 2 * LEVELS, 0)
        for rows in from_tiles(swapped, next_swapped, where, slice(SLOT - PAD, SLOT))
    )
    sum_low = below_part + edges[48 : 48 + PAD, :]
    sum_high = above_part + edges[48 + PAD : EDGES, :]
    even_column = where[5] == 0
    west_side[...] = jnp.where(even_column, next_beside[...], beside[...])
    east_side[...] = jnp.where(even_column, beside[...], next_beside[...])
    column, top, left, right = where[0], where[1], where[2], where[3]
    at_top = top == 1

    def comes_from(target):
        source = 0
        for s in range(sources):
            source = jnp.where(partner[s] == target, s, source)
        return source

    def turned(rows, source):
        back = COLS - 1 - iota((PAD, COLS), 1)
        return jnp.where(flip[source] == 1, jnp.take_along_axis(rows, back, axis=1), rows)

    level_lane = iota((PAD, COLS), 1)
    source = comes_from(column)
    earlier = comes_from(source)
    before = jnp.where(source == 0, sources - 1, source - 1)
    after = jnp.where(source == sources - 1, 0, source + 1)
    corner_left = west_side[24:25, :]
    corner_right = east_side[24:25, :]
    sum_low = sum_low + jnp.where(level_lane == 0, to_rows(corner_left, OFFSET[0]), 0.0)
    sum_low = sum_low + jnp.where(level_lane == COLS - 1, to_rows(corner_right, OFFSET[1]), 0.0)
    sum_high = sum_high + jnp.where(level_lane == 0, to_rows(corner_left, OFFSET[3]), 0.0)
    sum_high = sum_high + jnp.where(level_lane == COLS - 1, to_rows(corner_right, OFFSET[2]), 0.0)
    fold_first = turned(got[source, 0:PAD, :], source)
    sum_fold = got[source, LEVELS : LEVELS + PAD, :] + turned(got[earlier, 0:PAD, :], earlier)
    cross_west = to_rows(got[before, CORNER : CORNER + 1, :], OFFSET[0])
    cross_east = to_rows(got[after, CORNER : CORNER + 1, :], OFFSET[1])
    sum_fold = sum_fold + jnp.where(level_lane == 0, cross_west, 0.0) + jnp.where(level_lane == COLS - 1, cross_east, 0.0)
    fold_second = turned(turn(got[source, SLOT - PAD : SLOT, :], SLOT - PAD - 2 * LEVELS, 0) * sum_fold, source)
    lines[0:PAD, :] = jnp.where(at_top, fold_first, above_near)
    lines[PAD : 2 * PAD, :] = below_scale * sum_low
    lines[2 * PAD : 3 * PAD, :] = jnp.where(at_top, fold_second, above_scale * sum_high)
    lines[3 * PAD : 4 * PAD, :] = below_near
    from_left = comes_from(left)
    from_right = comes_from(right)
    fold_left = turned(got[from_left, 0:PAD, :], from_left)[:, COLS - 1 : COLS]
    fold_right = turned(got[from_right, 0:PAD, :], from_right)[:, 0:1]
    fold_left = jnp.where(at_top, to_lanes(fold_left, OFFSET[3]), 0.0)
    fold_right = jnp.where(at_top, to_lanes(fold_right, OFFSET[3]), 0.0)
    near_left = west_side[0:8, :]
    near_right = east_side[0:8, :]
    next_left = west_side[16:24, :] * (west_side[8:16, :] + edges[24:32, :] + spot_rows(0.0, fold_left))
    next_right = east_side[16:24, :] * (east_side[8:16, :] + edges[0:8, :] + spot_rows(0.0, fold_right))
    even = (iota((8, COLS), 1) & 1) == 0
    for ref, from_west, from_east in ((near_sides, near_left, near_right), (far_sides, next_left, next_right)):
        for g, offset in enumerate(OFFSET):
            ref[8 * g : 8 * g + 8, :] = jnp.where(even, turn(from_west, -offset), turn(from_east, -offset - 1))

    row, lane = iota((ROWS, COLS), 0), iota((ROWS, COLS), 1)

    def joined(k, r, sides, first, last):
        r = r + jnp.where((lane == 0) | (lane == COLS - 1), turn(sides[...], -2 * k), 0.0)
        r = r + jnp.where(row == 0, first, 0.0) + jnp.where(row == ROWS - 1, last, 0.0)
        return jnp.where(part[k] == LAND, 0.0, r)

    for k in range(LEVELS):
        if k % CHUNK == 0:
            chunk(part_far, part, loaded, k // CHUNK).wait()
        held[k] = joined(k, part[k], near_sides, lines[3 * PAD + k : 3 * PAD + k + 1, :], lines[k : k + 1, :])
    for k in range(LEVELS):
        r = terms(k, held, centre, side, vert)[0]
        result[k] = joined(k, r, far_sides, lines[PAD + k : PAD + k + 1, :], lines[2 * PAD + k : 2 * PAD + k + 1, :])
        if (k + 1) % CHUNK == 0:
            chunk(result, out, sent, k // CHUNK).start()
    for i in range(LEVELS // CHUNK):
        chunk(result, out, sent, i).wait()


def body(adjoint_in, centre, side_coeff, vert_coeff, land_mask, obs_misfit, obs_cell, obs_count, fold_partner, fold_flip):
    sources = obs_misfit.shape[2]
    tiles = lax.axis_size("tile")
    column, tile_row = lax.axis_index("col"), lax.axis_index("tile")
    where = jnp.stack(
        [
            column,
            (tile_row == tiles - 1).astype(jnp.int32),
            jnp.where(column == 0, sources - 1, column - 1),
            jnp.where(column == sources - 1, 0, column + 1),
            tile_row & 1,
            column & 1,
        ]
    )
    received = lax.all_to_all(obs_misfit, "col", split_axis=2, concat_axis=1, tiled=True)
    f32 = jnp.float32
    tile = jax.ShapeDtypeStruct((LEVELS, ROWS, COLS), f32)
    lines = pltpu.HBM((SLOT, COLS), f32)
    field = pltpu.VMEM((LEVELS, ROWS, COLS), f32)
    chunks = pltpu.SemaphoreType.DMA((LEVELS // CHUNK,))
    group = min(GROUP, sources)
    small = sources <= GROUP
    ahead = pl.CostEstimate(flops=10**10, bytes_accessed=2 * 10**8, transcendentals=0)
    scales = pl.pallas_call(
        scale_kernel,
        out_shape=jax.ShapeDtypeStruct((16 + 2 * PAD, COLS), f32),
        in_specs=[VMEM, VMEM],
        out_specs=VMEM,
        compiler_params=pltpu.CompilerParams(vmem_limit_bytes=4 * MIB),
        cost_estimate=ahead,
        name="edge_scales",
    )(side_coeff, land_mask)
    part, swap, next_swap, edges, slots = pl.pallas_call(
        functools.partial(first_kernel, sources),
        out_shape=(tile, lines, lines, jax.ShapeDtypeStruct((EDGES, COLS), f32), pltpu.HBM((sources, SLOT, COLS), f32)),
        in_specs=[VMEM, VMEM, SMEM, FAR, SMEM] + [VMEM] * 5,
        out_specs=(FAR, FAR, FAR, VMEM, FAR),
        scratch_shapes=[
            pltpu.VMEM((LEVELS * ROWS, group * CAP), jnp.bfloat16),
            pltpu.VMEM((2 * COLS, group * CAP), jnp.bfloat16),
            field,
            field,
            field,
            pltpu.VMEM((SLOT, COLS), f32),
            pltpu.VMEM((SLOT, COLS), f32),
            pltpu.VMEM((2 * PAD, COLS), f32),
            pltpu.VMEM((SLOT, COLS), f32),
            pltpu.VMEM((SLOT, COLS), f32),
            chunks,
            pltpu.SemaphoreType.DMA((sources + 2,)),
            pltpu.SemaphoreType.DMA,
        ],
        compiler_params=pltpu.CompilerParams(vmem_limit_bytes=(10 if small else 24) * MIB),
        name="first_step",
    )(
        received.reshape(sources, CAP),
        obs_cell.reshape(sources, CAP),
        obs_count.reshape(1, sources),
        pltpu.with_memory_space_constraint(adjoint_in, pltpu.HBM),
        where,
        scales,
        side_coeff,
        centre,
        vert_coeff,
        land_mask,
    )
    got = lax.all_to_all(slots, "col", split_axis=0, concat_axis=0, tiled=True)
    next_swapped = lax.ppermute(next_swap, "tile", swaps(1, tiles - 1))
    swapped = lax.ppermute(swap, "tile", swaps(0, tiles))
    edge = jax.ShapeDtypeStruct((EDGE, COLS), f32)
    beside, next_beside = pl.pallas_call(
        corner_kernel,
        out_shape=(edge, edge),
        in_specs=[VMEM, VMEM, VMEM, SMEM],
        out_specs=(VMEM, VMEM),
        compiler_params=pltpu.CompilerParams(vmem_limit_bytes=4 * MIB),
        cost_estimate=pl.CostEstimate(flops=10**6, bytes_accessed=4 * 10**6, transcendentals=0),
        name="corners",
    )(swapped, next_swapped, edges, where)
    round_trip = [(sources - 1, 0), (0, sources - 1)]
    next_beside = lax.ppermute(next_beside, "col", swaps(1, sources - 1) + round_trip)
    beside = lax.ppermute(beside, "col", swaps(0, sources))
    return pl.pallas_call(
        second_kernel,
        out_shape=tile,
        in_specs=[VMEM] * 6 + [SMEM] * 3 + [FAR] + [VMEM] * 3,
        out_specs=FAR,
        input_output_aliases={9: 0},
        scratch_shapes=[
            field,
            field,
            field,
            pltpu.VMEM((4 * PAD, COLS), f32),
            pltpu.VMEM((ROWS, COLS), f32),
            pltpu.VMEM((ROWS, COLS), f32),
            pltpu.VMEM((EDGE, COLS), f32),
            pltpu.VMEM((EDGE, COLS), f32),
            chunks,
            chunks,
        ],
        compiler_params=pltpu.CompilerParams(vmem_limit_bytes=(8 if small else 24) * MIB),
        name="second_step",
    )(
        swapped,
        next_swapped,
        beside,
        next_beside,
        edges,
        got,
        fold_partner,
        fold_flip,
        where,
        part,
        side_coeff,
        centre,
        vert_coeff,
    )


def swaps(first, end):
    return [pair for i in range(first, end - 1, 2) for pair in ((i, i + 1), (i + 1, i))]


def solution(mesh):
    in_specs = (
        P(None, "tile", "col"),
        P(None, "tile", "col"),
        P(None, None, "tile", "col"),
        P(None, None, "tile", "col"),
        P(None, "tile", "col"),
        P("tile", "col", None, None),
        P("tile", "col", None, None),
        P("tile", "col", None),
        P(),
        P(),
    )
    out_specs = P(None, "tile", "col")
    return jax.shard_map(body, mesh=mesh, in_specs=in_specs, out_specs=out_specs, check_vma=False)
```

```python
import functools

import jax
import jax.numpy as jnp
from jax import lax
from jax.experimental import pallas as pl
from jax.experimental.pallas import tpu as pltpu
from jax.sharding import PartitionSpec as P

LEVELS = 25
ROWS = 32
COLS = 128
CAP = 128
GROUP = 8
CHUNK = 5
PAD = 32
CORNER = 3 * LEVELS
SLOT = 80
EDGE = 32
OFFSET = (0, 50, 1, 51)
EDGES = 48 + 2 * PAD
LAND = 1e38
MIB = 1024 * 1024
VMEM = pl.BlockSpec(memory_space=pltpu.VMEM)
FAR = pl.BlockSpec(memory_space=pltpu.HBM)
SMEM = pl.BlockSpec(memory_space=pltpu.SMEM)


def iota(shape, dim):
    return lax.broadcasted_iota(jnp.int32, shape, dim)


def turn(x, shift, axis=1):
    shift = shift % x.shape[axis]
    return pltpu.roll(x, shift, axis) if shift else x


def terms(k, value, centre, side, vert):
    row, lane = iota((ROWS, COLS), 0), iota((ROWS, COLS), 1)
    y = value[k]
    east, west = side[0, k] * y, side[1, k] * y
    north, south = turn(side[2, k] * y, 1, 0), turn(side[3, k] * y, -1, 0)
    r = centre[k] * y
    r = r + jnp.where(lane > 0, turn(east, 1), 0.0) + jnp.where(lane < COLS - 1, turn(west, -1), 0.0)
    r = r + jnp.where(row > 0, north, 0.0) + jnp.where(row < ROWS - 1, south, 0.0)
    if k + 1 < LEVELS:
        r = r + vert[0, k + 1] * value[k + 1]
    if k > 0:
        r = r + vert[1, k - 1] * value[k - 1]
    return r, east, west, north, south


def outer(lane, last, first):
    return jnp.where(lane == COLS - 1, last, jnp.where(lane == 0, first, 0.0))


def scale_kernel(side, mask, scales):
    lane = iota((ROWS, COLS), 1)
    packed = jnp.zeros((ROWS, COLS), jnp.float32)
    for at in (16, 16 + PAD):
        scales[at + 24 : at + PAD, :] = jnp.zeros((8, COLS), jnp.float32)
    for k in range(LEVELS):
        m = mask[k].astype(jnp.float32)
        packed = packed + turn(m * outer(lane, side[0, k], side[1, k]), 2 * k + 1)
        scales[16 + k : 17 + k, :] = (m * side[2, k])[ROWS - 1 : ROWS]
        scales[16 + PAD + k : 17 + PAD + k, :] = (m * side[3, k])[0:1]
    scales[0:8, :], scales[8:16, :] = tight(packed)


def tight(packed):
    even = (iota((8, COLS), 1) & 1) == 0
    eastward = westward = jnp.zeros((8, COLS), jnp.float32)
    for g, offset in enumerate(OFFSET):
        rows = packed[8 * g : 8 * g + 8]
        eastward = eastward + turn(jnp.where(even, rows, 0.0), offset)
        westward = westward + turn(jnp.where(even, 0.0, rows), offset - 1)
    return eastward, westward


def forced(sources, misfit, cell, count, adjoint_far, start, hot, valued, adjoint, arrived):
    load = pltpu.make_async_copy(adjoint_far, adjoint, arrived)
    load.start()
    group = min(GROUP, sources)
    lane = iota((1, CAP), 1)
    for first in range(0, sources, group):
        for s in range(group):
            at = slice(s * CAP, (s + 1) * CAP)
            cells = cell[first + s : first + s + 1, :]
            v = jnp.where(lane < count[0, first + s], misfit[first + s : first + s + 1, :], 0.0)
            high = v.astype(jnp.bfloat16).astype(jnp.float32)
            low = v - high
            column = iota((COLS, CAP), 0) == (cells & (COLS - 1))
            for i, part in enumerate((high, low)):
                valued[i * COLS : (i + 1) * COLS, at] = jnp.where(column, part, 0.0).astype(jnp.bfloat16)
            place = cells >> 7
            for k in range(LEVELS):
                match = (iota((ROWS, CAP), 0) + k * ROWS) == place
                hot[k * ROWS : (k + 1) * ROWS, at] = jnp.where(match, 1.0, 0.0).astype(jnp.bfloat16)
        part = lax.dot_general(hot[...], valued[...], (((1,), (1,)), ((), ())), preferred_element_type=jnp.float32)
        part = part[:, 0:COLS] + part[:, COLS : 2 * COLS]
        if first == 0:
            load.wait()
        held = adjoint if first == 0 else start
        for k in range(LEVELS):
            start[k] = held[k] + part[k * ROWS : (k + 1) * ROWS, :]


def to_lanes(column, offset):
    level = iota((PAD, COLS), 0)
    spot = (iota((PAD, COLS), 1) == 2 * level + offset) & (level < LEVELS)
    return jnp.sum(jnp.where(spot, column, 0.0), axis=0, keepdims=True)


def to_rows(line, offset):
    level = iota((PAD, COLS), 0)
    spot = (iota((PAD, COLS), 1) == 2 * level + offset) & (level < LEVELS)
    return jnp.sum(jnp.where(spot, line, 0.0), axis=1, keepdims=True)


def spot_rows(first, last):
    row = iota((8, COLS), 0)
    return jnp.where(row == 0, first, 0.0) + jnp.where(row == 7, last, 0.0)


def ends(block):
    return block[:, COLS - 1 : COLS], block[:, 0:1]


def from_tiles(swapped, next_swapped, where, rows):
    upward = where[4] == 0
    first, second = swapped[rows, :], next_swapped[rows, :]
    return jnp.where(upward, second, first), jnp.where(upward, first, second)


def chunk(source, target, semaphores, i):
    levels = pl.ds(i * CHUNK, CHUNK)
    return pltpu.make_async_copy(source.at[levels], target.at[levels], semaphores.at[i])


def first_kernel(sources, misfit, cell, count, adjoint_far, where, scales, side, centre, vert, mask, part, swap, next_swap, edges, slots, hot, valued, adjoint, held, up, down, tips, picked, next_picked, posted, arrived):
    forced(sources, misfit, cell, count, adjoint_far, held, hot, valued, adjoint, arrived)
    for ref in (up, down):
        ref[CORNER + 1 : SLOT, :] = jnp.zeros((SLOT - CORNER - 1, COLS), jnp.float32)
    for i in range(2):
        tips[i * PAD + 24 : (i + 1) * PAD, :] = jnp.zeros((8, COLS), jnp.float32)
    lane = iota((ROWS, COLS), 1)
    packed = [jnp.zeros((ROWS, COLS), jnp.float32)] * 2
    for k in range(LEVELS):
        r, east, west, north, south = terms(k, held, centre, side, vert)
        part[k] = jnp.where(mask[k] == 0, LAND, r)
        sides = outer(lane, east, west)
        for i, (ref, leaving, at) in enumerate(((up, north[0:1], ROWS - 1), (down, south[ROWS - 1 : ROWS], 0))):
            ref[k : k + 1, :] = leaving
            ref[LEVELS + k : LEVELS + k + 1, :] = r[at : at + 1]
            tips[i * PAD + k : i * PAD + k + 1, :] = sides[at : at + 1]
        packed = [p + turn(x, 2 * k + 1) for p, x in zip(packed, (sides, outer(lane, r, r)))]
    for i, ref in enumerate((up, down)):
        ref[2 * LEVELS : 3 * LEVELS, :] = scales[16 + i * PAD : 16 + i * PAD + LEVELS, :]
        east, west = ends(tips[i * PAD : (i + 1) * PAD, :])
        ref[CORNER : CORNER + 1, :] = to_lanes(east, OFFSET[0]) + to_lanes(west, OFFSET[1])
    spread = [pltpu.make_async_copy(up, slots.at[s], posted.at[s]) for s in range(slots.shape[0])]
    for copy in spread:
        copy.start()
    upward = where[4] == 0
    picked[...] = jnp.where(upward, up[...], down[...])
    next_picked[...] = jnp.where(upward, down[...], up[...])
    spread.append(pltpu.make_async_copy(picked, swap, posted.at[slots.shape[0]]))
    spread.append(pltpu.make_async_copy(next_picked, next_swap, posted.at[slots.shape[0] + 1]))
    for copy in spread[-2:]:
        copy.start()
    for i, p in enumerate(packed):
        edges[8 * i : 8 * i + 8, :], edges[24 + 8 * i : 32 + 8 * i, :] = tight(p)
    edges[16:24, :] = scales[0:8, :]
    edges[40:48, :] = scales[8:16, :]
    edges[48 : 48 + PAD, :] = down[0:PAD, :]
    edges[48 + PAD : EDGES, :] = up[0:PAD, :]
    for copy in spread:
        copy.wait()


def corner_kernel(swapped, next_swapped, edges, where, swap, next_swap):
    low, high = from_tiles(swapped, next_swapped, where, slice(0, PAD))
    low_tips, high_tips = from_tiles(swapped, next_swapped, where, slice(CORNER, CORNER + 1))
    low_last, low_first = ends(low)
    high_last, high_first = ends(high)
    eastern = iota((1, COLS), 1) < OFFSET[1]
    corners = low_tips + turn(jnp.where(eastern, high_tips, 0.0), OFFSET[3] - OFFSET[0])
    corners = corners + turn(jnp.where(eastern, 0.0, high_tips), OFFSET[2] - OFFSET[1])
    eastward = spot_rows(to_lanes(low_last, OFFSET[0]), to_lanes(high_last, OFFSET[3]))
    westward = spot_rows(to_lanes(low_first, OFFSET[0]), to_lanes(high_first, OFFSET[3]))
    to_east = where[5] == 0
    for ref, chosen in ((swap, to_east), (next_swap, jnp.logical_not(to_east))):
        ref[0:24, :] = jnp.where(chosen, edges[0:24, :], edges[24:48, :])
        ref[8:16, :] += jnp.where(chosen, eastward, westward)
        ref[24:EDGE, :] = jnp.where(iota((EDGE - 24, COLS), 0) == 0, corners, 0.0)


def second_kernel(swapped, next_swapped, beside, next_beside, edges, got_far, partner, flip, where, part, side, centre, vert, out, held, result, lines, near_sides, far_sides, west_side, east_side, got, gathered, sent):
    gather = pltpu.make_async_copy(got_far, got, gathered)
    gather.start()
    sources = got.shape[0]
    below_near, above_near = from_tiles(swapped, next_swapped, where, slice(0, PAD))
    below_part, above_part = from_tiles(swapped, next_swapped, where, slice(LEVELS, LEVELS + PAD))
    below_scale, above_scale = (
        turn(rows, SLOT - PAD - 2 * LEVELS, 0)
        for rows in from_tiles(swapped, next_swapped, where, slice(SLOT - PAD, SLOT))
    )
    sum_low = below_part + edges[48 : 48 + PAD, :]
    sum_high = above_part + edges[48 + PAD : EDGES, :]
    even_column = where[5] == 0
    west_side[...] = jnp.where(even_column, next_beside[...], beside[...])
    east_side[...] = jnp.where(even_column, beside[...], next_beside[...])
    column, top, left, right = where[0], where[1], where[2], where[3]
    at_top = top == 1

    def comes_from(target):
        source = 0
        for s in range(sources):
            source = jnp.where(partner[s] == target, s, source)
        return source

    def turned(rows, source):
        back = COLS - 1 - iota((PAD, COLS), 1)
        return jnp.where(flip[source] == 1, jnp.take_along_axis(rows, back, axis=1), rows)

    lines[0:PAD, :] = jnp.where(at_top, 0.0, above_near)
    lines[3 * PAD : 4 * PAD, :] = below_near

    def spread_sides(ref, from_west, from_east):
        even = (iota((8, COLS), 1) & 1) == 0
        for g, offset in enumerate(OFFSET):
            ref[8 * g : 8 * g + 8, :] = jnp.where(even, turn(from_west, -offset), turn(from_east, -offset - 1))

    spread_sides(near_sides, west_side[0:8, :], east_side[0:8, :])
    row, lane = iota((ROWS, COLS), 0), iota((ROWS, COLS), 1)

    def joined(k, r, sides, first, last):
        r = r + jnp.where((lane == 0) | (lane == COLS - 1), turn(sides[...], -2 * k), 0.0)
        r = r + jnp.where(row == 0, first, 0.0) + jnp.where(row == ROWS - 1, last, 0.0)
        return jnp.where(part[k] == LAND, 0.0, r)

    for k in range(LEVELS):
        held[k] = joined(k, part[k], near_sides, lines[3 * PAD + k : 3 * PAD + k + 1, :], lines[k : k + 1, :])
    gather.wait()
    level_lane = iota((PAD, COLS), 1)
    source = comes_from(column)
    earlier = comes_from(source)
    before = jnp.where(source == 0, sources - 1, source - 1)
    after = jnp.where(source == sources - 1, 0, source + 1)
    corner_left = west_side[24:25, :]
    corner_right = east_side[24:25, :]
    sum_low = sum_low + jnp.where(level_lane == 0, to_rows(corner_left, OFFSET[0]), 0.0)
    sum_low = sum_low + jnp.where(level_lane == COLS - 1, to_rows(corner_right, OFFSET[1]), 0.0)
    sum_high = sum_high + jnp.where(level_lane == 0, to_rows(corner_left, OFFSET[3]), 0.0)
    sum_high = sum_high + jnp.where(level_lane == COLS - 1, to_rows(corner_right, OFFSET[2]), 0.0)
    fold_first = turned(got[source, 0:PAD, :], source)
    sum_fold = got[source, LEVELS : LEVELS + PAD, :] + turned(got[earlier, 0:PAD, :], earlier)
    cross_west = to_rows(got[before, CORNER : CORNER + 1, :], OFFSET[0])
    cross_east = to_rows(got[after, CORNER : CORNER + 1, :], OFFSET[1])
    sum_fold = sum_fold + jnp.where(level_lane == 0, cross_west, 0.0) + jnp.where(level_lane == COLS - 1, cross_east, 0.0)
    fold_second = turned(turn(got[source, SLOT - PAD : SLOT, :], SLOT - PAD - 2 * LEVELS, 0) * sum_fold, source)
    fold_first = jnp.where(at_top, fold_first, 0.0)
    for k in range(LEVELS):
        last = part[k, ROWS - 1 : ROWS, :]
        held[k, ROWS - 1 : ROWS, :] += jnp.where(last == LAND, 0.0, fold_first[k : k + 1, :])
    lines[PAD : 2 * PAD, :] = below_scale * sum_low
    lines[2 * PAD : 3 * PAD, :] = jnp.where(at_top, fold_second, above_scale * sum_high)
    from_left = comes_from(left)
    from_right = comes_from(right)
    fold_left = turned(got[from_left, 0:PAD, :], from_left)[:, COLS - 1 : COLS]
    fold_right = turned(got[from_right, 0:PAD, :], from_right)[:, 0:1]
    fold_left = jnp.where(at_top, to_lanes(fold_left, OFFSET[3]), 0.0)
    fold_right = jnp.where(at_top, to_lanes(fold_right, OFFSET[3]), 0.0)
    next_left = west_side[16:24, :] * (west_side[8:16, :] + edges[24:32, :] + spot_rows(0.0, fold_left))
    next_right = east_side[16:24, :] * (east_side[8:16, :] + edges[0:8, :] + spot_rows(0.0, fold_right))
    spread_sides(far_sides, next_left, next_right)
    for k in range(LEVELS):
        r = terms(k, held, centre, side, vert)[0]
        result[k] = joined(k, r, far_sides, lines[PAD + k : PAD + k + 1, :], lines[2 * PAD + k : 2 * PAD + k + 1, :])
        if (k + 1) % CHUNK == 0:
            chunk(result, out, sent, k // CHUNK).start()
    for i in range(LEVELS // CHUNK):
        chunk(result, out, sent, i).wait()


def body(adjoint_in, centre, side_coeff, vert_coeff, land_mask, obs_misfit, obs_cell, obs_count, fold_partner, fold_flip):
    sources = obs_misfit.shape[2]
    tiles = lax.axis_size("tile")
    column, tile_row = lax.axis_index("col"), lax.axis_index("tile")
    where = jnp.stack(
        [
            column,
            (tile_row == tiles - 1).astype(jnp.int32),
            jnp.where(column == 0, sources - 1, column - 1),
            jnp.where(column == sources - 1, 0, column + 1),
            tile_row & 1,
            column & 1,
        ]
    )
    received = lax.all_to_all(obs_misfit, "col", split_axis=2, concat_axis=1, tiled=True)
    f32 = jnp.float32
    tile = jax.ShapeDtypeStruct((LEVELS, ROWS, COLS), f32)
    lines = pltpu.HBM((SLOT, COLS), f32)
    field = pltpu.VMEM((LEVELS, ROWS, COLS), f32)
    chunks = pltpu.SemaphoreType.DMA((LEVELS // CHUNK,))
    group = min(GROUP, sources)
    small = sources <= GROUP
    ahead = pl.CostEstimate(flops=10**10, bytes_accessed=2 * 10**8, transcendentals=0)
    scales = pl.pallas_call(
        scale_kernel,
        out_shape=jax.ShapeDtypeStruct((16 + 2 * PAD, COLS), f32),
        in_specs=[VMEM, VMEM],
        out_specs=VMEM,
        compiler_params=pltpu.CompilerParams(vmem_limit_bytes=4 * MIB),
        cost_estimate=ahead,
        name="edge_scales",
    )(side_coeff, land_mask)
    part, swap, next_swap, edges, slots = pl.pallas_call(
        functools.partial(first_kernel, sources),
        out_shape=(tile, lines, lines, jax.ShapeDtypeStruct((EDGES, COLS), f32), pltpu.HBM((sources, SLOT, COLS), f32)),
        in_specs=[VMEM, VMEM, SMEM, FAR, SMEM] + [VMEM] * 5,
        out_specs=(VMEM, FAR, FAR, VMEM, FAR),
        scratch_shapes=[
            pltpu.VMEM((LEVELS * ROWS, group * CAP), jnp.bfloat16),
            pltpu.VMEM((2 * COLS, group * CAP), jnp.bfloat16),
            field,
            field,
            pltpu.VMEM((SLOT, COLS), f32),
            pltpu.VMEM((SLOT, COLS), f32),
            pltpu.VMEM((2 * PAD, COLS), f32),
            pltpu.VMEM((SLOT, COLS), f32),
            pltpu.VMEM((SLOT, COLS), f32),
            pltpu.SemaphoreType.DMA((sources + 2,)),
            pltpu.SemaphoreType.DMA,
        ],
        compiler_params=pltpu.CompilerParams(vmem_limit_bytes=(10 if small else 24) * MIB),
        name="first_step",
    )(
        received.reshape(sources, CAP),
        obs_cell.reshape(sources, CAP),
        obs_count.reshape(1, sources),
        pltpu.with_memory_space_constraint(adjoint_in, pltpu.HBM),
        where,
        scales,
        side_coeff,
        centre,
        vert_coeff,
        land_mask,
    )
    got = lax.all_to_all(slots, "col", split_axis=0, concat_axis=0, tiled=True)
    next_swapped = lax.ppermute(next_swap, "tile", swaps(1, tiles - 1))
    swapped = lax.ppermute(swap, "tile", swaps(0, tiles))
    edge = jax.ShapeDtypeStruct((EDGE, COLS), f32)
    beside, next_beside = pl.pallas_call(
        corner_kernel,
        out_shape=(edge, edge),
        in_specs=[VMEM, VMEM, VMEM, SMEM],
        out_specs=(VMEM, VMEM),
        compiler_params=pltpu.CompilerParams(vmem_limit_bytes=4 * MIB),
        cost_estimate=pl.CostEstimate(flops=10**6, bytes_accessed=4 * 10**6, transcendentals=0),
        name="corners",
    )(swapped, next_swapped, edges, where)
    round_trip = [(sources - 1, 0), (0, sources - 1)]
    next_beside = lax.ppermute(next_beside, "col", swaps(1, sources - 1) + round_trip)
    beside = lax.ppermute(beside, "col", swaps(0, sources))
    return pl.pallas_call(
        second_kernel,
        out_shape=tile,
        in_specs=[VMEM] * 5 + [FAR] + [SMEM] * 3 + [VMEM] * 4,
        out_specs=FAR,
        scratch_shapes=[
            field,
            field,
            pltpu.VMEM((4 * PAD, COLS), f32),
            pltpu.VMEM((ROWS, COLS), f32),
            pltpu.VMEM((ROWS, COLS), f32),
            pltpu.VMEM((EDGE, COLS), f32),
            pltpu.VMEM((EDGE, COLS), f32),
            pltpu.VMEM((sources, SLOT, COLS), f32),
            pltpu.SemaphoreType.DMA,
            chunks,
        ],
        compiler_params=pltpu.CompilerParams(vmem_limit_bytes=(8 if small else 24) * MIB),
        name="second_step",
    )(
        swapped,
        next_swapped,
        beside,
        next_beside,
        edges,
        pltpu.with_memory_space_constraint(got, pltpu.HBM),
        fold_partner,
        fold_flip,
        where,
        part,
        side_coeff,
        centre,
        vert_coeff,
    )


def swaps(first, end):
    return [pair for i in range(first, end - 1, 2) for pair in ((i, i + 1), (i + 1, i))]


def solution(mesh):
    in_specs = (
        P(None, "tile", "col"),
        P(None, "tile", "col"),
        P(None, None, "tile", "col"),
        P(None, None, "tile", "col"),
        P(None, "tile", "col"),
        P("tile", "col", None, None),
        P("tile", "col", None, None),
        P("tile", "col", None),
        P(),
        P(),
    )
    out_specs = P(None, "tile", "col")
    return jax.shard_map(body, mesh=mesh, in_specs=in_specs, out_specs=out_specs, check_vma=False)
```

```python
import functools

import jax
import jax.numpy as jnp
from jax import lax
from jax.experimental import pallas as pl
from jax.experimental.pallas import tpu as pltpu
from jax.sharding import PartitionSpec as P

LEVELS = 25
ROWS = 32
COLS = 128
CAP = 128
GROUP = 8
CHUNK = 5
PAD = 32
CORNER = 3 * LEVELS
SLOT = 80
EDGE = 32
OFFSET = (0, 50, 1, 51)
EDGES = 48 + 2 * PAD
LAND = 1e38
MIB = 1024 * 1024
VMEM = pl.BlockSpec(memory_space=pltpu.VMEM)
FAR = pl.BlockSpec(memory_space=pltpu.HBM)
SMEM = pl.BlockSpec(memory_space=pltpu.SMEM)


def iota(shape, dim):
    return lax.broadcasted_iota(jnp.int32, shape, dim)


def turn(x, shift, axis=1):
    shift = shift % x.shape[axis]
    return pltpu.roll(x, shift, axis) if shift else x


def terms(k, value, centre, side, vert):
    row, lane = iota((ROWS, COLS), 0), iota((ROWS, COLS), 1)
    y = value[k]
    east, west = side[0, k] * y, side[1, k] * y
    north, south = turn(side[2, k] * y, 1, 0), turn(side[3, k] * y, -1, 0)
    r = centre[k] * y
    r = r + jnp.where(lane > 0, turn(east, 1), 0.0) + jnp.where(lane < COLS - 1, turn(west, -1), 0.0)
    r = r + jnp.where(row > 0, north, 0.0) + jnp.where(row < ROWS - 1, south, 0.0)
    if k + 1 < LEVELS:
        r = r + vert[0, k + 1] * value[k + 1]
    if k > 0:
        r = r + vert[1, k - 1] * value[k - 1]
    return r, east, west, north, south


def outer(lane, last, first):
    return jnp.where(lane == COLS - 1, last, jnp.where(lane == 0, first, 0.0))


def scale_kernel(side, mask, scales):
    lane = iota((ROWS, COLS), 1)
    packed = jnp.zeros((ROWS, COLS), jnp.float32)
    for at in (16, 16 + PAD):
        scales[at + 24 : at + PAD, :] = jnp.zeros((8, COLS), jnp.float32)
    for k in range(LEVELS):
        m = mask[k].astype(jnp.float32)
        packed = packed + turn(m * outer(lane, side[0, k], side[1, k]), 2 * k + 1)
        scales[16 + k : 17 + k, :] = (m * side[2, k])[ROWS - 1 : ROWS]
        scales[16 + PAD + k : 17 + PAD + k, :] = (m * side[3, k])[0:1]
    scales[0:8, :], scales[8:16, :] = tight(packed)


def tight(packed):
    even = (iota((8, COLS), 1) & 1) == 0
    eastward = westward = jnp.zeros((8, COLS), jnp.float32)
    for g, offset in enumerate(OFFSET):
        rows = packed[8 * g : 8 * g + 8]
        eastward = eastward + turn(jnp.where(even, rows, 0.0), offset)
        westward = westward + turn(jnp.where(even, 0.0, rows), offset - 1)
    return eastward, westward


def forced(sources, misfit, cell, count, adjoint_far, start, hot, valued, adjoint, arrived):
    load = pltpu.make_async_copy(adjoint_far, adjoint, arrived)
    load.start()
    group = min(GROUP, sources)
    lane = iota((1, CAP), 1)
    for first in range(0, sources, group):
        for s in range(group):
            at = slice(s * CAP, (s + 1) * CAP)
            cells = cell[first + s : first + s + 1, :]
            v = jnp.where(lane < count[0, first + s], misfit[first + s : first + s + 1, :], 0.0)
            high = v.astype(jnp.bfloat16).astype(jnp.float32)
            low = v - high
            column = iota((COLS, CAP), 0) == (cells & (COLS - 1))
            for i, part in enumerate((high, low)):
                valued[i * COLS : (i + 1) * COLS, at] = jnp.where(column, part, 0.0).astype(jnp.bfloat16)
            place = cells >> 7
            for k in range(LEVELS):
                match = (iota((ROWS, CAP), 0) + k * ROWS) == place
                hot[k * ROWS : (k + 1) * ROWS, at] = jnp.where(match, 1.0, 0.0).astype(jnp.bfloat16)
        part = lax.dot_general(hot[...], valued[...], (((1,), (1,)), ((), ())), preferred_element_type=jnp.float32)
        part = part[:, 0:COLS] + part[:, COLS : 2 * COLS]
        if first == 0:
            load.wait()
        held = adjoint if first == 0 else start
        for k in range(LEVELS):
            start[k] = held[k] + part[k * ROWS : (k + 1) * ROWS, :]


def to_lanes(column, offset):
    level = iota((PAD, COLS), 0)
    spot = (iota((PAD, COLS), 1) == 2 * level + offset) & (level < LEVELS)
    return jnp.sum(jnp.where(spot, column, 0.0), axis=0, keepdims=True)


def to_rows(line, offset):
    level = iota((PAD, COLS), 0)
    spot = (iota((PAD, COLS), 1) == 2 * level + offset) & (level < LEVELS)
    return jnp.sum(jnp.where(spot, line, 0.0), axis=1, keepdims=True)


def spot_rows(first, last):
    row = iota((8, COLS), 0)
    return jnp.where(row == 0, first, 0.0) + jnp.where(row == 7, last, 0.0)


def ends(block):
    return block[:, COLS - 1 : COLS], block[:, 0:1]


def from_tiles(swapped, next_swapped, where, rows):
    upward = where[4] == 0
    first, second = swapped[rows, :], next_swapped[rows, :]
    return jnp.where(upward, second, first), jnp.where(upward, first, second)


def chunk(source, target, semaphores, i):
    levels = pl.ds(i * CHUNK, CHUNK)
    return pltpu.make_async_copy(source.at[levels], target.at[levels], semaphores.at[i])


def first_kernel(sources, misfit, cell, count, adjoint_far, where, scales, side, centre_far, vert, mask, part, swap, next_swap, edges, slots, hot, valued, adjoint, held, centre, up, down, tips, picked, next_picked, near, posted, arrived):
    load = pltpu.make_async_copy(centre_far, centre, near)
    load.start()
    forced(sources, misfit, cell, count, adjoint_far, held, hot, valued, adjoint, arrived)
    load.wait()
    for ref in (up, down):
        ref[CORNER + 1 : SLOT, :] = jnp.zeros((SLOT - CORNER - 1, COLS), jnp.float32)
    for i in range(2):
        tips[i * PAD + 24 : (i + 1) * PAD, :] = jnp.zeros((8, COLS), jnp.float32)
    lane = iota((ROWS, COLS), 1)
    packed = [jnp.zeros((ROWS, COLS), jnp.float32)] * 2
    for k in range(LEVELS):
        r, east, west, north, south = terms(k, held, centre, side, vert)
        part[k] = jnp.where(mask[k] == 0, LAND, r)
        sides = outer(lane, east, west)
        for i, (ref, leaving, at) in enumerate(((up, north[0:1], ROWS - 1), (down, south[ROWS - 1 : ROWS], 0))):
            ref[k : k + 1, :] = leaving
            ref[LEVELS + k : LEVELS + k + 1, :] = r[at : at + 1]
            tips[i * PAD + k : i * PAD + k + 1, :] = sides[at : at + 1]
        packed = [p + turn(x, 2 * k + 1) for p, x in zip(packed, (sides, outer(lane, r, r)))]
    for i, ref in enumerate((up, down)):
        ref[2 * LEVELS : 3 * LEVELS, :] = scales[16 + i * PAD : 16 + i * PAD + LEVELS, :]
        east, west = ends(tips[i * PAD : (i + 1) * PAD, :])
        ref[CORNER : CORNER + 1, :] = to_lanes(east, OFFSET[0]) + to_lanes(west, OFFSET[1])
    spread = [pltpu.make_async_copy(up, slots.at[s], posted.at[s]) for s in range(slots.shape[0])]
    for copy in spread:
        copy.start()
    upward = where[4] == 0
    picked[...] = jnp.where(upward, up[...], down[...])
    next_picked[...] = jnp.where(upward, down[...], up[...])
    spread.append(pltpu.make_async_copy(picked, swap, posted.at[slots.shape[0]]))
    spread.append(pltpu.make_async_copy(next_picked, next_swap, posted.at[slots.shape[0] + 1]))
    for copy in spread[-2:]:
        copy.start()
    for i, p in enumerate(packed):
        edges[8 * i : 8 * i + 8, :], edges[24 + 8 * i : 32 + 8 * i, :] = tight(p)
    edges[16:24, :] = scales[0:8, :]
    edges[40:48, :] = scales[8:16, :]
    edges[48 : 48 + PAD, :] = down[0:PAD, :]
    edges[48 + PAD : EDGES, :] = up[0:PAD, :]
    for copy in spread:
        copy.wait()


def corner_kernel(swapped, next_swapped, edges, where, swap, next_swap):
    low, high = from_tiles(swapped, next_swapped, where, slice(0, PAD))
    low_tips, high_tips = from_tiles(swapped, next_swapped, where, slice(CORNER, CORNER + 1))
    low_last, low_first = ends(low)
    high_last, high_first = ends(high)
    eastern = iota((1, COLS), 1) < OFFSET[1]
    corners = low_tips + turn(jnp.where(eastern, high_tips, 0.0), OFFSET[3] - OFFSET[0])
    corners = corners + turn(jnp.where(eastern, 0.0, high_tips), OFFSET[2] - OFFSET[1])
    eastward = spot_rows(to_lanes(low_last, OFFSET[0]), to_lanes(high_last, OFFSET[3]))
    westward = spot_rows(to_lanes(low_first, OFFSET[0]), to_lanes(high_first, OFFSET[3]))
    to_east = where[5] == 0
    for ref, chosen in ((swap, to_east), (next_swap, jnp.logical_not(to_east))):
        ref[0:24, :] = jnp.where(chosen, edges[0:24, :], edges[24:48, :])
        ref[8:16, :] += jnp.where(chosen, eastward, westward)
        ref[24:EDGE, :] = jnp.where(iota((EDGE - 24, COLS), 0) == 0, corners, 0.0)


def second_kernel(swapped, next_swapped, beside, next_beside, edges, got, partner, flip, where, part, side, centre_far, vert, out, held, centre, result, lines, near_sides, far_sides, west_side, east_side, near, sent):
    load = pltpu.make_async_copy(centre_far, centre, near)
    load.start()
    sources = got.shape[0]
    below_near, above_near = from_tiles(swapped, next_swapped, where, slice(0, PAD))
    below_part, above_part = from_tiles(swapped, next_swapped, where, slice(LEVELS, LEVELS + PAD))
    below_scale, above_scale = (
        turn(rows, SLOT - PAD - 2 * LEVELS, 0)
        for rows in from_tiles(swapped, next_swapped, where, slice(SLOT - PAD, SLOT))
    )
    sum_low = below_part + edges[48 : 48 + PAD, :]
    sum_high = above_part + edges[48 + PAD : EDGES, :]
    even_column = where[5] == 0
    west_side[...] = jnp.where(even_column, next_beside[...], beside[...])
    east_side[...] = jnp.where(even_column, beside[...], next_beside[...])
    column, top, left, right = where[0], where[1], where[2], where[3]
    at_top = top == 1

    def comes_from(target):
        source = 0
        for s in range(sources):
            source = jnp.where(partner[s] == target, s, source)
        return source

    def turned(rows, source):
        back = COLS - 1 - iota((PAD, COLS), 1)
        return jnp.where(flip[source] == 1, jnp.take_along_axis(rows, back, axis=1), rows)

    level_lane = iota((PAD, COLS), 1)
    source = comes_from(column)
    earlier = comes_from(source)
    before = jnp.where(source == 0, sources - 1, source - 1)
    after = jnp.where(source == sources - 1, 0, source + 1)
    corner_left = west_side[24:25, :]
    corner_right = east_side[24:25, :]
    sum_low = sum_low + jnp.where(level_lane == 0, to_rows(corner_left, OFFSET[0]), 0.0)
    sum_low = sum_low + jnp.where(level_lane == COLS - 1, to_rows(corner_right, OFFSET[1]), 0.0)
    sum_high = sum_high + jnp.where(level_lane == 0, to_rows(corner_left, OFFSET[3]), 0.0)
    sum_high = sum_high + jnp.where(level_lane == COLS - 1, to_rows(corner_right, OFFSET[2]), 0.0)
    fold_first = turned(got[source, 0:PAD, :], source)
    sum_fold = got[source, LEVELS : LEVELS + PAD, :] + turned(got[earlier, 0:PAD, :], earlier)
    cross_west = to_rows(got[before, CORNER : CORNER + 1, :], OFFSET[0])
    cross_east = to_rows(got[after, CORNER : CORNER + 1, :], OFFSET[1])
    sum_fold = sum_fold + jnp.where(level_lane == 0, cross_west, 0.0) + jnp.where(level_lane == COLS - 1, cross_east, 0.0)
    fold_second = turned(turn(got[source, SLOT - PAD : SLOT, :], SLOT - PAD - 2 * LEVELS, 0) * sum_fold, source)
    lines[0:PAD, :] = jnp.where(at_top, fold_first, above_near)
    lines[PAD : 2 * PAD, :] = below_scale * sum_low
    lines[2 * PAD : 3 * PAD, :] = jnp.where(at_top, fold_second, above_scale * sum_high)
    lines[3 * PAD : 4 * PAD, :] = below_near
    from_left = comes_from(left)
    from_right = comes_from(right)
    fold_left = turned(got[from_left, 0:PAD, :], from_left)[:, COLS - 1 : COLS]
    fold_right = turned(got[from_right, 0:PAD, :], from_right)[:, 0:1]
    fold_left = jnp.where(at_top, to_lanes(fold_left, OFFSET[3]), 0.0)
    fold_right = jnp.where(at_top, to_lanes(fold_right, OFFSET[3]), 0.0)
    near_left = west_side[0:8, :]
    near_right = east_side[0:8, :]
    next_left = west_side[16:24, :] * (west_side[8:16, :] + edges[24:32, :] + spot_rows(0.0, fold_left))
    next_right = east_side[16:24, :] * (east_side[8:16, :] + edges[0:8, :] + spot_rows(0.0, fold_right))
    even = (iota((8, COLS), 1) & 1) == 0
    for ref, from_west, from_east in ((near_sides, near_left, near_right), (far_sides, next_left, next_right)):
        for g, offset in enumerate(OFFSET):
            ref[8 * g : 8 * g + 8, :] = jnp.where(even, turn(from_west, -offset), turn(from_east, -offset - 1))

    row, lane = iota((ROWS, COLS), 0), iota((ROWS, COLS), 1)

    def joined(k, r, sides, first, last):
        r = r + jnp.where((lane == 0) | (lane == COLS - 1), turn(sides[...], -2 * k), 0.0)
        r = r + jnp.where(row == 0, first, 0.0) + jnp.where(row == ROWS - 1, last, 0.0)
        return jnp.where(part[k] == LAND, 0.0, r)

    for k in range(LEVELS):
        held[k] = joined(k, part[k], near_sides, lines[3 * PAD + k : 3 * PAD + k + 1, :], lines[k : k + 1, :])
    load.wait()
    for k in range(LEVELS):
        r = terms(k, held, centre, side, vert)[0]
        result[k] = joined(k, r, far_sides, lines[PAD + k : PAD + k + 1, :], lines[2 * PAD + k : 2 * PAD + k + 1, :])
        if (k + 1) % CHUNK == 0:
            chunk(result, out, sent, k // CHUNK).start()
    for i in range(LEVELS // CHUNK):
        chunk(result, out, sent, i).wait()


def body(adjoint_in, centre, side_coeff, vert_coeff, land_mask, obs_misfit, obs_cell, obs_count, fold_partner, fold_flip):
    sources = obs_misfit.shape[2]
    tiles = lax.axis_size("tile")
    column, tile_row = lax.axis_index("col"), lax.axis_index("tile")
    where = jnp.stack(
        [
            column,
            (tile_row == tiles - 1).astype(jnp.int32),
            jnp.where(column == 0, sources - 1, column - 1),
            jnp.where(column == sources - 1, 0, column + 1),
            tile_row & 1,
            column & 1,
        ]
    )
    received = lax.all_to_all(obs_misfit, "col", split_axis=2, concat_axis=1, tiled=True)
    f32 = jnp.float32
    tile = jax.ShapeDtypeStruct((LEVELS, ROWS, COLS), f32)
    lines = pltpu.HBM((SLOT, COLS), f32)
    field = pltpu.VMEM((LEVELS, ROWS, COLS), f32)
    chunks = pltpu.SemaphoreType.DMA((LEVELS // CHUNK,))
    group = min(GROUP, sources)
    small = sources <= GROUP
    ahead = pl.CostEstimate(flops=10**10, bytes_accessed=2 * 10**8, transcendentals=0)
    scales = pl.pallas_call(
        scale_kernel,
        out_shape=jax.ShapeDtypeStruct((16 + 2 * PAD, COLS), f32),
        in_specs=[VMEM, VMEM],
        out_specs=VMEM,
        compiler_params=pltpu.CompilerParams(vmem_limit_bytes=4 * MIB),
        cost_estimate=ahead,
        name="edge_scales",
    )(side_coeff, land_mask)
    part, swap, next_swap, edges, slots = pl.pallas_call(
        functools.partial(first_kernel, sources),
        out_shape=(tile, lines, lines, jax.ShapeDtypeStruct((EDGES, COLS), f32), pltpu.HBM((sources, SLOT, COLS), f32)),
        in_specs=[VMEM, VMEM, SMEM, FAR, SMEM, VMEM, VMEM, FAR, VMEM, VMEM],
        out_specs=(VMEM, FAR, FAR, VMEM, FAR),
        scratch_shapes=[
            pltpu.VMEM((LEVELS * ROWS, group * CAP), jnp.bfloat16),
            pltpu.VMEM((2 * COLS, group * CAP), jnp.bfloat16),
            field,
            field,
            field,
            pltpu.VMEM((SLOT, COLS), f32),
            pltpu.VMEM((SLOT, COLS), f32),
            pltpu.VMEM((2 * PAD, COLS), f32),
            pltpu.VMEM((SLOT, COLS), f32),
            pltpu.VMEM((SLOT, COLS), f32),
            pltpu.SemaphoreType.DMA,
            pltpu.SemaphoreType.DMA((sources + 2,)),
            pltpu.SemaphoreType.DMA,
        ],
        compiler_params=pltpu.CompilerParams(vmem_limit_bytes=(10 if small else 24) * MIB),
        name="first_step",
    )(
        received.reshape(sources, CAP),
        obs_cell.reshape(sources, CAP),
        obs_count.reshape(1, sources),
        pltpu.with_memory_space_constraint(adjoint_in, pltpu.HBM),
        where,
        scales,
        side_coeff,
        pltpu.with_memory_space_constraint(centre, pltpu.HBM),
        vert_coeff,
        land_mask,
    )
    got = lax.all_to_all(slots, "col", split_axis=0, concat_axis=0, tiled=True)
    next_swapped = lax.ppermute(next_swap, "tile", swaps(1, tiles - 1))
    swapped = lax.ppermute(swap, "tile", swaps(0, tiles))
    edge = jax.ShapeDtypeStruct((EDGE, COLS), f32)
    beside, next_beside = pl.pallas_call(
        corner_kernel,
        out_shape=(edge, edge),
        in_specs=[VMEM, VMEM, VMEM, SMEM],
        out_specs=(VMEM, VMEM),
        compiler_params=pltpu.CompilerParams(vmem_limit_bytes=4 * MIB),
        cost_estimate=pl.CostEstimate(flops=10**6, bytes_accessed=4 * 10**6, transcendentals=0),
        name="corners",
    )(swapped, next_swapped, edges, where)
    round_trip = [(sources - 1, 0), (0, sources - 1)]
    next_beside = lax.ppermute(next_beside, "col", swaps(1, sources - 1) + round_trip)
    beside = lax.ppermute(beside, "col", swaps(0, sources))
    return pl.pallas_call(
        second_kernel,
        out_shape=tile,
        in_specs=[VMEM] * 6 + [SMEM] * 3 + [VMEM, VMEM, FAR, VMEM],
        out_specs=FAR,
        scratch_shapes=[
            field,
            field,
            field,
            pltpu.VMEM((4 * PAD, COLS), f32),
            pltpu.VMEM((ROWS, COLS), f32),
            pltpu.VMEM((ROWS, COLS), f32),
            pltpu.VMEM((EDGE, COLS), f32),
            pltpu.VMEM((EDGE, COLS), f32),
            pltpu.SemaphoreType.DMA,
            chunks,
        ],
        compiler_params=pltpu.CompilerParams(vmem_limit_bytes=(8 if small else 24) * MIB),
        name="second_step",
    )(
        swapped,
        next_swapped,
        beside,
        next_beside,
        edges,
        got,
        fold_partner,
        fold_flip,
        where,
        part,
        side_coeff,
        pltpu.with_memory_space_constraint(centre, pltpu.HBM),
        vert_coeff,
    )


def swaps(first, end):
    return [pair for i in range(first, end - 1, 2) for pair in ((i, i + 1), (i + 1, i))]


def solution(mesh):
    in_specs = (
        P(None, "tile", "col"),
        P(None, "tile", "col"),
        P(None, None, "tile", "col"),
        P(None, None, "tile", "col"),
        P(None, "tile", "col"),
        P("tile", "col", None, None),
        P("tile", "col", None, None),
        P("tile", "col", None),
        P(),
        P(),
    )
    out_specs = P(None, "tile", "col")
    return jax.shard_map(body, mesh=mesh, in_specs=in_specs, out_specs=out_specs, check_vma=False)
```

```python
import functools

import jax
import jax.numpy as jnp
from jax import lax
from jax.experimental import pallas as pl
from jax.experimental.pallas import tpu as pltpu
from jax.sharding import PartitionSpec as P

LEVELS = 25
ROWS = 32
COLS = 128
CAP = 128
GROUP = 8
CHUNK = 5
PAD = 32
CORNER = 3 * LEVELS
SLOT = 80
EDGE = 32
OFFSET = (0, 50, 1, 51)
EDGES = 48 + 2 * PAD
LAND = 1e38
MIB = 1024 * 1024
VMEM = pl.BlockSpec(memory_space=pltpu.VMEM)
FAR = pl.BlockSpec(memory_space=pltpu.HBM)
SMEM = pl.BlockSpec(memory_space=pltpu.SMEM)


def iota(shape, dim):
    return lax.broadcasted_iota(jnp.int32, shape, dim)


def turn(x, shift, axis=1):
    shift = shift % x.shape[axis]
    return pltpu.roll(x, shift, axis) if shift else x


def terms(k, value, centre, side, vert):
    row, lane = iota((ROWS, COLS), 0), iota((ROWS, COLS), 1)
    y = value[k]
    east, west = side[0, k] * y, side[1, k] * y
    north, south = turn(side[2, k] * y, 1, 0), turn(side[3, k] * y, -1, 0)
    r = centre[k] * y
    r = r + jnp.where(lane > 0, turn(east, 1), 0.0) + jnp.where(lane < COLS - 1, turn(west, -1), 0.0)
    r = r + jnp.where(row > 0, north, 0.0) + jnp.where(row < ROWS - 1, south, 0.0)
    if k + 1 < LEVELS:
        r = r + vert[0, k + 1] * value[k + 1]
    if k > 0:
        r = r + vert[1, k - 1] * value[k - 1]
    return r, east, west, north, south


def outer(lane, last, first):
    return jnp.where(lane == COLS - 1, last, jnp.where(lane == 0, first, 0.0))


def scale_kernel(side, mask, scales):
    lane = iota((ROWS, COLS), 1)
    packed = jnp.zeros((ROWS, COLS), jnp.float32)
    for at in (16, 16 + PAD):
        scales[at + 24 : at + PAD, :] = jnp.zeros((8, COLS), jnp.float32)
    for k in range(LEVELS):
        m = mask[k].astype(jnp.float32)
        packed = packed + turn(m * outer(lane, side[0, k], side[1, k]), 2 * k + 1)
        scales[16 + k : 17 + k, :] = (m * side[2, k])[ROWS - 1 : ROWS]
        scales[16 + PAD + k : 17 + PAD + k, :] = (m * side[3, k])[0:1]
    scales[0:8, :], scales[8:16, :] = tight(packed)


def tight(packed):
    even = (iota((8, COLS), 1) & 1) == 0
    eastward = westward = jnp.zeros((8, COLS), jnp.float32)
    for g, offset in enumerate(OFFSET):
        rows = packed[8 * g : 8 * g + 8]
        eastward = eastward + turn(jnp.where(even, rows, 0.0), offset)
        westward = westward + turn(jnp.where(even, 0.0, rows), offset - 1)
    return eastward, westward


def forced(sources, misfit, cell, count, adjoint_far, start, hot, valued, adjoint, arrived):
    load = pltpu.make_async_copy(adjoint_far, adjoint, arrived)
    load.start()
    group = min(GROUP, sources)
    lane = iota((1, CAP), 1)
    for first in range(0, sources, group):
        for s in range(group):
            at = slice(s * CAP, (s + 1) * CAP)
            cells = cell[first + s : first + s + 1, :]
            v = jnp.where(lane < count[0, first + s], misfit[first + s : first + s + 1, :], 0.0)
            high = v.astype(jnp.bfloat16).astype(jnp.float32)
            low = v - high
            column = iota((COLS, CAP), 0) == (cells & (COLS - 1))
            for i, part in enumerate((high, low)):
                valued[i * COLS : (i + 1) * COLS, at] = jnp.where(column, part, 0.0).astype(jnp.bfloat16)
            place = cells >> 7
            for k in range(LEVELS):
                match = iota((ROWS, CAP), 0) == place - k * ROWS
                hot[k * ROWS : (k + 1) * ROWS, at] = jnp.where(match, 1.0, 0.0).astype(jnp.bfloat16)
        part = lax.dot_general(hot[...], valued[...], (((1,), (1,)), ((), ())), preferred_element_type=jnp.float32)
        part = part[:, 0:COLS] + part[:, COLS : 2 * COLS]
        if first == 0:
            load.wait()
        held = adjoint if first == 0 else start
        for k in range(LEVELS):
            start[k] = held[k] + part[k * ROWS : (k + 1) * ROWS, :]


def to_lanes(column, offset):
    level = iota((PAD, COLS), 0)
    spot = (iota((PAD, COLS), 1) == 2 * level + offset) & (level < LEVELS)
    return jnp.sum(jnp.where(spot, column, 0.0), axis=0, keepdims=True)


def to_rows(line, offset):
    level = iota((PAD, COLS), 0)
    spot = (iota((PAD, COLS), 1) == 2 * level + offset) & (level < LEVELS)
    return jnp.sum(jnp.where(spot, line, 0.0), axis=1, keepdims=True)


def spot_rows(first, last):
    row = iota((8, COLS), 0)
    return jnp.where(row == 0, first, 0.0) + jnp.where(row == 7, last, 0.0)


def ends(block):
    return block[:, COLS - 1 : COLS], block[:, 0:1]


def from_tiles(swapped, next_swapped, where, rows):
    upward = where[4] == 0
    first, second = swapped[rows, :], next_swapped[rows, :]
    return jnp.where(upward, second, first), jnp.where(upward, first, second)


def chunk(source, target, semaphores, i):
    levels = pl.ds(i * CHUNK, CHUNK)
    return pltpu.make_async_copy(source.at[levels], target.at[levels], semaphores.at[i])


def first_kernel(sources, misfit, cell, count, adjoint_far, where, scales, side, centre, vert, mask, part_far, swap, next_swap, edges, slots, hot, valued, adjoint, held, part, up, down, tips, picked, next_picked, sent, posted, arrived):
    forced(sources, misfit, cell, count, adjoint_far, held, hot, valued, adjoint, arrived)
    for ref in (up, down):
        ref[CORNER + 1 : SLOT, :] = jnp.zeros((SLOT - CORNER - 1, COLS), jnp.float32)
    for i in range(2):
        tips[i * PAD + 24 : (i + 1) * PAD, :] = jnp.zeros((8, COLS), jnp.float32)
    lane = iota((ROWS, COLS), 1)
    packed = [jnp.zeros((ROWS, COLS), jnp.float32)] * 2
    for k in range(LEVELS):
        r, east, west, north, south = terms(k, held, centre, side, vert)
        part[k] = jnp.where(mask[k] == 0, LAND, r)
        sides = outer(lane, east, west)
        for i, (ref, leaving, at) in enumerate(((up, north[0:1], ROWS - 1), (down, south[ROWS - 1 : ROWS], 0))):
            ref[k : k + 1, :] = leaving
            ref[LEVELS + k : LEVELS + k + 1, :] = r[at : at + 1]
            tips[i * PAD + k : i * PAD + k + 1, :] = sides[at : at + 1]
        packed = [p + turn(x, 2 * k + 1) for p, x in zip(packed, (sides, outer(lane, r, r)))]
        if (k + 1) % CHUNK == 0:
            chunk(part, part_far, sent, k // CHUNK).start()
    for i, ref in enumerate((up, down)):
        ref[2 * LEVELS : 3 * LEVELS, :] = scales[16 + i * PAD : 16 + i * PAD + LEVELS, :]
        east, west = ends(tips[i * PAD : (i + 1) * PAD, :])
        ref[CORNER : CORNER + 1, :] = to_lanes(east, OFFSET[0]) + to_lanes(west, OFFSET[1])
    spread = [pltpu.make_async_copy(up, slots.at[s], posted.at[s]) for s in range(slots.shape[0])]
    for copy in spread:
        copy.start()
    upward = where[4] == 0
    picked[...] = jnp.where(upward, up[...], down[...])
    next_picked[...] = jnp.where(upward, down[...], up[...])
    spread.append(pltpu.make_async_copy(picked, swap, posted.at[slots.shape[0]]))
    spread.append(pltpu.make_async_copy(next_picked, next_swap, posted.at[slots.shape[0] + 1]))
    for copy in spread[-2:]:
        copy.start()
    for i, p in enumerate(packed):
        edges[8 * i : 8 * i + 8, :], edges[24 + 8 * i : 32 + 8 * i, :] = tight(p)
    edges[16:24, :] = scales[0:8, :]
    edges[40:48, :] = scales[8:16, :]
    edges[48 : 48 + PAD, :] = down[0:PAD, :]
    edges[48 + PAD : EDGES, :] = up[0:PAD, :]
    for i in range(LEVELS // CHUNK):
        chunk(part, part_far, sent, i).wait()
    for copy in spread:
        copy.wait()


def corner_kernel(swapped, next_swapped, edges, where, swap, next_swap):
    low, high = from_tiles(swapped, next_swapped, where, slice(0, PAD))
    low_tips, high_tips = from_tiles(swapped, next_swapped, where, slice(CORNER, CORNER + 1))
    low_last, low_first = ends(low)
    high_last, high_first = ends(high)
    eastern = iota((1, COLS), 1) < OFFSET[1]
    corners = low_tips + turn(jnp.where(eastern, high_tips, 0.0), OFFSET[3] - OFFSET[0])
    corners = corners + turn(jnp.where(eastern, 0.0, high_tips), OFFSET[2] - OFFSET[1])
    eastward = spot_rows(to_lanes(low_last, OFFSET[0]), to_lanes(high_last, OFFSET[3]))
    westward = spot_rows(to_lanes(low_first, OFFSET[0]), to_lanes(high_first, OFFSET[3]))
    to_east = where[5] == 0
    for ref, chosen in ((swap, to_east), (next_swap, jnp.logical_not(to_east))):
        ref[0:24, :] = jnp.where(chosen, edges[0:24, :], edges[24:48, :])
        ref[8:16, :] += jnp.where(chosen, eastward, westward)
        ref[24:EDGE, :] = jnp.where(iota((EDGE - 24, COLS), 0) == 0, corners, 0.0)


def second_kernel(swapped, next_swapped, beside, next_beside, edges, got, partner, flip, where, part_far, side, centre, vert, out, held, part, result, lines, near_sides, far_sides, west_side, east_side, loaded, sent):
    for i in range(LEVELS // CHUNK):
        chunk(part_far, part, loaded, i).start()
    sources = got.shape[0]
    below_near, above_near = from_tiles(swapped, next_swapped, where, slice(0, PAD))
    below_part, above_part = from_tiles(swapped, next_swapped, where, slice(LEVELS, LEVELS + PAD))
    below_scale, above_scale = (
        turn(rows, SLOT - PAD - 2 * LEVELS, 0)
        for rows in from_tiles(swapped, next_swapped, where, slice(SLOT - PAD, SLOT))
    )
    sum_low = below_part + edges[48 : 48 + PAD, :]
    sum_high = above_part + edges[48 + PAD : EDGES, :]
    even_column = where[5] == 0
    west_side[...] = jnp.where(even_column, next_beside[...], beside[...])
    east_side[...] = jnp.where(even_column, beside[...], next_beside[...])
    column, top, left, right = where[0], where[1], where[2], where[3]
    at_top = top == 1

    def comes_from(target):
        source = 0
        for s in range(sources):
            source = jnp.where(partner[s] == target, s, source)
        return source

    def turned(rows, source):
        back = COLS - 1 - iota((PAD, COLS), 1)
        return jnp.where(flip[source] == 1, jnp.take_along_axis(rows, back, axis=1), rows)

    level_lane = iota((PAD, COLS), 1)
    source = comes_from(column)
    earlier = comes_from(source)
    before = jnp.where(source == 0, sources - 1, source - 1)
    after = jnp.where(source == sources - 1, 0, source + 1)
    corner_left = west_side[24:25, :]
    corner_right = east_side[24:25, :]
    sum_low = sum_low + jnp.where(level_lane == 0, to_rows(corner_left, OFFSET[0]), 0.0)
    sum_low = sum_low + jnp.where(level_lane == COLS - 1, to_rows(corner_right, OFFSET[1]), 0.0)
    sum_high = sum_high + jnp.where(level_lane == 0, to_rows(corner_left, OFFSET[3]), 0.0)
    sum_high = sum_high + jnp.where(level_lane == COLS - 1, to_rows(corner_right, OFFSET[2]), 0.0)
    fold_first = turned(got[source, 0:PAD, :], source)
    sum_fold = got[source, LEVELS : LEVELS + PAD, :] + turned(got[earlier, 0:PAD, :], earlier)
    cross_west = to_rows(got[before, CORNER : CORNER + 1, :], OFFSET[0])
    cross_east = to_rows(got[after, CORNER : CORNER + 1, :], OFFSET[1])
    sum_fold = sum_fold + jnp.where(level_lane == 0, cross_west, 0.0) + jnp.where(level_lane == COLS - 1, cross_east, 0.0)
    fold_second = turned(turn(got[source, SLOT - PAD : SLOT, :], SLOT - PAD - 2 * LEVELS, 0) * sum_fold, source)
    lines[0:PAD, :] = jnp.where(at_top, fold_first, above_near)
    lines[PAD : 2 * PAD, :] = below_scale * sum_low
    lines[2 * PAD : 3 * PAD, :] = jnp.where(at_top, fold_second, above_scale * sum_high)
    lines[3 * PAD : 4 * PAD, :] = below_near
    from_left = comes_from(left)
    from_right = comes_from(right)
    fold_left = turned(got[from_left, 0:PAD, :], from_left)[:, COLS - 1 : COLS]
    fold_right = turned(got[from_right, 0:PAD, :], from_right)[:, 0:1]
    fold_left = jnp.where(at_top, to_lanes(fold_left, OFFSET[3]), 0.0)
    fold_right = jnp.where(at_top, to_lanes(fold_right, OFFSET[3]), 0.0)
    near_left = west_side[0:8, :]
    near_right = east_side[0:8, :]
    next_left = west_side[16:24, :] * (west_side[8:16, :] + edges[24:32, :] + spot_rows(0.0, fold_left))
    next_right = east_side[16:24, :] * (east_side[8:16, :] + edges[0:8, :] + spot_rows(0.0, fold_right))
    even = (iota((8, COLS), 1) & 1) == 0
    for ref, from_west, from_east in ((near_sides, near_left, near_right), (far_sides, next_left, next_right)):
        for g, offset in enumerate(OFFSET):
            ref[8 * g : 8 * g + 8, :] = jnp.where(even, turn(from_west, -offset), turn(from_east, -offset - 1))

    row, lane = iota((ROWS, COLS), 0), iota((ROWS, COLS), 1)

    def joined(k, r, sides, first, last):
        r = r + jnp.where((lane == 0) | (lane == COLS - 1), turn(sides[...], -2 * k), 0.0)
        r = r + jnp.where(row == 0, first, 0.0) + jnp.where(row == ROWS - 1, last, 0.0)
        return jnp.where(part[k] == LAND, 0.0, r)

    for k in range(LEVELS):
        if k % CHUNK == 0:
            chunk(part_far, part, loaded, k // CHUNK).wait()
        held[k] = joined(k, part[k], near_sides, lines[3 * PAD + k : 3 * PAD + k + 1, :], lines[k : k + 1, :])
    for k in range(LEVELS):
        r = terms(k, held, centre, side, vert)[0]
        result[k] = joined(k, r, far_sides, lines[PAD + k : PAD + k + 1, :], lines[2 * PAD + k : 2 * PAD + k + 1, :])
        if (k + 1) % CHUNK == 0:
            chunk(result, out, sent, k // CHUNK).start()
    for i in range(LEVELS // CHUNK):
        chunk(result, out, sent, i).wait()


def body(adjoint_in, centre, side_coeff, vert_coeff, land_mask, obs_misfit, obs_cell, obs_count, fold_partner, fold_flip):
    sources = obs_misfit.shape[2]
    tiles = lax.axis_size("tile")
    column, tile_row = lax.axis_index("col"), lax.axis_index("tile")
    where = jnp.stack(
        [
            column,
            (tile_row == tiles - 1).astype(jnp.int32),
            jnp.where(column == 0, sources - 1, column - 1),
            jnp.where(column == sources - 1, 0, column + 1),
            tile_row & 1,
            column & 1,
        ]
    )
    received = lax.all_to_all(obs_misfit, "col", split_axis=2, concat_axis=1, tiled=True)
    f32 = jnp.float32
    tile = jax.ShapeDtypeStruct((LEVELS, ROWS, COLS), f32)
    lines = pltpu.HBM((SLOT, COLS), f32)
    field = pltpu.VMEM((LEVELS, ROWS, COLS), f32)
    chunks = pltpu.SemaphoreType.DMA((LEVELS // CHUNK,))
    group = min(GROUP, sources)
    small = sources <= GROUP
    ahead = pl.CostEstimate(flops=10**10, bytes_accessed=2 * 10**8, transcendentals=0)
    scales = pl.pallas_call(
        scale_kernel,
        out_shape=jax.ShapeDtypeStruct((16 + 2 * PAD, COLS), f32),
        in_specs=[VMEM, VMEM],
        out_specs=VMEM,
        compiler_params=pltpu.CompilerParams(vmem_limit_bytes=4 * MIB),
        cost_estimate=ahead,
        name="edge_scales",
    )(side_coeff, land_mask)
    part, swap, next_swap, edges, slots = pl.pallas_call(
        functools.partial(first_kernel, sources),
        out_shape=(tile, lines, lines, jax.ShapeDtypeStruct((EDGES, COLS), f32), pltpu.HBM((sources, SLOT, COLS), f32)),
        in_specs=[VMEM, VMEM, SMEM, FAR, SMEM] + [VMEM] * 5,
        out_specs=(FAR, FAR, FAR, VMEM, FAR),
        scratch_shapes=[
            pltpu.VMEM((LEVELS * ROWS, group * CAP), jnp.bfloat16),
            pltpu.VMEM((2 * COLS, group * CAP), jnp.bfloat16),
            field,
            field,
            field,
            pltpu.VMEM((SLOT, COLS), f32),
            pltpu.VMEM((SLOT, COLS), f32),
            pltpu.VMEM((2 * PAD, COLS), f32),
            pltpu.VMEM((SLOT, COLS), f32),
            pltpu.VMEM((SLOT, COLS), f32),
            chunks,
            pltpu.SemaphoreType.DMA((sources + 2,)),
            pltpu.SemaphoreType.DMA,
        ],
        compiler_params=pltpu.CompilerParams(vmem_limit_bytes=(10 if small else 24) * MIB),
        name="first_step",
    )(
        received.reshape(sources, CAP),
        obs_cell.reshape(sources, CAP),
        obs_count.reshape(1, sources),
        pltpu.with_memory_space_constraint(adjoint_in, pltpu.HBM),
        where,
        scales,
        side_coeff,
        centre,
        vert_coeff,
        land_mask,
    )
    got = lax.all_to_all(slots, "col", split_axis=0, concat_axis=0, tiled=True)
    next_swapped = lax.ppermute(next_swap, "tile", swaps(1, tiles - 1))
    swapped = lax.ppermute(swap, "tile", swaps(0, tiles))
    edge = jax.ShapeDtypeStruct((EDGE, COLS), f32)
    beside, next_beside = pl.pallas_call(
        corner_kernel,
        out_shape=(edge, edge),
        in_specs=[VMEM, VMEM, VMEM, SMEM],
        out_specs=(VMEM, VMEM),
        compiler_params=pltpu.CompilerParams(vmem_limit_bytes=4 * MIB),
        cost_estimate=pl.CostEstimate(flops=10**6, bytes_accessed=4 * 10**6, transcendentals=0),
        name="corners",
    )(swapped, next_swapped, edges, where)
    round_trip = [(sources - 1, 0), (0, sources - 1)]
    next_beside = lax.ppermute(next_beside, "col", swaps(1, sources - 1) + round_trip)
    beside = lax.ppermute(beside, "col", swaps(0, sources))
    return pl.pallas_call(
        second_kernel,
        out_shape=tile,
        in_specs=[VMEM] * 6 + [SMEM] * 3 + [FAR] + [VMEM] * 3,
        out_specs=FAR,
        input_output_aliases={9: 0},
        scratch_shapes=[
            field,
            field,
            field,
            pltpu.VMEM((4 * PAD, COLS), f32),
            pltpu.VMEM((ROWS, COLS), f32),
            pltpu.VMEM((ROWS, COLS), f32),
            pltpu.VMEM((EDGE, COLS), f32),
            pltpu.VMEM((EDGE, COLS), f32),
            chunks,
            chunks,
        ],
        compiler_params=pltpu.CompilerParams(vmem_limit_bytes=(8 if small else 24) * MIB),
        name="second_step",
    )(
        swapped,
        next_swapped,
        beside,
        next_beside,
        edges,
        got,
        fold_partner,
        fold_flip,
        where,
        part,
        side_coeff,
        centre,
        vert_coeff,
    )


def swaps(first, end):
    return [pair for i in range(first, end - 1, 2) for pair in ((i, i + 1), (i + 1, i))]


def solution(mesh):
    in_specs = (
        P(None, "tile", "col"),
        P(None, "tile", "col"),
        P(None, None, "tile", "col"),
        P(None, None, "tile", "col"),
        P(None, "tile", "col"),
        P("tile", "col", None, None),
        P("tile", "col", None, None),
        P("tile", "col", None),
        P(),
        P(),
    )
    out_specs = P(None, "tile", "col")
    return jax.shard_map(body, mesh=mesh, in_specs=in_specs, out_specs=out_specs, check_vma=False)
```
